512 devices in a mesh: ctx: 64 (over z, x), tp: 8 (over y, core).
Axes of the slice: x: 4, y: 4, z: 16, core: 2. Of those that a mesh axis runs over, the one named last changes fastest.
Arguments:
- queries: bfloat16 [8192, 8192], P('ctx', 'tp'), may hold values from -1.75 to 1.75
- key_rows: bfloat16 [8192, 8192], P('ctx', 'tp'), may hold values from -1.8 to 1.8
- value_rows: bfloat16 [8192, 8192], P('ctx', 'tp'), may hold values from -6 to 6
- log_decay: float32 [8192, 64], P('ctx', 'tp'), may hold values from -1 to 0
- norm_gain: float32 [8192], P('tp'), may hold values from 0.5 to 1.5
- grad_output: bfloat16 [8192, 8192], P('ctx', 'tp'), may hold values from -6 to 6
Outputs:
- normed: bfloat16 [8192, 8192], P('ctx', 'tp')
- grad_queries: bfloat16 [8192, 8192], P('ctx', 'tp')
- grad_keys: bfloat16 [8192, 8192], P('ctx', 'tp')
- grad_values: bfloat16 [8192, 8192], P('ctx', 'tp')
The draws below stay inside these ranges and needn't reach their ends.
All inputs are finite; a program needn't handle non-finite values.
Results may differ from the reference program's by a relative error of at most 0.002.
Values sent between devices are 32-bit elements; how exact they have to be, the bound alone decides.
No kernel may reach another device: no remote copies, remote signals or barrier semaphores. Data moves between devices by JAX's collectives and lax.ppermute only.
A program may use at most 192 MiB of HBM per device.

```python
import math
import jax
import jax.numpy as jnp
from jax import lax

HEAD_TOTAL = 64
DH = 128
TOK_DEV = 128
SEQUENCE_LENGTH = 8192


def head_rates(key, slow_share):
    key = jax.random.fold_in(key, 5)
    pieces = jax.random.split(key, 3)
    slow_heads = jax.random.uniform(pieces[0], (HEAD_TOTAL,)) < slow_share
    slow_rate = jnp.exp(jax.random.uniform(pieces[1], (HEAD_TOTAL,), minval=math.log(0.2), maxval=math.log(0.8))) / SEQUENCE_LENGTH
    spread_rate = jnp.exp(jax.random.uniform(pieces[2], (HEAD_TOTAL,), minval=math.log(0.0003), maxval=math.log(0.08)))
    return jnp.where(slow_heads, slow_rate, spread_rate)


def block_levels(key, lowest):
    block_level = jnp.exp(jax.random.uniform(key, (SEQUENCE_LENGTH // TOK_DEV, HEAD_TOTAL), minval=lowest, maxval=0.0))
    return block_level


def spread_rows(level_table):
    level_rows = jnp.repeat(level_table, TOK_DEV, axis=0)
    return jnp.repeat(level_rows, DH, axis=1)


def draw_log_decay(key, part):
    slow_share = 0.5
    baseline_rate = head_rates(key, slow_share)
    key = jax.random.fold_in(key, 11)
    key_tensor = jax.random.split(key, 4)
    processor_factor = jnp.exp(jax.random.uniform(key_tensor[0], (SEQUENCE_LENGTH // TOK_DEV, HEAD_TOTAL), minval=math.log(0.5), maxval=math.log(2.0)))
    processor_factor = jnp.repeat(processor_factor, TOK_DEV, axis=0)
    random_noise = jax.random.uniform(key_tensor[1], (SEQUENCE_LENGTH, HEAD_TOTAL), minval=0.5, maxval=1.5)
    spike_positions = jax.random.randint(key_tensor[2], (2,), 0, SEQUENCE_LENGTH)
    token_positions = jnp.arange(SEQUENCE_LENGTH)
    spike_rows = jnp.any(token_positions[:, None] == spike_positions[None, :], axis=1).astype(jnp.float32)
    spike_loss = jax.random.uniform(key_tensor[3], (HEAD_TOTAL,), minval=0.2, maxval=0.4)
    value_tensor = -baseline_rate[None, :] * processor_factor * random_noise + spike_rows[:, None] * jnp.log1p(-spike_loss)[None, :]
    return value_tensor.astype(jnp.float32)


def draw_key_rows(key, part):
    key = jax.random.fold_in(key, 17)
    pieces = jax.random.split(key, 2)
    level_rows = spread_rows(block_levels(pieces[0], -5.0))
    gaussian = jnp.clip(jax.random.normal(pieces[1], (SEQUENCE_LENGTH, HEAD_TOTAL * DH)), -6.0, 6.0)
    return (0.3 * gaussian * level_rows).astype(jnp.bfloat16)


def draw_value_rows(key, part):
    slow_share = 0.5
    head_level = jnp.minimum(1.0, jnp.sqrt(64.0 * head_rates(key, slow_share)))
    key = jax.random.fold_in(key, 13)
    pieces = jax.random.split(key, 2)
    level_rows = spread_rows(block_levels(pieces[0], -5.0) * head_level[None, :])
    gaussian = jnp.clip(jax.random.normal(pieces[1], (SEQUENCE_LENGTH, HEAD_TOTAL * DH)), -6.0, 6.0)
    return (gaussian * level_rows).astype(jnp.bfloat16)


def steps_of(stream_key, dims, cuts, smallest, high):
    factor_of = 1.0
    for dim, blocks in cuts:
        steps = jax.random.uniform(jax.random.fold_in(jax.random.fold_in(stream_key, 6), dim), (blocks,), jnp.float32, smallest / len(cuts), high / len(cuts))
        factor_of = factor_of * jnp.repeat(jnp.exp(steps), dims[dim] // blocks).reshape((-1,) + (1,) * (len(dims) - 1 - dim))
    return factor_of


def bell_draw(key, shape, scale, reach, shards=(), held_as=jnp.bfloat16):
    values = jax.random.normal(key, shape, jnp.float32) * scale
    if len(shards) > 0:
        values = steps_of(key, shape, shards, -0.22, 0.18) * values
    return jnp.clip(values, min=-reach, max=reach).astype(held_as)


def setup_inputs(seed: int = 0) -> dict:
    splits = jax.random.split(jax.random.key(seed), 7)
    queries = bell_draw(splits[0], (SEQUENCE_LENGTH, HEAD_TOTAL * DH), 0.3, 1.75, ((0, 64), (1, 8)))
    key_rows = draw_key_rows(jax.random.fold_in(splits[6], 71), 0)
    value_rows = draw_value_rows(jax.random.fold_in(splits[6], 71), 0)
    log_decay = draw_log_decay(jax.random.fold_in(splits[6], 71), 0)
    norm_gain = jnp.clip(1.0 + 0.1 * jax.random.normal(splits[4], (HEAD_TOTAL * DH,), jnp.float32), 0.5, 1.5)
    grad_output = bell_draw(splits[5], (SEQUENCE_LENGTH, HEAD_TOTAL * DH), 1.0, 6.0, ((0, 64), (1, 8)))
    return {"queries": queries, "key_rows": key_rows, "value_rows": value_rows, "log_decay": log_decay, "norm_gain": norm_gain, "grad_output": grad_output}


epsilon = 1e-06
highest = lax.Precision.HIGHEST

def attend(query_all, key_all, value_all, log_decay):
    tok_count, feat_width = query_all.shape
    head_count = log_decay.shape[1]
    head_size = feat_width // head_count
    block_rows = min(128, tok_count)
    block_count = tok_count // block_rows
    block_shape = (block_count, block_rows, head_count, head_size)
    query_blocks = query_all.reshape(block_shape)
    key_blocks = key_all.reshape(block_shape)
    value_blocks = value_all.reshape(block_shape)
    decay_blocks = log_decay.reshape(block_count, block_rows, head_count)
    places = jnp.arange(block_rows)
    lower_mask = (places[:, None] >= places[None, :])[:, :, None]

    def advance(state, pieces):
        query_blk, key_blk, value_blk, decay_blk = pieces
        cumulative = jnp.cumsum(decay_blk, axis=0)
        totals = cumulative[-1]
        differences = cumulative[:, None, :] - cumulative[None, :, :]
        weights = jnp.where(lower_mask, jnp.exp(jnp.where(lower_mask, differences, 0.0)), 0.0)
        scores = jnp.einsum('thd,shd->hts', query_blk, key_blk, precision=highest) * jnp.transpose(weights, (2, 0, 1))
        inside = jnp.einsum('hts,she->the', scores, value_blk, precision=highest)
        outside = jnp.einsum('thd,hde->the', query_blk, state, precision=highest) * jnp.exp(cumulative)[:, :, None]
        trailing = jnp.exp(totals[None, :] - cumulative)[:, :, None]
        state = jnp.exp(totals)[:, None, None] * state + jnp.einsum('shd,she->hde', key_blk * trailing, value_blk, precision=highest)
        return (state, inside + outside)
    initial = jnp.zeros((head_count, head_size, head_size), query_all.dtype)
    _, result = lax.scan(jax.checkpoint(advance), initial, (query_blocks, key_blocks, value_blocks, decay_blocks))
    return result.reshape(tok_count, feat_width)

def reference(queries, key_rows, value_rows, log_decay, norm_gain, grad_output):

    def forward(query_all, key_all, value_all):
        mixed = attend(query_all, key_all, value_all, log_decay)
        mean_sq = lax.optimization_barrier(jnp.mean(mixed * mixed, axis=1, keepdims=True))
        return mixed * lax.rsqrt(mean_sq + epsilon) * norm_gain
    primals = (queries.astype(jnp.float32), key_rows.astype(jnp.float32), value_rows.astype(jnp.float32))
    normed, pullback = jax.vjp(forward, *primals)
    grad_q, grad_k, grad_v = pullback(grad_output.astype(jnp.float32))
    return (normed.astype(jnp.bfloat16), grad_q.astype(jnp.bfloat16), grad_k.astype(jnp.bfloat16), grad_v.astype(jnp.bfloat16))
```

```python
import functools

import jax
import jax.numpy as jnp
from jax import lax
from jax.experimental import pallas as pl
from jax.experimental.pallas import tpu as pltpu
from jax.sharding import Mesh
from jax.sharding import PartitionSpec as P

epsilon = 1e-06
highest = lax.Precision.HIGHEST
f32 = jnp.float32
bf16 = jnp.bfloat16

NN = (((1,), (0,)), ((), ()))
NT = (((1,), (1,)), ((), ()))
TN = (((0,), (0,)), ((), ()))


def halves(wide):
    high = wide.astype(bf16)
    return high, (wide - high.astype(f32)).astype(bf16)


def product(left, right, dims):
    lefts = halves(left) if left.dtype == f32 else (left,)
    rights = halves(right) if right.dtype == f32 else (right,)
    total = None
    for i, a in enumerate(lefts):
        for j, b in enumerate(rights):
            if i + j < 2:
                term = lax.dot_general(a, b, dims, preferred_element_type=f32)
                total = term if total is None else total + term
    return total


def decays(log_decay):
    rows = log_decay.shape[0]
    above = lax.broadcasted_iota(jnp.int32, (rows, rows), 0)
    along = lax.broadcasted_iota(jnp.int32, (rows, rows), 1)
    upper = (above <= along).astype(f32)
    lower = (above >= along).astype(f32)
    tall = lax.dot_general(lower, log_decay, NN, precision=highest, preferred_element_type=f32)
    wide = lax.dot_general(log_decay, upper, TN, precision=highest, preferred_element_type=f32)
    return tall, wide, above >= along


def weights_of(tall, wide, mask, head):
    differences = tall[:, head : head + 1] - wide[head : head + 1, :]
    return jnp.where(mask, jnp.exp(jnp.where(mask, differences, 0.0)), 0.0)


def cols(head, size):
    return slice(head * size, (head + 1) * size)


def states_kernel(heads, members, key_ref, value_ref, decay_ref, out_ref):
    size = key_ref.shape[1] // heads
    per = members // heads
    rows = size // per
    tall, _, _ = decays(decay_ref[...])
    total = tall[-1:, :]
    trailing = jnp.exp(total - tall)
    for head in range(heads):
        key = key_ref[:, cols(head, size)].astype(f32) * trailing[:, head : head + 1]
        state = product(key, value_ref[:, cols(head, size)], TN)
        mark = jnp.broadcast_to(total[:, head : head + 1], (8, size))
        for part in range(per):
            out_ref[head * per + part, :rows, :] = state[part * rows : (part + 1) * rows, :]
            out_ref[head * per + part, rows:, :] = mark


def times(gain, state):
    return (gain[None] * state.reshape(-1, 8, state.shape[-1])).reshape(state.shape)


def group_kernel(members, copies, backward, rows, piece_ref, decay_ref, out_ref):
    total = None
    order = reversed(range(members)) if backward else range(members)
    whole = jnp.zeros(decay_ref.shape[1:], f32)
    for member in order:
        mark = decay_ref[member]
        state = piece_ref[member, :rows, :]
        total = state if total is None else times(jnp.exp(mark), total) + state
        whole = whole + mark
    for copy in range(copies):
        out_ref[copy, :rows, :] = total
        out_ref[copy, rows:, :] = whole


def spread_kernel(members, groups, backward, rows, mine_ref, piece_ref, decay_ref, total_ref, out_ref):
    mine = mine_ref[0]
    running = jnp.zeros((rows, piece_ref.shape[-1]), f32)
    for group in reversed(range(groups)) if backward else range(groups):
        longer = times(jnp.exp(total_ref[group, rows:, :]), running) + total_ref[group, :rows, :]
        running = jnp.where(group > mine if backward else group < mine, longer, running)
    for member in reversed(range(members)) if backward else range(members):
        out_ref[member] = running
        running = times(jnp.exp(decay_ref[member]), running) + piece_ref[member, :rows, :]


def inside_kernel(heads, query_ref, key_ref, value_ref, decay_ref, out_ref):
    size = key_ref.shape[1] // heads
    tall, wide, mask = decays(decay_ref[...])
    for head in range(heads):
        here = cols(head, size)
        scores = product(query_ref[:, here], key_ref[:, here], NT) * weights_of(tall, wide, mask, head)
        out_ref[:, here] = product(scores, value_ref[:, here], NN)


def mixed_kernel(
    heads, query_ref, decay_ref, inside_ref, state_ref, gain_ref, grad_ref, out_ref, sums_ref
):
    size = query_ref.shape[1] // heads
    rows = query_ref.shape[0]
    tall, _, _ = decays(decay_ref[...])
    rising = jnp.exp(tall)
    squares = jnp.zeros((rows, size), f32)
    products = jnp.zeros((rows, size), f32)
    for head in range(heads):
        here = cols(head, size)
        outside = product(query_ref[:, here], state_ref[head], NN)
        mixed = inside_ref[:, here] + outside * rising[:, head : head + 1]
        out_ref[:, here] = mixed
        squares = squares + mixed * mixed
        products = products + grad_ref[:, here].astype(f32) * gain_ref[:, here] * mixed
    ones = jnp.ones((8, size), f32)
    square = lax.dot_general(ones, squares, NT, precision=highest, preferred_element_type=f32)
    product_ = lax.dot_general(ones, products, NT, precision=highest, preferred_element_type=f32)
    sums_ref[0:1, :] = square[0:1, :]
    sums_ref[1:2, :] = product_[0:1, :]


def norm_kernel(
    heads, members, full_width, query_ref, decay_ref, mixed_ref, gain_ref, grad_ref, sums_ref, normed_ref, slope_ref, out_ref
):
    size = query_ref.shape[1] // heads
    per = members // heads
    cut = size // per
    tall, _, _ = decays(decay_ref[...])
    rising = jnp.exp(tall)
    ones = jnp.ones((sums_ref.shape[0], size), f32)
    square = lax.dot_general(sums_ref[:, 0, :], ones, TN, precision=highest, preferred_element_type=f32)
    product_ = lax.dot_general(sums_ref[:, 1, :], ones, TN, precision=highest, preferred_element_type=f32)
    scale = lax.rsqrt(square / full_width + epsilon)
    pull = scale * scale * scale * (product_ / full_width)
    for head in range(heads):
        here = cols(head, size)
        mixed = mixed_ref[:, here]
        gain = gain_ref[:, here]
        normed_ref[:, here] = (mixed * scale * gain).astype(bf16)
        slope = scale * (grad_ref[:, here].astype(f32) * gain) - pull * mixed
        slope_ref[:, here] = slope
        state = product(query_ref[:, here], slope * rising[:, head : head + 1], TN)
        for part in range(per):
            out_ref[head * per + part] = state[part * cut : (part + 1) * cut, :]


def near_kernel(
    heads, query_ref, key_ref, value_ref, decay_ref, state_ref, slope_ref, grad_q_ref, near_k_ref, near_v_ref
):
    size = key_ref.shape[1] // heads
    tall, wide, mask = decays(decay_ref[...])
    rising = jnp.exp(tall)
    for head in range(heads):
        here = cols(head, size)
        query, key, value = query_ref[:, here], key_ref[:, here], value_ref[:, here]
        slope = slope_ref[:, here]
        weights = weights_of(tall, wide, mask, head)
        scores = product(query, key, NT) * weights
        grad_scores = product(slope, value, NT) * weights
        outer = product(slope, state_ref[head], NT) * rising[:, head : head + 1]
        grad_q_ref[:, here] = (product(grad_scores, key, NN) + outer).astype(bf16)
        near_k_ref[:, here] = product(grad_scores, query, TN)
        near_v_ref[:, here] = product(scores, slope, TN)


def far_kernel(heads, key_ref, value_ref, decay_ref, state_ref, near_k_ref, near_v_ref, grad_k_ref, grad_v_ref):
    size = key_ref.shape[1] // heads
    tall, _, _ = decays(decay_ref[...])
    trailing = jnp.exp(tall[-1:, :] - tall)
    for head in range(heads):
        here = cols(head, size)
        late = trailing[:, head : head + 1]
        state = state_ref[head]
        grad_k = near_k_ref[:, here] + product(value_ref[:, here], state, NT) * late
        grad_v = near_v_ref[:, here] + product(key_ref[:, here], state, NN) * late
        grad_k_ref[:, here] = grad_k.astype(bf16)
        grad_v_ref[:, here] = grad_v.astype(bf16)


def call(kernel, outs, *args, scalars=0, flops=0):
    vmem = pl.BlockSpec(memory_space=pltpu.VMEM)
    smem = pl.BlockSpec(memory_space=pltpu.SMEM)
    moved = sum(a.size * a.dtype.itemsize for a in (*args, *outs))
    return pl.pallas_call(
        kernel,
        out_shape=outs,
        in_specs=[smem] * scalars + [vmem] * (len(args) - scalars),
        out_specs=[vmem] * len(outs),
        cost_estimate=pl.CostEstimate(flops=flops, bytes_accessed=moved, transcendentals=0),
        compiler_params=pltpu.CompilerParams(vmem_limit_bytes=32 * 1024 * 1024),
    )(*args)


def shards(groups, tp, queries, key_rows, value_rows, log_decay, norm_gain, grad_output):
    near, far = ("zl", "x"), "zh"
    members = lax.axis_size(near)
    tok_rows, feat_width = queries.shape
    heads = log_decay.shape[1]
    size = feat_width // heads
    rows = heads * size // members
    wide = jax.ShapeDtypeStruct((tok_rows, feat_width), f32)
    narrow = jax.ShapeDtypeStruct((tok_rows, feat_width), bf16)
    gain = norm_gain.reshape(1, feat_width)
    mine = lax.axis_index(far).astype(jnp.int32).reshape(1)
    bind = functools.partial
    shape = jax.ShapeDtypeStruct
    unit = 2 * heads * tok_rows * size * size

    def exchange(parts, axis):
        return lax.all_to_all(parts, axis, 0, 0)

    def carried(pieces, marks, backward):
        (total,) = call(
            bind(group_kernel, members, groups, backward, rows),
            [shape((groups, rows + 8, size), f32)],
            pieces,
            marks,
        )
        totals = exchange(total, far)
        (entering,) = call(
            bind(spread_kernel, members, groups, backward, rows),
            [shape((members, rows, size), f32)],
            mine,
            pieces,
            marks,
            totals,
            scalars=1,
        )
        return exchange(entering, near).reshape(heads, size, size)

    (states,) = call(
        bind(states_kernel, heads, members),
        [shape((members, rows + 8, size), f32)],
        key_rows,
        value_rows,
        log_decay,
        flops=2 * unit,
    )
    pieces = exchange(states, near)
    marks = pieces[:, rows:, :]
    (inside,) = call(
        bind(inside_kernel, heads), [wide], queries, key_rows, value_rows, log_decay, flops=3 * unit
    )
    entry = carried(pieces, marks, False)
    mixed, sums = call(
        bind(mixed_kernel, heads),
        [wide, shape((2, tok_rows), f32)],
        queries,
        log_decay,
        inside,
        entry,
        gain,
        grad_output,
        flops=2 * unit,
    )
    gathered = lax.all_gather(sums, tp)
    normed, slope, back = call(
        bind(norm_kernel, heads, members, feat_width * lax.axis_size(tp)),
        [narrow, wide, shape((members, rows, size), f32)],
        queries,
        log_decay,
        mixed,
        gain,
        grad_output,
        gathered,
        flops=2 * unit,
    )
    back_pieces = exchange(back, near)
    grad_q, near_k, near_v = call(
        bind(near_kernel, heads),
        [narrow, wide, wide],
        queries,
        key_rows,
        value_rows,
        log_decay,
        entry,
        slope,
        flops=13 * unit,
    )
    leaving = carried(back_pieces, marks, True)
    grad_k, grad_v = call(
        bind(far_kernel, heads),
        [narrow, narrow],
        key_rows,
        value_rows,
        log_decay,
        leaving,
        near_k,
        near_v,
        flops=4 * unit,
    )
    return normed, grad_q, grad_k, grad_v


def solution(mesh):
    groups = 4
    folded = Mesh(mesh.devices.reshape(groups, 4, 4, -1), ("zh", "zl", "x", "tp"))
    both = P(("zh", "zl", "x"), "tp")
    return jax.shard_map(
        functools.partial(shards, groups, "tp"),
        mesh=folded,
        in_specs=(both, both, both, both, P("tp"), both),
        out_specs=(both, both, both, both),
        check_vma=False,
    )
```

```python
import functools

import jax
import jax.numpy as jnp
from jax import lax
from jax.experimental import pallas as pl
from jax.experimental.pallas import tpu as pltpu
from jax.sharding import Mesh
from jax.sharding import PartitionSpec as P

epsilon = 1e-06
highest = lax.Precision.HIGHEST
f32 = jnp.float32
bf16 = jnp.bfloat16

NN = (((1,), (0,)), ((), ()))
NT = (((1,), (1,)), ((), ()))
TN = (((0,), (0,)), ((), ()))


def halves(wide):
    high = wide.astype(bf16)
    return high, (wide - high.astype(f32)).astype(bf16)


def product(left, right, dims):
    lefts = halves(left) if left.dtype == f32 else (left,)
    rights = halves(right) if right.dtype == f32 else (right,)
    total = None
    for i, a in enumerate(lefts):
        for j, b in enumerate(rights):
            if i + j < 2:
                term = lax.dot_general(a, b, dims, preferred_element_type=f32)
                total = term if total is None else total + term
    return total


def decays(log_decay):
    rows = log_decay.shape[1]
    above = lax.broadcasted_iota(jnp.int32, (rows, rows), 0)
    along = lax.broadcasted_iota(jnp.int32, (rows, rows), 1)
    upper = (above <= along).astype(f32)
    lower = (above >= along).astype(f32)
    tall = lax.dot_general(lower, log_decay, NT, precision=highest, preferred_element_type=f32)
    wide = lax.dot_general(log_decay, upper, NN, precision=highest, preferred_element_type=f32)
    return tall, wide, above >= along


def weights_of(tall, wide, mask, head):
    differences = tall[:, head : head + 1] - wide[head : head + 1, :]
    return jnp.where(mask, jnp.exp(jnp.where(mask, differences, 0.0)), 0.0)


def cols(head, size):
    return slice(head * size, (head + 1) * size)


def states_kernel(heads, members, key_far, value_far, decay_far, out_ref, key_ref, value_ref, decay_ref, sems):
    size = key_ref.shape[1] // heads
    per = members // heads
    rows = size // per
    copies = [
        pltpu.make_async_copy(source, target, sems.at[i])
        for i, (source, target) in enumerate(
            ((decay_far, decay_ref), (key_far, key_ref), (value_far, value_ref))
        )
    ]
    for copy in copies:
        copy.start()
    copies[0].wait()
    tall, _, _ = decays(decay_ref[...])
    total = tall[-1:, :]
    trailing = jnp.exp(total - tall)
    copies[1].wait()
    copies[2].wait()
    for head in range(heads):
        key = key_ref[:, cols(head, size)].astype(f32) * trailing[:, head : head + 1]
        state = product(key, value_ref[:, cols(head, size)], TN)
        mark = jnp.broadcast_to(total[:, head : head + 1], (8, size))
        for part in range(per):
            out_ref[head * per + part, :rows, :] = state[part * rows : (part + 1) * rows, :]
            out_ref[head * per + part, rows:, :] = mark


def times(gain, state):
    return (gain[None] * state.reshape(-1, 8, state.shape[-1])).reshape(state.shape)


def group_kernel(members, copies, backward, rows, piece_ref, decay_ref, out_ref):
    total = None
    order = reversed(range(members)) if backward else range(members)
    whole = jnp.zeros(decay_ref.shape[1:], f32)
    for member in order:
        mark = decay_ref[member]
        state = piece_ref[member, :rows, :]
        total = state if total is None else times(jnp.exp(mark), total) + state
        whole = whole + mark
    for copy in range(copies):
        out_ref[copy, :rows, :] = total
        out_ref[copy, rows:, :] = whole


def spread_kernel(members, groups, backward, rows, mine_ref, piece_ref, decay_ref, total_ref, out_ref):
    mine = mine_ref[0]
    running = jnp.zeros((rows, piece_ref.shape[-1]), f32)
    for group in reversed(range(groups)) if backward else range(groups):
        longer = times(jnp.exp(total_ref[group, rows:, :]), running) + total_ref[group, :rows, :]
        running = jnp.where(group > mine if backward else group < mine, longer, running)
    for member in reversed(range(members)) if backward else range(members):
        out_ref[member] = running
        running = times(jnp.exp(decay_ref[member]), running) + piece_ref[member, :rows, :]


def inside_kernel(heads, query_ref, key_ref, value_ref, decay_ref, out_ref):
    size = key_ref.shape[1] // heads
    tall, wide, mask = decays(decay_ref[...])
    for head in range(heads):
        here = cols(head, size)
        scores = product(query_ref[:, here], key_ref[:, here], NT) * weights_of(tall, wide, mask, head)
        out_ref[:, here] = product(scores, value_ref[:, here], NN)


def mixed_kernel(
    heads, query_ref, decay_ref, inside_ref, state_ref, gain_ref, grad_ref, out_ref, sums_ref
):
    size = query_ref.shape[1] // heads
    rows = query_ref.shape[0]
    tall, _, _ = decays(decay_ref[...])
    rising = jnp.exp(tall)
    squares = jnp.zeros((rows, size), f32)
    products = jnp.zeros((rows, size), f32)
    for head in range(heads):
        here = cols(head, size)
        outside = product(query_ref[:, here], state_ref[head], NN)
        mixed = inside_ref[:, here] + outside * rising[:, head : head + 1]
        out_ref[:, here] = mixed
        squares = squares + mixed * mixed
        products = products + grad_ref[:, here].astype(f32) * gain_ref[:, here] * mixed
    ones = jnp.ones((8, size), f32)
    square = lax.dot_general(ones, squares, NT, precision=highest, preferred_element_type=f32)
    product_ = lax.dot_general(ones, products, NT, precision=highest, preferred_element_type=f32)
    sums_ref[0:1, :] = square[0:1, :]
    sums_ref[1:2, :] = product_[0:1, :]


def norm_kernel(
    heads, members, full_width, query_ref, decay_ref, mixed_ref, gain_ref, grad_ref, sums_ref, normed_ref, slope_ref, out_ref
):
    size = query_ref.shape[1] // heads
    per = members // heads
    cut = size // per
    tall, _, _ = decays(decay_ref[...])
    rising = jnp.exp(tall)
    ones = jnp.ones((sums_ref.shape[0], size), f32)
    square = lax.dot_general(sums_ref[:, 0, :], ones, TN, precision=highest, preferred_element_type=f32)
    product_ = lax.dot_general(sums_ref[:, 1, :], ones, TN, precision=highest, preferred_element_type=f32)
    scale = lax.rsqrt(square / full_width + epsilon)
    pull = scale * scale * scale * (product_ / full_width)
    for head in range(heads):
        here = cols(head, size)
        mixed = mixed_ref[:, here]
        gain = gain_ref[:, here]
        normed_ref[:, here] = (mixed * scale * gain).astype(bf16)
        slope = scale * (grad_ref[:, here].astype(f32) * gain) - pull * mixed
        slope_ref[:, here] = slope
        state = product(query_ref[:, here], slope * rising[:, head : head + 1], TN)
        for part in range(per):
            out_ref[head * per + part] = state[part * cut : (part + 1) * cut, :]


def near_kernel(
    heads, query_ref, key_ref, value_ref, decay_ref, state_ref, slope_ref, grad_q_ref, near_k_ref, near_v_ref
):
    size = key_ref.shape[1] // heads
    tall, wide, mask = decays(decay_ref[...])
    rising = jnp.exp(tall)
    for head in range(heads):
        here = cols(head, size)
        query, key, value = query_ref[:, here], key_ref[:, here], value_ref[:, here]
        slope = slope_ref[:, here]
        weights = weights_of(tall, wide, mask, head)
        scores = product(query, key, NT) * weights
        grad_scores = product(slope, value, NT) * weights
        outer = product(slope, state_ref[head], NT) * rising[:, head : head + 1]
        grad_q_ref[:, here] = (product(grad_scores, key, NN) + outer).astype(bf16)
        near_k_ref[:, here] = product(grad_scores, query, TN)
        near_v_ref[:, here] = product(scores, slope, TN)


def far_kernel(heads, key_ref, value_ref, decay_ref, state_ref, near_k_ref, near_v_ref, grad_k_ref, grad_v_ref):
    size = key_ref.shape[1] // heads
    tall, _, _ = decays(decay_ref[...])
    trailing = jnp.exp(tall[-1:, :] - tall)
    for head in range(heads):
        here = cols(head, size)
        late = trailing[:, head : head + 1]
        state = state_ref[head]
        grad_k = near_k_ref[:, here] + product(value_ref[:, here], state, NT) * late
        grad_v = near_v_ref[:, here] + product(key_ref[:, here], state, NN) * late
        grad_k_ref[:, here] = grad_k.astype(bf16)
        grad_v_ref[:, here] = grad_v.astype(bf16)


def call(kernel, outs, *args, scalars=0, flops=0, copied=()):
    vmem = pl.BlockSpec(memory_space=pltpu.VMEM)
    hbm = pl.BlockSpec(memory_space=pltpu.HBM)
    smem = pl.BlockSpec(memory_space=pltpu.SMEM)
    moved = sum(a.size * a.dtype.itemsize for a in (*args, *outs))
    return pl.pallas_call(
        kernel,
        out_shape=outs,
        in_specs=[smem] * scalars + [hbm if copied else vmem] * (len(args) - scalars),
        out_specs=[vmem] * len(outs),
        scratch_shapes=[pltpu.VMEM(a.shape, a.dtype) for a in copied]
        + ([pltpu.SemaphoreType.DMA((len(copied),))] if copied else []),
        cost_estimate=pl.CostEstimate(flops=flops, bytes_accessed=moved, transcendentals=0),
        compiler_params=pltpu.CompilerParams(vmem_limit_bytes=12 * 1024 * 1024),
    )(*args)


def shards(groups, tp, queries, key_rows, value_rows, log_decay, norm_gain, grad_output):
    near, far = ("zl", "x"), "zh"
    members = lax.axis_size(near)
    tok_rows, feat_width = queries.shape
    heads = log_decay.shape[1]
    size = feat_width // heads
    rows = heads * size // members
    wide = jax.ShapeDtypeStruct((tok_rows, feat_width), f32)
    narrow = jax.ShapeDtypeStruct((tok_rows, feat_width), bf16)
    gain = norm_gain.reshape(1, feat_width)
    log_decay = log_decay.T
    mine = lax.axis_index(far).astype(jnp.int32).reshape(1)
    bind = functools.partial
    shape = jax.ShapeDtypeStruct
    unit = 2 * heads * tok_rows * size * size

    def exchange(parts, axis):
        return lax.all_to_all(parts, axis, 0, 0)

    def carried(pieces, marks, backward):
        (total,) = call(
            bind(group_kernel, members, groups, backward, rows),
            [shape((groups, rows + 8, size), f32)],
            pieces,
            marks,
        )
        totals = exchange(total, far)
        (entering,) = call(
            bind(spread_kernel, members, groups, backward, rows),
            [shape((members, rows, size), f32)],
            mine,
            pieces,
            marks,
            totals,
            scalars=1,
        )
        return exchange(entering, near).reshape(heads, size, size)

    (states,) = call(
        bind(states_kernel, heads, members),
        [shape((members, rows + 8, size), f32)],
        key_rows,
        value_rows,
        log_decay,
        flops=2 * unit,
        copied=(key_rows, value_rows, log_decay),
    )
    pieces = exchange(states, near)
    marks = pieces[:, rows:, :]
    (inside,) = call(
        bind(inside_kernel, heads), [wide], queries, key_rows, value_rows, log_decay, flops=3 * unit
    )
    entry = carried(pieces, marks, False)
    mixed, sums = call(
        bind(mixed_kernel, heads),
        [wide, shape((2, tok_rows), f32)],
        queries,
        log_decay,
        inside,
        entry,
        gain,
        grad_output,
        flops=2 * unit,
    )
    gathered = lax.all_gather(sums, tp)
    normed, slope, back = call(
        bind(norm_kernel, heads, members, feat_width * lax.axis_size(tp)),
        [narrow, wide, shape((members, rows, size), f32)],
        queries,
        log_decay,
        mixed,
        gain,
        grad_output,
        gathered,
        flops=2 * unit,
    )
    back_pieces = exchange(back, near)
    grad_q, near_k, near_v = call(
        bind(near_kernel, heads),
        [narrow, wide, wide],
        queries,
        key_rows,
        value_rows,
        log_decay,
        entry,
        slope,
        flops=13 * unit,
    )
    leaving = carried(back_pieces, marks, True)
    grad_k, grad_v = call(
        bind(far_kernel, heads),
        [narrow, narrow],
        key_rows,
        value_rows,
        log_decay,
        leaving,
        near_k,
        near_v,
        flops=4 * unit,
    )
    return normed, grad_q, grad_k, grad_v


def solution(mesh):
    groups = 4
    folded = Mesh(mesh.devices.reshape(groups, 4, 4, -1), ("zh", "zl", "x", "tp"))
    both = P(("zh", "zl", "x"), "tp")
    return jax.shard_map(
        functools.partial(shards, groups, "tp"),
        mesh=folded,
        in_specs=(both, both, both, both, P("tp"), both),
        out_specs=(both, both, both, both),
        check_vma=False,
    )
```

```python
import functools

import jax
import jax.numpy as jnp
from jax import lax
from jax.experimental import pallas as pl
from jax.experimental.pallas import tpu as pltpu
from jax.sharding import Mesh
from jax.sharding import PartitionSpec as P

epsilon = 1e-06
highest = lax.Precision.HIGHEST
f32 = jnp.float32
bf16 = jnp.bfloat16

NN = (((1,), (0,)), ((), ()))
NT = (((1,), (1,)), ((), ()))
TN = (((0,), (0,)), ((), ()))


def halves(wide):
    high = wide.astype(bf16)
    return high, (wide - high.astype(f32)).astype(bf16)


def product(left, right, dims):
    lefts = halves(left) if left.dtype == f32 else (left,)
    rights = halves(right) if right.dtype == f32 else (right,)
    total = None
    for i, a in enumerate(lefts):
        for j, b in enumerate(rights):
            if i + j < 2:
                term = lax.dot_general(a, b, dims, preferred_element_type=f32)
                total = term if total is None else total + term
    return total


def decays(log_decay):
    rows = log_decay.shape[1]
    above = lax.broadcasted_iota(jnp.int32, (rows, rows), 0)
    along = lax.broadcasted_iota(jnp.int32, (rows, rows), 1)
    upper = (above <= along).astype(f32)
    lower = (above >= along).astype(f32)
    tall = lax.dot_general(lower, log_decay, NT, precision=highest, preferred_element_type=f32)
    wide = lax.dot_general(log_decay, upper, NN, precision=highest, preferred_element_type=f32)
    return tall, wide, above >= along


def weights_of(tall, wide, mask, head):
    differences = tall[:, head : head + 1] - wide[head : head + 1, :]
    return jnp.where(mask, jnp.exp(jnp.where(mask, differences, 0.0)), 0.0)


def cols(head, size):
    return slice(head * size, (head + 1) * size)


def states_kernel(heads, members, key_far, value_far, decay_far, out_ref, key_ref, value_ref, decay_ref, sems):
    size = key_ref.shape[1] // heads
    per = members // heads
    rows = size // per
    copies = [
        pltpu.make_async_copy(source, target, sems.at[i])
        for i, (source, target) in enumerate(
            ((decay_far, decay_ref), (key_far, key_ref), (value_far, value_ref))
        )
    ]
    for copy in copies:
        copy.start()
    copies[0].wait()
    tall, _, _ = decays(decay_ref[...])
    total = tall[-1:, :]
    trailing = jnp.exp(total - tall)
    copies[1].wait()
    copies[2].wait()
    for head in range(heads):
        key = key_ref[:, cols(head, size)].astype(f32) * trailing[:, head : head + 1]
        state = product(key, value_ref[:, cols(head, size)], TN)
        mark = jnp.broadcast_to(total[:, head : head + 1], (8, size))
        for part in range(per):
            out_ref[head * per + part, :rows, :] = state[part * rows : (part + 1) * rows, :]
            out_ref[head * per + part, rows:, :] = mark


def times(gain, state):
    return (gain[None] * state.reshape(-1, 8, state.shape[-1])).reshape(state.shape)


def group_kernel(members, copies, backward, rows, piece_ref, decay_ref, out_ref):
    total = None
    order = reversed(range(members)) if backward else range(members)
    whole = jnp.zeros(decay_ref.shape[1:], f32)
    for member in order:
        mark = decay_ref[member]
        state = piece_ref[member, :rows, :]
        total = state if total is None else times(jnp.exp(mark), total) + state
        whole = whole + mark
    for copy in range(copies):
        out_ref[copy, :rows, :] = total
        out_ref[copy, rows:, :] = whole


def spread_kernel(members, groups, backward, rows, mine_ref, piece_ref, decay_ref, total_ref, out_ref):
    mine = mine_ref[0]
    running = jnp.zeros((rows, piece_ref.shape[-1]), f32)
    for group in reversed(range(groups)) if backward else range(groups):
        longer = times(jnp.exp(total_ref[group, rows:, :]), running) + total_ref[group, :rows, :]
        running = jnp.where(group > mine if backward else group < mine, longer, running)
    for member in reversed(range(members)) if backward else range(members):
        out_ref[member] = running
        running = times(jnp.exp(decay_ref[member]), running) + piece_ref[member, :rows, :]


def inside_kernel(heads, query_ref, key_ref, value_ref, decay_ref, out_ref):
    size = key_ref.shape[1] // heads
    tall, wide, mask = decays(decay_ref[...])
    for head in range(heads):
        here = cols(head, size)
        scores = product(query_ref[:, here], key_ref[:, here], NT) * weights_of(tall, wide, mask, head)
        out_ref[:, here] = product(scores, value_ref[:, here], NN)


def mixed_kernel(
    heads, query_ref, decay_ref, inside_ref, state_ref, gain_ref, grad_ref, out_ref, sums_ref
):
    size = query_ref.shape[1] // heads
    rows = query_ref.shape[0]
    tall, _, _ = decays(decay_ref[...])
    rising = jnp.exp(tall)
    squares = jnp.zeros((rows, size), f32)
    products = jnp.zeros((rows, size), f32)
    for head in range(heads):
        here = cols(head, size)
        outside = product(query_ref[:, here], state_ref[head], NN)
        mixed = inside_ref[:, here] + outside * rising[:, head : head + 1]
        out_ref[:, here] = mixed
        squares = squares + mixed * mixed
        products = products + grad_ref[:, here].astype(f32) * gain_ref[:, here] * mixed
    ones = jnp.ones((8, size), f32)
    square = lax.dot_general(ones, squares, NT, precision=highest, preferred_element_type=f32)
    product_ = lax.dot_general(ones, products, NT, precision=highest, preferred_element_type=f32)
    sums_ref[0:1, :] = square[0:1, :]
    sums_ref[1:2, :] = product_[0:1, :]


def norm_kernel(
    heads, members, full_width, query_ref, decay_ref, mixed_ref, gain_ref, grad_ref, sums_ref, normed_ref, slope_ref, out_ref
):
    size = query_ref.shape[1] // heads
    per = members // heads
    cut = size // per
    tall, _, _ = decays(decay_ref[...])
    rising = jnp.exp(tall)
    ones = jnp.ones((sums_ref.shape[0], size), f32)
    square = lax.dot_general(sums_ref[:, 0, :], ones, TN, precision=highest, preferred_element_type=f32)
    product_ = lax.dot_general(sums_ref[:, 1, :], ones, TN, precision=highest, preferred_element_type=f32)
    scale = lax.rsqrt(square / full_width + epsilon)
    pull = scale * scale * scale * (product_ / full_width)
    for head in range(heads):
        here = cols(head, size)
        mixed = mixed_ref[:, here]
        gain = gain_ref[:, here]
        normed_ref[:, here] = (mixed * scale * gain).astype(bf16)
        slope = scale * (grad_ref[:, here].astype(f32) * gain) - pull * mixed
        slope_ref[:, here] = slope
        state = product(query_ref[:, here], slope * rising[:, head : head + 1], TN)
        for part in range(per):
            out_ref[head * per + part] = state[part * cut : (part + 1) * cut, :]


def near_kernel(
    heads, query_ref, key_ref, value_ref, decay_ref, state_ref, slope_ref, grad_q_ref, near_k_ref, near_v_ref
):
    size = key_ref.shape[1] // heads
    tall, wide, mask = decays(decay_ref[...])
    rising = jnp.exp(tall)
    for head in range(heads):
        here = cols(head, size)
        query, key, value = query_ref[:, here], key_ref[:, here], value_ref[:, here]
        slope = slope_ref[:, here]
        weights = weights_of(tall, wide, mask, head)
        scores = product(query, key, NT) * weights
        grad_scores = product(slope, value, NT) * weights
        outer = product(slope, state_ref[head], NT) * rising[:, head : head + 1]
        grad_q_ref[:, here] = (product(grad_scores, key, NN) + outer).astype(bf16)
        near_k_ref[head] = product(grad_scores, query, TN)
        near_v_ref[:, here] = product(scores, slope, TN)


def far_kernel(heads, key_ref, value_ref, decay_ref, state_ref, near_k_ref, near_v_ref, grad_k_ref, grad_v_ref):
    size = key_ref.shape[1] // heads
    tall, _, _ = decays(decay_ref[...])
    trailing = jnp.exp(tall[-1:, :] - tall)
    for head in range(heads):
        here = cols(head, size)
        late = trailing[:, head : head + 1]
        state = state_ref[head]
        grad_k = near_k_ref[head] + product(value_ref[:, here], state, NT) * late
        grad_v = near_v_ref[:, here] + product(key_ref[:, here], state, NN) * late
        grad_k_ref[:, here] = grad_k.astype(bf16)
        grad_v_ref[:, here] = grad_v.astype(bf16)


def call(kernel, outs, *args, scalars=0, flops=0, copied=(), aliases=None):
    vmem = pl.BlockSpec(memory_space=pltpu.VMEM)
    hbm = pl.BlockSpec(memory_space=pltpu.HBM)
    smem = pl.BlockSpec(memory_space=pltpu.SMEM)
    if copied:
        args = [pltpu.with_memory_space_constraint(a, pltpu.HBM) for a in args]
    moved = sum(a.size * a.dtype.itemsize for a in (*args, *outs))
    return pl.pallas_call(
        kernel,
        out_shape=outs,
        in_specs=[smem] * scalars + [hbm if copied else vmem] * (len(args) - scalars),
        out_specs=[vmem] * len(outs),
        input_output_aliases=aliases or {},
        scratch_shapes=[pltpu.VMEM(a.shape, a.dtype) for a in copied]
        + ([pltpu.SemaphoreType.DMA((len(copied),))] if copied else []),
        cost_estimate=pl.CostEstimate(flops=flops, bytes_accessed=moved, transcendentals=0),
        compiler_params=pltpu.CompilerParams(vmem_limit_bytes=12 * 1024 * 1024),
    )(*args)


def shards(groups, tp, queries, key_rows, value_rows, log_decay, norm_gain, grad_output):
    near, far = ("zl", "x"), "zh"
    members = lax.axis_size(near)
    tok_rows, feat_width = queries.shape
    heads = log_decay.shape[1]
    size = feat_width // heads
    rows = heads * size // members
    wide = jax.ShapeDtypeStruct((tok_rows, feat_width), f32)
    narrow = jax.ShapeDtypeStruct((tok_rows, feat_width), bf16)
    gain = norm_gain.reshape(1, feat_width)
    log_decay = log_decay.T
    mine = lax.axis_index(far).astype(jnp.int32).reshape(1)
    bind = functools.partial
    shape = jax.ShapeDtypeStruct
    unit = 2 * heads * tok_rows * size * size

    def exchange(parts, axis):
        return lax.all_to_all(parts, axis, 0, 0)

    def carried(pieces, marks, backward):
        (total,) = call(
            bind(group_kernel, members, groups, backward, rows),
            [shape((groups, rows + 8, size), f32)],
            pieces,
            marks,
        )
        totals = exchange(total, far)
        (entering,) = call(
            bind(spread_kernel, members, groups, backward, rows),
            [shape((members, rows, size), f32)],
            mine,
            pieces,
            marks,
            totals,
            scalars=1,
        )
        return exchange(entering, near).reshape(heads, size, size)

    (states,) = call(
        bind(states_kernel, heads, members),
        [shape((members, rows + 8, size), f32)],
        key_rows,
        value_rows,
        log_decay,
        flops=2 * unit,
        copied=(key_rows, value_rows, log_decay),
    )
    pieces = exchange(states, near)
    marks = pieces[:, rows:, :]
    (inside,) = call(
        bind(inside_kernel, heads), [wide], queries, key_rows, value_rows, log_decay, flops=3 * unit
    )
    entry = carried(pieces, marks, False)
    mixed, sums = call(
        bind(mixed_kernel, heads),
        [wide, shape((2, tok_rows), f32)],
        queries,
        log_decay,
        inside,
        entry,
        gain,
        grad_output,
        flops=2 * unit,
    )
    gathered = lax.all_gather(sums, tp)
    normed, slope, back = call(
        bind(norm_kernel, heads, members, feat_width * lax.axis_size(tp)),
        [narrow, wide, shape((members, rows, size), f32)],
        queries,
        log_decay,
        mixed,
        gain,
        grad_output,
        gathered,
        flops=2 * unit,
    )
    back_pieces = exchange(back, near)
    grad_q, near_k, near_v = call(
        bind(near_kernel, heads),
        [narrow, shape((heads, size, size), f32), wide],
        queries,
        key_rows,
        value_rows,
        log_decay,
        entry,
        slope,
        flops=13 * unit,
        aliases={4: 1, 5: 2},
    )
    leaving = carried(back_pieces, marks, True)
    grad_k, grad_v = call(
        bind(far_kernel, heads),
        [narrow, narrow],
        key_rows,
        value_rows,
        log_decay,
        leaving,
        near_k,
        near_v,
        flops=4 * unit,
    )
    return normed, grad_q, grad_k, grad_v


def solution(mesh):
    groups = 4
    folded = Mesh(mesh.devices.reshape(groups, 4, 4, -1), ("zh", "zl", "x", "tp"))
    both = P(("zh", "zl", "x"), "tp")
    return jax.shard_map(
        functools.partial(shards, groups, "tp"),
        mesh=folded,
        in_specs=(both, both, both, both, P("tp"), both),
        out_specs=(both, both, both, both),
        check_vma=False,
    )
```

```python
import functools

import jax
import jax.numpy as jnp
from jax import lax
from jax.experimental import pallas as pl
from jax.experimental.pallas import tpu as pltpu
from jax.sharding import PartitionSpec as P

epsilon = 1e-06
highest = lax.Precision.HIGHEST
f32 = jnp.float32
bf16 = jnp.bfloat16

NN = (((1,), (0,)), ((), ()))
NT = (((1,), (1,)), ((), ()))
TN = (((0,), (0,)), ((), ()))


def halves(wide):
    high = wide.astype(bf16)
    return high, (wide - high.astype(f32)).astype(bf16)


def product(left, right, dims):
    lefts = halves(left) if left.dtype == f32 else (left,)
    rights = halves(right) if right.dtype == f32 else (right,)
    total = None
    for i, a in enumerate(lefts):
        for j, b in enumerate(rights):
            if i + j < 2:
                term = lax.dot_general(a, b, dims, preferred_element_type=f32)
                total = term if total is None else total + term
    return total


def decays(log_decay):
    rows = log_decay.shape[1]
    above = lax.broadcasted_iota(jnp.int32, (rows, rows), 0)
    along = lax.broadcasted_iota(jnp.int32, (rows, rows), 1)
    upper = (above <= along).astype(f32)
    lower = (above >= along).astype(f32)
    tall = lax.dot_general(lower, log_decay, NT, precision=highest, preferred_element_type=f32)
    wide = lax.dot_general(log_decay, upper, NN, precision=highest, preferred_element_type=f32)
    return tall, wide, above >= along


def weights_of(tall, wide, mask, head):
    differences = tall[:, head : head + 1] - wide[head : head + 1, :]
    return jnp.where(mask, jnp.exp(jnp.where(mask, differences, 0.0)), 0.0)


def group_here(heads):
    return lax.div(lax.axis_index("ctx"), 2 * heads)


def turned(head, heads):
    half = lax.axis_size("ctx") // (2 * heads) // 2
    return (head + jnp.where(group_here(heads) < half, 0, heads // 2)) & (heads - 1)


def cols(head, size):
    return slice(head * size, (head + 1) * size)


def states_kernel(heads, members, key_far, value_far, decay_far, out_ref, key_ref, value_ref, decay_ref, sems):
    size = key_ref.shape[1] // heads
    per = members // heads
    rows = size // per
    copies = [
        pltpu.make_async_copy(source, target, sems.at[i])
        for i, (source, target) in enumerate(
            ((decay_far, decay_ref), (key_far, key_ref), (value_far, value_ref))
        )
    ]
    for copy in copies:
        copy.start()
    copies[0].wait()
    tall, _, _ = decays(decay_ref[...])
    total = tall[-1:, :]
    trailing = jnp.exp(total - tall)
    copies[1].wait()
    copies[2].wait()
    for head in range(heads):
        key = key_ref[:, cols(head, size)].astype(f32) * trailing[:, head : head + 1]
        state = product(key, value_ref[:, cols(head, size)], TN)
        mark = jnp.broadcast_to(total[:, head : head + 1], (8, size))
        first = turned(head, heads) * per
        for part in range(per):
            out_ref[first + part, :rows, :] = state[part * rows : (part + 1) * rows, :]
            out_ref[first + part, rows:, :] = mark


def times(gain, state):
    return (gain[None] * state.reshape(-1, 8, state.shape[-1])).reshape(state.shape)


def group_kernel(members, copies, backward, rows, piece_ref, decay_ref, out_ref):
    total = None
    order = reversed(range(members)) if backward else range(members)
    whole = jnp.zeros(decay_ref.shape[1:], f32)
    for member in order:
        mark = decay_ref[member]
        state = piece_ref[member, :rows, :]
        total = state if total is None else times(jnp.exp(mark), total) + state
        whole = whole + mark
    for copy in range(copies):
        out_ref[copy, :rows, :] = total
        out_ref[copy, rows:, :] = whole


def spread_kernel(members, groups, backward, rows, piece_ref, decay_ref, total_ref, out_ref):
    mine = group_here(members // 2)
    running = jnp.zeros((rows, piece_ref.shape[-1]), f32)
    for group in reversed(range(groups)) if backward else range(groups):
        longer = times(jnp.exp(total_ref[group, rows:, :]), running) + total_ref[group, :rows, :]
        running = jnp.where(group > mine if backward else group < mine, longer, running)
    for member in reversed(range(members)) if backward else range(members):
        out_ref[member] = running
        running = times(jnp.exp(decay_ref[member]), running) + piece_ref[member, :rows, :]


def inside_kernel(heads, query_ref, key_ref, value_ref, decay_ref, out_ref):
    size = key_ref.shape[1] // heads
    tall, wide, mask = decays(decay_ref[...])
    for head in range(heads):
        here = cols(head, size)
        scores = product(query_ref[:, here], key_ref[:, here], NT) * weights_of(tall, wide, mask, head)
        out_ref[:, here] = product(scores, value_ref[:, here], NN)


def mixed_kernel(
    heads, query_ref, decay_ref, inside_ref, state_ref, gain_ref, grad_ref, out_ref, sums_ref
):
    size = query_ref.shape[1] // heads
    rows = query_ref.shape[0]
    tall, _, _ = decays(decay_ref[...])
    rising = jnp.exp(tall)
    squares = jnp.zeros((rows, size), f32)
    products = jnp.zeros((rows, size), f32)
    for head in range(heads):
        here = cols(head, size)
        outside = product(query_ref[:, here], state_ref[turned(head, heads)], NN)
        mixed = inside_ref[:, here] + outside * rising[:, head : head + 1]
        out_ref[:, here] = mixed
        squares = squares + mixed * mixed
        products = products + grad_ref[:, here].astype(f32) * gain_ref[:, here] * mixed
    ones = jnp.ones((8, size), f32)
    square = lax.dot_general(ones, squares, NT, precision=highest, preferred_element_type=f32)
    product_ = lax.dot_general(ones, products, NT, precision=highest, preferred_element_type=f32)
    sums_ref[0:1, :] = square[0:1, :]
    sums_ref[1:2, :] = product_[0:1, :]


def norm_kernel(
    heads, members, full_width, query_ref, decay_ref, mixed_ref, gain_ref, grad_ref, sums_ref, normed_ref, slope_ref, out_ref
):
    size = query_ref.shape[1] // heads
    per = members // heads
    cut = size // per
    tall, _, _ = decays(decay_ref[...])
    rising = jnp.exp(tall)
    ones = jnp.ones((sums_ref.shape[0], size), f32)
    square = lax.dot_general(sums_ref[:, 0, :], ones, TN, precision=highest, preferred_element_type=f32)
    product_ = lax.dot_general(sums_ref[:, 1, :], ones, TN, precision=highest, preferred_element_type=f32)
    scale = lax.rsqrt(square / full_width + epsilon)
    pull = scale * scale * scale * (product_ / full_width)
    for head in range(heads):
        here = cols(head, size)
        mixed = mixed_ref[:, here]
        gain = gain_ref[:, here]
        normed_ref[:, here] = (mixed * scale * gain).astype(bf16)
        slope = scale * (grad_ref[:, here].astype(f32) * gain) - pull * mixed
        slope_ref[:, here] = slope
        state = product(query_ref[:, here], slope * rising[:, head : head + 1], TN)
        first = turned(head, heads) * per
        for part in range(per):
            out_ref[first + part] = state[part * cut : (part + 1) * cut, :]


def near_kernel(
    heads, query_ref, key_ref, value_ref, decay_ref, state_ref, slope_ref, grad_q_ref, near_k_ref, near_v_ref
):
    size = key_ref.shape[1] // heads
    tall, wide, mask = decays(decay_ref[...])
    rising = jnp.exp(tall)
    for head in range(heads):
        here = cols(head, size)
        query, key, value = query_ref[:, here], key_ref[:, here], value_ref[:, here]
        slope = slope_ref[:, here]
        weights = weights_of(tall, wide, mask, head)
        scores = product(query, key, NT) * weights
        grad_scores = product(slope, value, NT) * weights
        there = turned(head, heads)
        outer = product(slope, state_ref[there], NT) * rising[:, head : head + 1]
        grad_q_ref[:, here] = (product(grad_scores, key, NN) + outer).astype(bf16)
        near_k_ref[there] = product(grad_scores, query, TN)
        near_v_ref[:, here] = product(scores, slope, TN)


def far_kernel(heads, key_ref, value_ref, decay_ref, state_ref, near_k_ref, near_v_ref, grad_k_ref, grad_v_ref):
    size = key_ref.shape[1] // heads
    tall, _, _ = decays(decay_ref[...])
    trailing = jnp.exp(tall[-1:, :] - tall)
    for head in range(heads):
        here = cols(head, size)
        late = trailing[:, head : head + 1]
        there = turned(head, heads)
        state = state_ref[there]
        grad_k = near_k_ref[there] + product(value_ref[:, here], state, NT) * late
        grad_v = near_v_ref[:, here] + product(key_ref[:, here], state, NN) * late
        grad_k_ref[:, here] = grad_k.astype(bf16)
        grad_v_ref[:, here] = grad_v.astype(bf16)


def call(kernel, outs, *args, flops=0, copied=(), aliases=None):
    vmem = pl.BlockSpec(memory_space=pltpu.VMEM)
    hbm = pl.BlockSpec(memory_space=pltpu.HBM)
    if copied:
        args = [pltpu.with_memory_space_constraint(a, pltpu.HBM) for a in args]
    moved = sum(a.size * a.dtype.itemsize for a in (*args, *outs))
    return pl.pallas_call(
        kernel,
        out_shape=outs,
        in_specs=[hbm if copied else vmem] * len(args),
        out_specs=[vmem] * len(outs),
        input_output_aliases=aliases or {},
        scratch_shapes=[pltpu.VMEM(a.shape, a.dtype) for a in copied]
        + ([pltpu.SemaphoreType.DMA((len(copied),))] if copied else []),
        cost_estimate=pl.CostEstimate(flops=flops, bytes_accessed=moved, transcendentals=0),
        compiler_params=pltpu.CompilerParams(vmem_limit_bytes=12 * 1024 * 1024),
    )(*args)


def levels(count, heads):
    members = 2 * heads
    groups = count // members
    near = [[group * members + member for member in range(members)] for group in range(groups)]
    far = [
        [
            group * members + (piece + (members // 2 if group >= groups // 2 else 0)) % members
            for group in range(groups)
        ]
        for piece in range(members)
    ]
    return groups, members, near, far


def shards(queries, key_rows, value_rows, log_decay, norm_gain, grad_output):
    tok_rows, feat_width = queries.shape
    heads = log_decay.shape[1]
    groups, members, near, far = levels(lax.axis_size("ctx"), heads)
    size = feat_width // heads
    rows = heads * size // members
    wide = jax.ShapeDtypeStruct((tok_rows, feat_width), f32)
    narrow = jax.ShapeDtypeStruct((tok_rows, feat_width), bf16)
    gain = norm_gain.reshape(1, feat_width)
    log_decay = log_decay.T
    bind = functools.partial
    shape = jax.ShapeDtypeStruct
    unit = 2 * heads * tok_rows * size * size

    def exchange(parts, lists):
        return lax.all_to_all(parts, "ctx", 0, 0, axis_index_groups=lists)

    def carried(pieces, marks, backward):
        (total,) = call(
            bind(group_kernel, members, groups, backward, rows),
            [shape((groups, rows + 8, size), f32)],
            pieces,
            marks,
        )
        totals = exchange(total, far)
        (entering,) = call(
            bind(spread_kernel, members, groups, backward, rows),
            [shape((members, rows, size), f32)],
                pieces,
            marks,
            totals,
            )
        return exchange(entering, near).reshape(heads, size, size)

    (states,) = call(
        bind(states_kernel, heads, members),
        [shape((members, rows + 8, size), f32)],
        key_rows,
        value_rows,
        log_decay,
        flops=2 * unit,
        copied=(key_rows, value_rows, log_decay),
    )
    pieces = exchange(states, near)
    marks = pieces[:, rows:, :]
    (inside,) = call(
        bind(inside_kernel, heads), [wide], queries, key_rows, value_rows, log_decay, flops=3 * unit
    )
    entry = carried(pieces, marks, False)
    mixed, sums = call(
        bind(mixed_kernel, heads),
        [wide, shape((2, tok_rows), f32)],
        queries,
        log_decay,
        inside,
        entry,
        gain,
        grad_output,
        flops=2 * unit,
    )
    gathered = lax.all_gather(sums, "tp")
    normed, slope, back = call(
        bind(norm_kernel, heads, members, feat_width * lax.axis_size("tp")),
        [narrow, wide, shape((members, rows, size), f32)],
        queries,
        log_decay,
        mixed,
        gain,
        grad_output,
        gathered,
        flops=2 * unit,
    )
    back_pieces = exchange(back, near)
    grad_q, near_k, near_v = call(
        bind(near_kernel, heads),
        [narrow, shape((heads, size, size), f32), wide],
        queries,
        key_rows,
        value_rows,
        log_decay,
        entry,
        slope,
        flops=13 * unit,
        aliases={4: 1, 5: 2},
    )
    leaving = carried(back_pieces, marks, True)
    grad_k, grad_v = call(
        bind(far_kernel, heads),
        [narrow, narrow],
        key_rows,
        value_rows,
        log_decay,
        leaving,
        near_k,
        near_v,
        flops=4 * unit,
    )
    return normed, grad_q, grad_k, grad_v


def solution(mesh):
    both = P("ctx", "tp")
    return jax.shard_map(
        shards,
        mesh=mesh,
        in_specs=(both, both, both, both, P("tp"), both),
        out_specs=(both, both, both, both),
        check_vma=False,
    )
```

```python
import functools

import jax
import jax.numpy as jnp
from jax import lax
from jax.experimental import pallas as pl
from jax.experimental.pallas import tpu as pltpu
from jax.sharding import PartitionSpec as P

epsilon = 1e-06
highest = lax.Precision.HIGHEST
f32 = jnp.float32
bf16 = jnp.bfloat16

NN = (((1,), (0,)), ((), ()))
NT = (((1,), (1,)), ((), ()))
TN = (((0,), (0,)), ((), ()))


def halves(wide):
    high = wide.astype(bf16)
    return high, (wide - high.astype(f32)).astype(bf16)


def product(left, right, dims):
    lefts = halves(left) if left.dtype == f32 else (left,)
    rights = halves(right) if right.dtype == f32 else (right,)
    total = None
    for i, a in enumerate(lefts):
        for j, b in enumerate(rights):
            if i + j < 2:
                term = lax.dot_general(a, b, dims, preferred_element_type=f32)
                total = term if total is None else total + term
    return total


def decays(log_decay):
    rows = log_decay.shape[1]
    above = lax.broadcasted_iota(jnp.int32, (rows, rows), 0)
    along = lax.broadcasted_iota(jnp.int32, (rows, rows), 1)
    upper = (above <= along).astype(f32)
    lower = (above >= along).astype(f32)
    tall = lax.dot_general(lower, log_decay, NT, precision=highest, preferred_element_type=f32)
    wide = lax.dot_general(log_decay, upper, NN, precision=highest, preferred_element_type=f32)
    return tall, wide, above >= along


def weights_of(tall, wide, mask, head):
    differences = tall[:, head : head + 1] - wide[head : head + 1, :]
    return jnp.where(mask, jnp.exp(jnp.where(mask, differences, 0.0)), 0.0)


def group_here(heads):
    return lax.div(lax.axis_index("ctx"), 2 * heads)


def rank(place):
    return place % 4 * 4 + place // 4


def turned(head, heads):
    half = lax.axis_size("ctx") // (2 * heads) // 2
    return head ^ jnp.where(group_here(heads) < half, 0, 1)


def cols(head, size):
    return slice(head * size, (head + 1) * size)


def states_kernel(
    heads, members, query_far, key_far, value_far, decay_far, out_ref, inside_ref, query_ref, key_ref, value_ref, decay_ref, sems
):
    size = key_ref.shape[1] // heads
    per = members // heads
    rows = size // per
    copies = [
        pltpu.make_async_copy(source, target, sems.at[i])
        for i, (source, target) in enumerate(
            ((decay_far, decay_ref), (key_far, key_ref), (value_far, value_ref), (query_far, query_ref))
        )
    ]
    for copy in copies:
        copy.start()
    copies[0].wait()
    tall, wide, mask = decays(decay_ref[...])
    total = tall[-1:, :]
    trailing = jnp.exp(total - tall)
    for copy in copies[1:]:
        copy.wait()
    for head in range(heads):
        here = cols(head, size)
        key, value = key_ref[:, here], value_ref[:, here]
        state = product(key.astype(f32) * trailing[:, head : head + 1], value, TN)
        mark = jnp.broadcast_to(total[:, head : head + 1], (8, size))
        first = turned(head, heads) * per
        for part in range(per):
            out_ref[first + part, :rows, :] = state[part * rows : (part + 1) * rows, :]
            out_ref[first + part, rows:, :] = mark
        scores = product(query_ref[:, here], key, NT) * weights_of(tall, wide, mask, head)
        inside_ref[:, here] = product(scores, value, NN)


def times(gain, state):
    return (gain[None] * state.reshape(-1, 8, state.shape[-1])).reshape(state.shape)


def group_kernel(members, copies, backward, rows, piece_ref, decay_ref, out_ref):
    total = None
    order = reversed(range(members)) if backward else range(members)
    whole = jnp.zeros(decay_ref.shape[1:], f32)
    for member in order:
        mark = decay_ref[rank(member)]
        state = piece_ref[rank(member), :rows, :]
        total = state if total is None else times(jnp.exp(mark), total) + state
        whole = whole + mark
    for copy in range(copies):
        out_ref[copy, :rows, :] = total
        out_ref[copy, rows:, :] = whole


def spread_kernel(members, groups, backward, rows, piece_ref, decay_ref, total_ref, out_ref):
    mine = group_here(members // 2)
    running = jnp.zeros((rows, piece_ref.shape[-1]), f32)
    for group in reversed(range(groups)) if backward else range(groups):
        longer = times(jnp.exp(total_ref[group, rows:, :]), running) + total_ref[group, :rows, :]
        running = jnp.where(group > mine if backward else group < mine, longer, running)
    for member in reversed(range(members)) if backward else range(members):
        place = rank(member)
        out_ref[place] = running
        running = times(jnp.exp(decay_ref[place]), running) + piece_ref[place, :rows, :]


def mixed_kernel(
    heads, query_ref, decay_ref, inside_ref, state_ref, gain_ref, grad_ref, out_ref, sums_ref
):
    size = query_ref.shape[1] // heads
    rows = query_ref.shape[0]
    tall, _, _ = decays(decay_ref[...])
    rising = jnp.exp(tall)
    squares = jnp.zeros((rows, size), f32)
    products = jnp.zeros((rows, size), f32)
    for head in range(heads):
        here = cols(head, size)
        outside = product(query_ref[:, here], state_ref[turned(head, heads)], NN)
        mixed = inside_ref[:, here] + outside * rising[:, head : head + 1]
        out_ref[:, here] = mixed
        squares = squares + mixed * mixed
        products = products + grad_ref[:, here].astype(f32) * gain_ref[:, here] * mixed
    ones = jnp.ones((8, size), f32)
    square = lax.dot_general(ones, squares, NT, precision=highest, preferred_element_type=f32)
    product_ = lax.dot_general(ones, products, NT, precision=highest, preferred_element_type=f32)
    for copy in range(sums_ref.shape[0]):
        sums_ref[copy, 0:1, :] = square[0:1, :]
        sums_ref[copy, 1:2, :] = product_[0:1, :]


def norm_kernel(
    heads, members, full_width, query_ref, decay_ref, mixed_ref, gain_ref, grad_ref, sums_ref, normed_ref, slope_ref, out_ref
):
    size = query_ref.shape[1] // heads
    per = members // heads
    cut = size // per
    tall, _, _ = decays(decay_ref[...])
    rising = jnp.exp(tall)
    ones = jnp.ones((sums_ref.shape[0], size), f32)
    square = lax.dot_general(sums_ref[:, 0, :], ones, TN, precision=highest, preferred_element_type=f32)
    product_ = lax.dot_general(sums_ref[:, 1, :], ones, TN, precision=highest, preferred_element_type=f32)
    scale = lax.rsqrt(square / full_width + epsilon)
    pull = scale * scale * scale * (product_ / full_width)
    for head in range(heads):
        here = cols(head, size)
        mixed = mixed_ref[:, here]
        gain = gain_ref[:, here]
        normed_ref[:, here] = (mixed * scale * gain).astype(bf16)
        slope = scale * (grad_ref[:, here].astype(f32) * gain) - pull * mixed
        slope_ref[:, here] = slope
        state = product(query_ref[:, here], slope * rising[:, head : head + 1], TN)
        first = turned(head, heads) * per
        for part in range(per):
            out_ref[first + part] = state[part * cut : (part + 1) * cut, :]


def near_kernel(
    heads, query_ref, key_ref, value_ref, decay_ref, state_ref, slope_ref, grad_q_ref, near_k_ref, near_v_ref
):
    size = key_ref.shape[1] // heads
    tall, wide, mask = decays(decay_ref[...])
    rising = jnp.exp(tall)
    for head in range(heads):
        here = cols(head, size)
        query, key, value = query_ref[:, here], key_ref[:, here], value_ref[:, here]
        slope = slope_ref[:, here]
        weights = weights_of(tall, wide, mask, head)
        scores = product(query, key, NT) * weights
        grad_scores = product(slope, value, NT) * weights
        there = turned(head, heads)
        outer = product(slope, state_ref[there], NT) * rising[:, head : head + 1]
        grad_q_ref[:, here] = (product(grad_scores, key, NN) + outer).astype(bf16)
        near_k_ref[there] = product(grad_scores, query, TN)
        near_v_ref[:, here] = product(scores, slope, TN)


def far_kernel(heads, key_ref, value_ref, decay_ref, state_ref, near_k_ref, near_v_ref, grad_k_ref, grad_v_ref):
    size = key_ref.shape[1] // heads
    tall, _, _ = decays(decay_ref[...])
    trailing = jnp.exp(tall[-1:, :] - tall)
    for head in range(heads):
        here = cols(head, size)
        late = trailing[:, head : head + 1]
        there = turned(head, heads)
        state = state_ref[there]
        grad_k = near_k_ref[there] + product(value_ref[:, here], state, NT) * late
        grad_v = near_v_ref[:, here] + product(key_ref[:, here], state, NN) * late
        grad_k_ref[:, here] = grad_k.astype(bf16)
        grad_v_ref[:, here] = grad_v.astype(bf16)


def call(kernel, outs, *args, flops=0, copied=(), aliases=None):
    vmem = pl.BlockSpec(memory_space=pltpu.VMEM)
    hbm = pl.BlockSpec(memory_space=pltpu.HBM)
    if copied:
        args = [pltpu.with_memory_space_constraint(a, pltpu.HBM) for a in args]
    moved = sum(a.size * a.dtype.itemsize for a in (*args, *outs))
    return pl.pallas_call(
        kernel,
        out_shape=outs,
        in_specs=[hbm if copied else vmem] * len(args),
        out_specs=[vmem] * len(outs),
        input_output_aliases=aliases or {},
        scratch_shapes=[pltpu.VMEM(a.shape, a.dtype) for a in copied]
        + ([pltpu.SemaphoreType.DMA((len(copied),))] if copied else []),
        cost_estimate=pl.CostEstimate(flops=flops, bytes_accessed=moved, transcendentals=0),
        compiler_params=pltpu.CompilerParams(vmem_limit_bytes=12 * 1024 * 1024),
    )(*args)


def levels(count, heads):
    members = 2 * heads
    groups = count // members
    near = [[group * members + rank(i) for i in range(members)] for group in range(groups)]
    far = [
        [group * members + rank(piece ^ (2 if group >= groups // 2 else 0)) for group in range(groups)]
        for piece in range(members)
    ]
    return groups, members, near, far


def shards(queries, key_rows, value_rows, log_decay, norm_gain, grad_output):
    tok_rows, feat_width = queries.shape
    heads = log_decay.shape[1]
    groups, members, near, far = levels(lax.axis_size("ctx"), heads)
    size = feat_width // heads
    rows = heads * size // members
    wide = jax.ShapeDtypeStruct((tok_rows, feat_width), f32)
    narrow = jax.ShapeDtypeStruct((tok_rows, feat_width), bf16)
    gain = norm_gain.reshape(1, feat_width)
    log_decay = log_decay.T
    bind = functools.partial
    shape = jax.ShapeDtypeStruct
    unit = 2 * heads * tok_rows * size * size

    def exchange(parts, lists):
        return lax.all_to_all(parts, "ctx", 0, 0, axis_index_groups=lists)

    def carried(pieces, marks, backward):
        (total,) = call(
            bind(group_kernel, members, groups, backward, rows),
            [shape((groups, rows + 8, size), f32)],
            pieces,
            marks,
        )
        totals = exchange(total, far)
        (entering,) = call(
            bind(spread_kernel, members, groups, backward, rows),
            [shape((members, rows, size), f32)],
                pieces,
            marks,
            totals,
            )
        return exchange(entering, near).reshape(heads, size, size)

    states, inside = call(
        bind(states_kernel, heads, members),
        [shape((members, rows + 8, size), f32), wide],
        queries,
        key_rows,
        value_rows,
        log_decay,
        flops=5 * unit,
        copied=(queries, key_rows, value_rows, log_decay),
    )
    pieces = exchange(states, near)
    marks = pieces[:, rows:, :]
    entry = carried(pieces, marks, False)
    mixed, sums = call(
        bind(mixed_kernel, heads),
        [wide, shape((lax.axis_size("tp"), 2, tok_rows), f32)],
        queries,
        log_decay,
        inside,
        entry,
        gain,
        grad_output,
        flops=2 * unit,
    )
    gathered = lax.all_to_all(sums, "tp", 0, 0)
    normed, slope, back = call(
        bind(norm_kernel, heads, members, feat_width * lax.axis_size("tp")),
        [narrow, wide, shape((members, rows, size), f32)],
        queries,
        log_decay,
        mixed,
        gain,
        grad_output,
        gathered,
        flops=2 * unit,
    )
    back_pieces = exchange(back, near)
    grad_q, near_k, near_v = call(
        bind(near_kernel, heads),
        [narrow, shape((heads, size, size), f32), wide],
        queries,
        key_rows,
        value_rows,
        log_decay,
        entry,
        slope,
        flops=13 * unit,
        aliases={4: 1, 5: 2},
    )
    leaving = carried(back_pieces, marks, True)
    grad_k, grad_v = call(
        bind(far_kernel, heads),
        [narrow, narrow],
        key_rows,
        value_rows,
        log_decay,
        leaving,
        near_k,
        near_v,
        flops=4 * unit,
    )
    return normed, grad_q, grad_k, grad_v


def solution(mesh):
    both = P("ctx", "tp")
    return jax.shard_map(
        shards,
        mesh=mesh,
        in_specs=(both, both, both, both, P("tp"), both),
        out_specs=(both, both, both, both),
        check_vma=False,
    )
```

```python
import functools

import jax
import jax.numpy as jnp
from jax import lax
from jax.experimental import pallas as pl
from jax.experimental.pallas import tpu as pltpu
from jax.sharding import PartitionSpec as P

epsilon = 1e-06
highest = lax.Precision.HIGHEST
f32 = jnp.float32
bf16 = jnp.bfloat16

NN = (((1,), (0,)), ((), ()))
NT = (((1,), (1,)), ((), ()))
TN = (((0,), (0,)), ((), ()))


def halves(wide):
    high = wide.astype(bf16)
    return high, (wide - high.astype(f32)).astype(bf16)


def product(left, right, dims):
    lefts = halves(left) if left.dtype == f32 else (left,)
    rights = halves(right) if right.dtype == f32 else (right,)
    total = None
    for i, a in enumerate(lefts):
        for j, b in enumerate(rights):
            if i + j < 2:
                term = lax.dot_general(a, b, dims, preferred_element_type=f32)
                total = term if total is None else total + term
    return total


def decays(log_decay):
    rows = log_decay.shape[1]
    above = lax.broadcasted_iota(jnp.int32, (rows, rows), 0)
    along = lax.broadcasted_iota(jnp.int32, (rows, rows), 1)
    upper = (above <= along).astype(f32)
    lower = (above >= along).astype(f32)
    tall = lax.dot_general(lower, log_decay, NT, precision=highest, preferred_element_type=f32)
    wide = lax.dot_general(log_decay, upper, NN, precision=highest, preferred_element_type=f32)
    return tall, wide


def weights_of(tall, wide, head):
    rows = tall.shape[0]
    above = lax.broadcasted_iota(jnp.int32, (rows, rows), 0)
    along = lax.broadcasted_iota(jnp.int32, (rows, rows), 1)
    mask = above >= along
    differences = tall[:, head : head + 1] - wide[head : head + 1, :]
    return jnp.where(mask, jnp.exp(jnp.where(mask, differences, 0.0)), 0.0)


def group_here(heads):
    return lax.div(lax.axis_index("ctx"), 2 * heads)


def rank(place):
    return place % 4 * 4 + place // 4


def turned(head, heads):
    half = lax.axis_size("ctx") // (2 * heads) // 2
    return head ^ jnp.where(group_here(heads) < half, 0, 1)


def cols(head, size):
    return slice(head * size, (head + 1) * size)


def states_kernel(
    heads, members, key_far, value_far, decay_far, out_ref, tall_ref, wide_ref, key_ref, value_ref, decay_ref, sems
):
    size = key_ref.shape[1] // heads
    per = members // heads
    rows = size // per
    copies = [
        pltpu.make_async_copy(source, target, sems.at[i])
        for i, (source, target) in enumerate(
            ((decay_far, decay_ref), (key_far, key_ref), (value_far, value_ref))
        )
    ]
    for copy in copies:
        copy.start()
    copies[0].wait()
    tall, wide = decays(decay_ref[...])
    tall_ref[...] = tall
    wide_ref[...] = wide
    total = tall[-1:, :]
    trailing = jnp.exp(total - tall)
    copies[1].wait()
    copies[2].wait()
    for head in range(heads):
        here = cols(head, size)
        key, value = key_ref[:, here], value_ref[:, here]
        state = product(key.astype(f32) * trailing[:, head : head + 1], value, TN)
        mark = jnp.broadcast_to(total[:, head : head + 1], (8, size))
        first = turned(head, heads) * per
        for part in range(per):
            out_ref[first + part, :rows, :] = state[part * rows : (part + 1) * rows, :]
            out_ref[first + part, rows:, :] = mark


def times(gain, state):
    return (gain[None] * state.reshape(-1, 8, state.shape[-1])).reshape(state.shape)


def group_kernel(members, copies, rows, piece_ref, out_ref):
    total = jnp.zeros((rows, piece_ref.shape[-1]), f32)
    whole = jnp.zeros((8, piece_ref.shape[-1]), f32)
    for member in range(members):
        place = rank(member)
        mark = piece_ref[place, rows:, :]
        total = times(jnp.exp(mark), total) + piece_ref[place, :rows, :]
        whole = whole + mark
    for copy in range(copies):
        out_ref[copy, :rows, :] = total
        out_ref[copy, rows:, :] = whole


def spread_kernel(members, groups, rows, piece_ref, total_ref, out_ref, near_ref, far_ref):
    mine = group_here(members // 2)
    running = jnp.zeros((rows, piece_ref.shape[-1]), f32)
    for group in range(groups):
        gain = jnp.exp(total_ref[group, rows:, :])
        far_ref[group] = gain
        longer = times(gain, running) + total_ref[group, :rows, :]
        running = jnp.where(group < mine, longer, running)
    for member in range(members):
        place = rank(member)
        gain = jnp.exp(piece_ref[place, rows:, :])
        near_ref[place] = gain
        out_ref[place] = running
        running = times(gain, running) + piece_ref[place, :rows, :]


def back_group_kernel(members, copies, piece_ref, near_ref, out_ref):
    total = jnp.zeros(piece_ref.shape[1:], f32)
    for member in reversed(range(members)):
        place = rank(member)
        total = times(near_ref[place], total) + piece_ref[place]
    for copy in range(copies):
        out_ref[copy] = total


def back_spread_kernel(members, groups, piece_ref, near_ref, total_ref, far_ref, out_ref):
    mine = group_here(members // 2)
    running = jnp.zeros(piece_ref.shape[1:], f32)
    for group in reversed(range(groups)):
        longer = times(far_ref[group], running) + total_ref[group]
        running = jnp.where(group > mine, longer, running)
    for member in reversed(range(members)):
        place = rank(member)
        out_ref[place] = running
        running = times(near_ref[place], running) + piece_ref[place]


def inside_kernel(heads, query_ref, key_ref, value_ref, tall_ref, wide_ref, out_ref):
    size = key_ref.shape[1] // heads
    tall, wide = tall_ref[...], wide_ref[...]
    for head in range(heads):
        here = cols(head, size)
        scores = product(query_ref[:, here], key_ref[:, here], NT) * weights_of(tall, wide, head)
        out_ref[:, here] = product(scores, value_ref[:, here], NN)


def mixed_kernel(
    heads, query_ref, tall_ref, inside_ref, state_ref, gain_ref, grad_ref, out_ref, sums_ref
):
    size = query_ref.shape[1] // heads
    rows = query_ref.shape[0]
    rising = jnp.exp(tall_ref[...])
    squares = jnp.zeros((rows, size), f32)
    products = jnp.zeros((rows, size), f32)
    for head in range(heads):
        here = cols(head, size)
        outside = product(query_ref[:, here], state_ref[turned(head, heads)], NN)
        mixed = inside_ref[:, here] + outside * rising[:, head : head + 1]
        out_ref[:, here] = mixed
        squares = squares + mixed * mixed
        products = products + grad_ref[:, here].astype(f32) * gain_ref[:, here] * mixed
    ones = jnp.ones((8, size), f32)
    square = lax.dot_general(ones, squares, NT, precision=highest, preferred_element_type=f32)
    product_ = lax.dot_general(ones, products, NT, precision=highest, preferred_element_type=f32)
    for copy in range(sums_ref.shape[0]):
        sums_ref[copy, 0:1, :] = square[0:1, :]
        sums_ref[copy, 1:2, :] = product_[0:1, :]


def row_factors(full_width, size, sums_ref):
    ones = jnp.ones((sums_ref.shape[0], size), f32)
    square = lax.dot_general(sums_ref[:, 0, :], ones, TN, precision=highest, preferred_element_type=f32)
    product_ = lax.dot_general(sums_ref[:, 1, :], ones, TN, precision=highest, preferred_element_type=f32)
    scale = lax.rsqrt(square / full_width + epsilon)
    return scale, scale * scale * scale * (product_ / full_width)


def back_kernel(
    heads, members, full_width, query_ref, tall_ref, mixed_ref, gain_ref, grad_ref, sums_ref, out_ref
):
    size = query_ref.shape[1] // heads
    per = members // heads
    cut = size // per
    rising = jnp.exp(tall_ref[...])
    scale, pull = row_factors(full_width, size, sums_ref)
    for head in range(heads):
        here = cols(head, size)
        slope = scale * (grad_ref[:, here].astype(f32) * gain_ref[:, here]) - pull * mixed_ref[:, here]
        state = product(query_ref[:, here], slope * rising[:, head : head + 1], TN)
        first = turned(head, heads) * per
        for part in range(per):
            out_ref[first + part] = state[part * cut : (part + 1) * cut, :]


def near_kernel(
    heads,
    full_width,
    query_ref,
    key_ref,
    value_ref,
    tall_ref,
    wide_ref,
    state_ref,
    mixed_ref,
    gain_ref,
    grad_ref,
    sums_ref,
    normed_ref,
    grad_q_ref,
    near_k_ref,
    near_v_ref,
):
    size = key_ref.shape[1] // heads
    tall, wide = tall_ref[...], wide_ref[...]
    rising = jnp.exp(tall)
    scale, pull = row_factors(full_width, size, sums_ref)
    for head in range(heads):
        here = cols(head, size)
        query, key, value = query_ref[:, here], key_ref[:, here], value_ref[:, here]
        gain, mixed = gain_ref[:, here], mixed_ref[:, here]
        normed_ref[:, here] = (mixed * scale * gain).astype(bf16)
        slope = scale * (grad_ref[:, here].astype(f32) * gain) - pull * mixed
        weights = weights_of(tall, wide, head)
        scores = product(query, key, NT) * weights
        grad_scores = product(slope, value, NT) * weights
        there = turned(head, heads)
        outer = product(slope, state_ref[there], NT) * rising[:, head : head + 1]
        grad_q_ref[:, here] = (product(grad_scores, key, NN) + outer).astype(bf16)
        near_k_ref[there] = product(grad_scores, query, TN)
        near_v_ref[:, here] = product(scores, slope, TN)


def far_kernel(heads, key_ref, value_ref, tall_ref, state_ref, near_k_ref, near_v_ref, grad_k_ref, grad_v_ref):
    size = key_ref.shape[1] // heads
    tall = tall_ref[...]
    trailing = jnp.exp(tall[-1:, :] - tall)
    for head in range(heads):
        here = cols(head, size)
        late = trailing[:, head : head + 1]
        there = turned(head, heads)
        state = state_ref[there]
        grad_k = near_k_ref[there] + product(value_ref[:, here], state, NT) * late
        grad_v = near_v_ref[:, here] + product(key_ref[:, here], state, NN) * late
        grad_k_ref[:, here] = grad_k.astype(bf16)
        grad_v_ref[:, here] = grad_v.astype(bf16)


def call(kernel, outs, *args, flops=0, copied=(), aliases=None):
    vmem = pl.BlockSpec(memory_space=pltpu.VMEM)
    hbm = pl.BlockSpec(memory_space=pltpu.HBM)
    if copied:
        args = [pltpu.with_memory_space_constraint(a, pltpu.HBM) for a in args]
    moved = sum(a.size * a.dtype.itemsize for a in (*args, *outs))
    return pl.pallas_call(
        kernel,
        out_shape=outs,
        in_specs=[hbm if copied else vmem] * len(args),
        out_specs=[vmem] * len(outs),
        input_output_aliases=aliases or {},
        scratch_shapes=[pltpu.VMEM(a.shape, a.dtype) for a in copied]
        + ([pltpu.SemaphoreType.DMA((len(copied),))] if copied else []),
        cost_estimate=pl.CostEstimate(flops=flops, bytes_accessed=moved, transcendentals=0),
        compiler_params=pltpu.CompilerParams(vmem_limit_bytes=12 * 1024 * 1024),
    )(*args)


def levels(count, heads):
    members = 2 * heads
    groups = count // members
    near = [[group * members + rank(i) for i in range(members)] for group in range(groups)]
    far = [
        [group * members + rank(piece ^ (2 if group >= groups // 2 else 0)) for group in range(groups)]
        for piece in range(members)
    ]
    return groups, members, near, far


def shards(queries, key_rows, value_rows, log_decay, norm_gain, grad_output):
    tok_rows, feat_width = queries.shape
    heads = log_decay.shape[1]
    groups, members, near, far = levels(lax.axis_size("ctx"), heads)
    size = feat_width // heads
    rows = heads * size // members
    wide = jax.ShapeDtypeStruct((tok_rows, feat_width), f32)
    narrow = jax.ShapeDtypeStruct((tok_rows, feat_width), bf16)
    gain = norm_gain.reshape(1, feat_width)
    log_decay = log_decay.T
    bind = functools.partial
    shape = jax.ShapeDtypeStruct
    unit = 2 * heads * tok_rows * size * size

    def exchange(parts, lists):
        return lax.all_to_all(parts, "ctx", 0, 0, axis_index_groups=lists)

    states, tall, across = call(
        bind(states_kernel, heads, members),
        [shape((members, rows + 8, size), f32), shape((tok_rows, heads), f32), shape((heads, tok_rows), f32)],
        key_rows,
        value_rows,
        log_decay,
        flops=2 * unit,
        copied=(key_rows, value_rows, log_decay),
    )
    pieces = exchange(states, near)
    (total,) = call(
        bind(group_kernel, members, groups, rows), [shape((groups, rows + 8, size), f32)], pieces
    )
    (inside,) = call(
        bind(inside_kernel, heads), [wide], queries, key_rows, value_rows, tall, across, flops=3 * unit
    )
    entering, near_gains, far_gains = call(
        bind(spread_kernel, members, groups, rows),
        [shape((members, rows, size), f32), shape((members, 8, size), f32), shape((groups, 8, size), f32)],
        pieces,
        exchange(total, far),
    )
    entry = exchange(entering, near).reshape(heads, size, size)
    mixed, sums = call(
        bind(mixed_kernel, heads),
        [wide, shape((lax.axis_size("tp"), 2, tok_rows), f32)],
        queries,
        tall,
        inside,
        entry,
        gain,
        grad_output,
        flops=2 * unit,
    )
    gathered = lax.all_to_all(sums, "tp", 0, 0)
    full_width = feat_width * lax.axis_size("tp")
    (back,) = call(
        bind(back_kernel, heads, members, full_width),
        [shape((members, rows, size), f32)],
        queries,
        tall,
        mixed,
        gain,
        grad_output,
        gathered,
        flops=2 * unit,
    )
    back_pieces = exchange(back, near)
    (back_total,) = call(
        bind(back_group_kernel, members, groups),
        [shape((groups, rows, size), f32)],
        back_pieces,
        near_gains,
    )
    (returning,) = call(
        bind(back_spread_kernel, members, groups),
        [shape((members, rows, size), f32)],
        back_pieces,
        near_gains,
        exchange(back_total, far),
        far_gains,
    )
    leaving = exchange(returning, near).reshape(heads, size, size)
    normed, grad_q, near_k, near_v = call(
        bind(near_kernel, heads, full_width),
        [narrow, narrow, shape((heads, size, size), f32), wide],
        queries,
        key_rows,
        value_rows,
        tall,
        across,
        entry,
        mixed,
        gain,
        grad_output,
        gathered,
        flops=13 * unit,
        aliases={5: 2, 6: 3},
    )
    grad_k, grad_v = call(
        bind(far_kernel, heads),
        [narrow, narrow],
        key_rows,
        value_rows,
        tall,
        leaving,
        near_k,
        near_v,
        flops=4 * unit,
    )
    return normed, grad_q, grad_k, grad_v


def solution(mesh):
    both = P("ctx", "tp")
    return jax.shard_map(
        shards,
        mesh=mesh,
        in_specs=(both, both, both, both, P("tp"), both),
        out_specs=(both, both, both, both),
        check_vma=False,
    )
```

```python
import functools

import jax
import jax.numpy as jnp
from jax import lax
from jax.experimental import pallas as pl
from jax.experimental.pallas import tpu as pltpu
from jax.sharding import PartitionSpec as P

epsilon = 1e-06
highest = lax.Precision.HIGHEST
f32 = jnp.float32
bf16 = jnp.bfloat16

NN = (((1,), (0,)), ((), ()))
NT = (((1,), (1,)), ((), ()))
TN = (((0,), (0,)), ((), ()))


def halves(wide):
    high = wide.astype(bf16)
    return high, (wide - high.astype(f32)).astype(bf16)


def product(left, right, dims):
    lefts = halves(left) if left.dtype == f32 else (left,)
    rights = halves(right) if right.dtype == f32 else (right,)
    total = None
    for i, a in enumerate(lefts):
        for j, b in enumerate(rights):
            if i + j < 2:
                term = lax.dot_general(a, b, dims, preferred_element_type=f32)
                total = term if total is None else total + term
    return total


def decays(log_decay):
    rows = log_decay.shape[1]
    above = lax.broadcasted_iota(jnp.int32, (rows, rows), 0)
    along = lax.broadcasted_iota(jnp.int32, (rows, rows), 1)
    upper = (above <= along).astype(f32)
    lower = (above >= along).astype(f32)
    tall = lax.dot_general(lower, log_decay, NT, precision=highest, preferred_element_type=f32)
    wide = lax.dot_general(log_decay, upper, NN, precision=highest, preferred_element_type=f32)
    return tall, wide


def weights_of(tall, wide, head):
    rows = tall.shape[0]
    above = lax.broadcasted_iota(jnp.int32, (rows, rows), 0)
    along = lax.broadcasted_iota(jnp.int32, (rows, rows), 1)
    mask = above >= along
    differences = tall[:, head : head + 1] - wide[head : head + 1, :]
    return jnp.where(mask, jnp.exp(jnp.where(mask, differences, 0.0)), 0.0)


def whereabouts(heads):
    span = 2 * heads // 4
    z_rows = lax.axis_size("ctx") // 4
    shift = (lax.axis_index("tp") & 1) * (span // 2)
    group = lax.div((lax.div(lax.axis_index("ctx"), 4) - shift) & (z_rows - 1), span)
    cut = jnp.logical_and(shift > 0, group == z_rows // span - 1)
    return group, shift, cut


def turned(head, heads):
    half = lax.axis_size("ctx") // (2 * heads) // 2
    return head ^ jnp.where(whereabouts(heads)[0] < half, 0, 1)


def rank(member, cut):
    return member % 4 * 4 + ((member // 4) ^ jnp.where(cut, 2, 0))


def cols(head, size):
    return slice(head * size, (head + 1) * size)


def states_kernel(
    heads, members, key_far, value_far, decay_far, out_ref, tall_ref, wide_ref, key_ref, value_ref, decay_ref, sems
):
    size = key_ref.shape[1] // heads
    per = members // heads
    rows = size // per
    copies = [
        pltpu.make_async_copy(source, target, sems.at[i])
        for i, (source, target) in enumerate(
            ((decay_far, decay_ref), (key_far, key_ref), (value_far, value_ref))
        )
    ]
    for copy in copies:
        copy.start()
    copies[0].wait()
    tall, wide = decays(decay_ref[...])
    tall_ref[...] = tall
    wide_ref[...] = wide
    total = tall[-1:, :]
    trailing = jnp.exp(total - tall)
    copies[1].wait()
    copies[2].wait()
    for head in range(heads):
        here = cols(head, size)
        key, value = key_ref[:, here], value_ref[:, here]
        state = product(key.astype(f32) * trailing[:, head : head + 1], value, TN)
        mark = jnp.broadcast_to(total[:, head : head + 1], (8, size))
        first = turned(head, heads) * per
        for part in range(per):
            out_ref[first + part, :rows, :] = state[part * rows : (part + 1) * rows, :]
            out_ref[first + part, rows:, :] = mark


def times(gain, state):
    return (gain[None] * state.reshape(-1, 8, state.shape[-1])).reshape(state.shape)


def group_kernel(members, copies, rows, piece_ref, out_ref):
    _, _, cut = whereabouts(members // 2)
    total = jnp.zeros((rows, piece_ref.shape[-1]), f32)
    whole = jnp.zeros((8, piece_ref.shape[-1]), f32)
    early = total
    for member in range(members):
        if member == members // 2:
            early = total
        place = rank(member, cut)
        mark = piece_ref[place, rows:, :]
        total = times(jnp.exp(mark), total) + piece_ref[place, :rows, :]
        whole = whole + mark
    total = jnp.where(cut, early, total)
    for copy in range(copies):
        out_ref[copy, :rows, :] = total
        out_ref[copy, rows:, :] = whole


def spread_kernel(members, groups, rows, piece_ref, total_ref, out_ref, near_ref, far_ref):
    mine, shift, cut = whereabouts(members // 2)
    first = jnp.where(shift > 0, groups - 1, 0)
    before = jnp.where(cut, 0, mine + jnp.where(shift > 0, 1, 0))
    every = jnp.zeros((rows, piece_ref.shape[-1]), f32)
    running = every
    for step in range(groups):
        group = (step + first) & (groups - 1)
        gain = jnp.exp(total_ref[group, rows:, :])
        far_ref[group] = gain
        every = times(gain, every) + total_ref[group, :rows, :]
        running = jnp.where(step < before, every, running)
    for member in range(members):
        if member == members // 2:
            running = jnp.where(cut, every, running)
        place = rank(member, cut)
        gain = jnp.exp(piece_ref[place, rows:, :])
        near_ref[place] = gain
        out_ref[place] = running
        running = times(gain, running) + piece_ref[place, :rows, :]


def back_group_kernel(members, copies, piece_ref, near_ref, out_ref):
    _, _, cut = whereabouts(members // 2)
    total = jnp.zeros(piece_ref.shape[1:], f32)
    late = total
    for member in reversed(range(members)):
        place = rank(member, cut)
        total = times(near_ref[place], total) + piece_ref[place]
        if member == members // 2:
            late = total
    total = jnp.where(cut, late, total)
    for copy in range(copies):
        out_ref[copy] = total


def back_spread_kernel(members, groups, piece_ref, near_ref, total_ref, far_ref, out_ref):
    mine, _, cut = whereabouts(members // 2)
    every = jnp.zeros(piece_ref.shape[1:], f32)
    running = every
    for group in reversed(range(groups)):
        every = times(far_ref[group], every) + total_ref[group]
        running = jnp.where(group > mine, every, running)
    for member in reversed(range(members)):
        place = rank(member, cut)
        out_ref[place] = running
        running = times(near_ref[place], running) + piece_ref[place]
        if member == members // 2:
            running = jnp.where(cut, every, running)


def inside_kernel(heads, query_ref, key_ref, value_ref, tall_ref, wide_ref, out_ref):
    size = key_ref.shape[1] // heads
    tall, wide = tall_ref[...], wide_ref[...]
    for head in range(heads):
        here = cols(head, size)
        scores = product(query_ref[:, here], key_ref[:, here], NT) * weights_of(tall, wide, head)
        out_ref[:, here] = product(scores, value_ref[:, here], NN)


def mixed_kernel(
    heads, query_ref, tall_ref, inside_ref, state_ref, gain_ref, grad_ref, out_ref, sums_ref
):
    size = query_ref.shape[1] // heads
    rows = query_ref.shape[0]
    rising = jnp.exp(tall_ref[...])
    squares = jnp.zeros((rows, size), f32)
    products = jnp.zeros((rows, size), f32)
    for head in range(heads):
        here = cols(head, size)
        outside = product(query_ref[:, here], state_ref[turned(head, heads)], NN)
        mixed = inside_ref[:, here] + outside * rising[:, head : head + 1]
        out_ref[:, here] = mixed
        squares = squares + mixed * mixed
        products = products + grad_ref[:, here].astype(f32) * gain_ref[:, here] * mixed
    ones = jnp.ones((8, size), f32)
    square = lax.dot_general(ones, squares, NT, precision=highest, preferred_element_type=f32)
    product_ = lax.dot_general(ones, products, NT, precision=highest, preferred_element_type=f32)
    for copy in range(sums_ref.shape[0]):
        sums_ref[copy, 0:1, :] = square[0:1, :]
        sums_ref[copy, 1:2, :] = product_[0:1, :]


def row_factors(full_width, size, sums_ref):
    ones = jnp.ones((sums_ref.shape[0], size), f32)
    square = lax.dot_general(sums_ref[:, 0, :], ones, TN, precision=highest, preferred_element_type=f32)
    product_ = lax.dot_general(sums_ref[:, 1, :], ones, TN, precision=highest, preferred_element_type=f32)
    scale = lax.rsqrt(square / full_width + epsilon)
    return scale, scale * scale * scale * (product_ / full_width)


def back_kernel(
    heads, members, full_width, query_ref, tall_ref, mixed_ref, gain_ref, grad_ref, sums_ref, out_ref
):
    size = query_ref.shape[1] // heads
    per = members // heads
    cut = size // per
    rising = jnp.exp(tall_ref[...])
    scale, pull = row_factors(full_width, size, sums_ref)
    for head in range(heads):
        here = cols(head, size)
        slope = scale * (grad_ref[:, here].astype(f32) * gain_ref[:, here]) - pull * mixed_ref[:, here]
        state = product(query_ref[:, here], slope * rising[:, head : head + 1], TN)
        first = turned(head, heads) * per
        for part in range(per):
            out_ref[first + part] = state[part * cut : (part + 1) * cut, :]


def near_kernel(
    heads,
    full_width,
    query_ref,
    key_ref,
    value_ref,
    tall_ref,
    wide_ref,
    state_ref,
    mixed_ref,
    gain_ref,
    grad_ref,
    sums_ref,
    normed_ref,
    grad_q_ref,
    near_k_ref,
    near_v_ref,
):
    size = key_ref.shape[1] // heads
    tall, wide = tall_ref[...], wide_ref[...]
    rising = jnp.exp(tall)
    scale, pull = row_factors(full_width, size, sums_ref)
    for head in range(heads):
        here = cols(head, size)
        query, key, value = query_ref[:, here], key_ref[:, here], value_ref[:, here]
        gain, mixed = gain_ref[:, here], mixed_ref[:, here]
        normed_ref[:, here] = (mixed * scale * gain).astype(bf16)
        slope = scale * (grad_ref[:, here].astype(f32) * gain) - pull * mixed
        weights = weights_of(tall, wide, head)
        scores = product(query, key, NT) * weights
        grad_scores = product(slope, value, NT) * weights
        there = turned(head, heads)
        outer = product(slope, state_ref[there], NT) * rising[:, head : head + 1]
        grad_q_ref[:, here] = (product(grad_scores, key, NN) + outer).astype(bf16)
        near_k_ref[there] = product(grad_scores, query, TN)
        near_v_ref[:, here] = product(scores, slope, TN)


def far_kernel(heads, key_ref, value_ref, tall_ref, state_ref, near_k_ref, near_v_ref, grad_k_ref, grad_v_ref):
    size = key_ref.shape[1] // heads
    tall = tall_ref[...]
    trailing = jnp.exp(tall[-1:, :] - tall)
    for head in range(heads):
        here = cols(head, size)
        late = trailing[:, head : head + 1]
        there = turned(head, heads)
        state = state_ref[there]
        grad_k = near_k_ref[there] + product(value_ref[:, here], state, NT) * late
        grad_v = near_v_ref[:, here] + product(key_ref[:, here], state, NN) * late
        grad_k_ref[:, here] = grad_k.astype(bf16)
        grad_v_ref[:, here] = grad_v.astype(bf16)


def call(kernel, outs, *args, flops=0, copied=(), aliases=None):
    vmem = pl.BlockSpec(memory_space=pltpu.VMEM)
    hbm = pl.BlockSpec(memory_space=pltpu.HBM)
    if copied:
        args = [pltpu.with_memory_space_constraint(a, pltpu.HBM) for a in args]
    moved = sum(a.size * a.dtype.itemsize for a in (*args, *outs))
    return pl.pallas_call(
        kernel,
        out_shape=outs,
        in_specs=[hbm if copied else vmem] * len(args),
        out_specs=[vmem] * len(outs),
        input_output_aliases=aliases or {},
        scratch_shapes=[pltpu.VMEM(a.shape, a.dtype) for a in copied]
        + ([pltpu.SemaphoreType.DMA((len(copied),))] if copied else []),
        cost_estimate=pl.CostEstimate(flops=flops, bytes_accessed=moved, transcendentals=0),
        compiler_params=pltpu.CompilerParams(vmem_limit_bytes=12 * 1024 * 1024),
    )(*args)


def levels(count, tp, heads):
    members = 2 * heads
    span = members // 4
    groups = count // members
    near, far = [], []
    for index in range(tp):
        shift = index % 2 * (span // 2)

        def device(group, place):
            z = (group * span + shift + place % 4) % (count // 4)
            return (z * 4 + place // 4) * tp + index

        for group in range(groups):
            near.append([device(group, place) for place in range(members)])
        for piece in range(members):
            far.append(
                [device(group, piece ^ (2 if group >= groups // 2 else 0)) for group in range(groups)]
            )
    return groups, members, near, far


def shards(queries, key_rows, value_rows, log_decay, norm_gain, grad_output):
    tok_rows, feat_width = queries.shape
    heads = log_decay.shape[1]
    groups, members, near, far = levels(lax.axis_size("ctx"), lax.axis_size("tp"), heads)
    size = feat_width // heads
    rows = heads * size // members
    wide = jax.ShapeDtypeStruct((tok_rows, feat_width), f32)
    narrow = jax.ShapeDtypeStruct((tok_rows, feat_width), bf16)
    gain = norm_gain.reshape(1, feat_width)
    log_decay = log_decay.T
    bind = functools.partial
    shape = jax.ShapeDtypeStruct
    unit = 2 * heads * tok_rows * size * size

    def exchange(parts, lists):
        return lax.all_to_all(parts, ("ctx", "tp"), 0, 0, axis_index_groups=lists)

    states, tall, across = call(
        bind(states_kernel, heads, members),
        [shape((members, rows + 8, size), f32), shape((tok_rows, heads), f32), shape((heads, tok_rows), f32)],
        key_rows,
        value_rows,
        log_decay,
        flops=2 * unit,
        copied=(key_rows, value_rows, log_decay),
    )
    pieces = exchange(states, near)
    (total,) = call(
        bind(group_kernel, members, groups, rows), [shape((groups, rows + 8, size), f32)], pieces
    )
    (inside,) = call(
        bind(inside_kernel, heads), [wide], queries, key_rows, value_rows, tall, across, flops=3 * unit
    )
    entering, near_gains, far_gains = call(
        bind(spread_kernel, members, groups, rows),
        [shape((members, rows, size), f32), shape((members, 8, size), f32), shape((groups, 8, size), f32)],
        pieces,
        exchange(total, far),
    )
    entry = exchange(entering, near).reshape(heads, size, size)
    mixed, sums = call(
        bind(mixed_kernel, heads),
        [wide, shape((lax.axis_size("tp"), 2, tok_rows), f32)],
        queries,
        tall,
        inside,
        entry,
        gain,
        grad_output,
        flops=2 * unit,
    )
    gathered = lax.all_to_all(sums, "tp", 0, 0)
    full_width = feat_width * lax.axis_size("tp")
    (back,) = call(
        bind(back_kernel, heads, members, full_width),
        [shape((members, rows, size), f32)],
        queries,
        tall,
        mixed,
        gain,
        grad_output,
        gathered,
        flops=2 * unit,
    )
    back_pieces = exchange(back, near)
    (back_total,) = call(
        bind(back_group_kernel, members, groups),
        [shape((groups, rows, size), f32)],
        back_pieces,
        near_gains,
    )
    (returning,) = call(
        bind(back_spread_kernel, members, groups),
        [shape((members, rows, size), f32)],
        back_pieces,
        near_gains,
        exchange(back_total, far),
        far_gains,
    )
    leaving = exchange(returning, near).reshape(heads, size, size)
    normed, grad_q, near_k, near_v = call(
        bind(near_kernel, heads, full_width),
        [narrow, narrow, shape((heads, size, size), f32), wide],
        queries,
        key_rows,
        value_rows,
        tall,
        across,
        entry,
        mixed,
        gain,
        grad_output,
        gathered,
        flops=13 * unit,
        aliases={5: 2, 6: 3},
    )
    grad_k, grad_v = call(
        bind(far_kernel, heads),
        [narrow, narrow],
        key_rows,
        value_rows,
        tall,
        leaving,
        near_k,
        near_v,
        flops=4 * unit,
    )
    return normed, grad_q, grad_k, grad_v


def solution(mesh):
    both = P("ctx", "tp")
    return jax.shard_map(
        shards,
        mesh=mesh,
        in_specs=(both, both, both, both, P("tp"), both),
        out_specs=(both, both, both, both),
        check_vma=False,
    )
```

```python
import functools

import jax
import jax.numpy as jnp
from jax import lax
from jax.experimental import pallas as pl
from jax.experimental.pallas import tpu as pltpu
from jax.sharding import PartitionSpec as P

epsilon = 1e-06
highest = lax.Precision.HIGHEST
f32 = jnp.float32
bf16 = jnp.bfloat16

NN = (((1,), (0,)), ((), ()))
NT = (((1,), (1,)), ((), ()))
TN = (((0,), (0,)), ((), ()))


def halves(wide):
    high = wide.astype(bf16)
    return high, (wide - high.astype(f32)).astype(bf16)


def product(left, right, dims):
    lefts = halves(left) if left.dtype == f32 else (left,)
    rights = halves(right) if right.dtype == f32 else (right,)
    total = None
    for i, a in enumerate(lefts):
        for j, b in enumerate(rights):
            if i + j < 2:
                term = lax.dot_general(a, b, dims, preferred_element_type=f32)
                total = term if total is None else total + term
    return total


def decays(log_decay):
    rows = log_decay.shape[1]
    above = lax.broadcasted_iota(jnp.int32, (rows, rows), 0)
    along = lax.broadcasted_iota(jnp.int32, (rows, rows), 1)
    upper = (above <= along).astype(f32)
    lower = (above >= along).astype(f32)
    tall = lax.dot_general(lower, log_decay, NT, precision=highest, preferred_element_type=f32)
    wide = lax.dot_general(log_decay, upper, NN, precision=highest, preferred_element_type=f32)
    return tall, wide


def weights_of(tall, wide, head):
    rows = tall.shape[0]
    above = lax.broadcasted_iota(jnp.int32, (rows, rows), 0)
    along = lax.broadcasted_iota(jnp.int32, (rows, rows), 1)
    mask = above >= along
    differences = tall[:, head : head + 1] - wide[head : head + 1, :]
    return jnp.where(mask, jnp.exp(jnp.where(mask, differences, 0.0)), 0.0)


def whereabouts(heads):
    span = 2 * heads // 4
    z_rows = lax.axis_size("ctx") // 4
    shift = (lax.axis_index("tp") & 1) * (span // 2)
    group = lax.div((lax.div(lax.axis_index("ctx"), 4) - shift) & (z_rows - 1), span)
    cut = jnp.logical_and(shift > 0, group == z_rows // span - 1)
    return group, shift, cut


def turned(head, heads):
    half = lax.axis_size("ctx") // (2 * heads) // 2
    return head ^ jnp.where(whereabouts(heads)[0] < half, 0, 1)


def rank(member, cut):
    return member % 4 * 4 + ((member // 4) ^ jnp.where(cut, 2, 0))


def cols(head, size):
    return slice(head * size, (head + 1) * size)


def parted(heads, size):
    return [slice(2 * pair * size, 2 * (pair + 1) * size) for pair in range(heads // 2)]


def states_kernel(
    heads, members, key_far, value_far, decay_far, out_ref, tall_ref, wide_ref, key_ref, value_ref, decay_ref, sems
):
    size = key_ref.shape[1] // heads
    per = members // heads
    rows = size // per
    first = pltpu.make_async_copy(decay_far, decay_ref, sems.at[heads])
    first.start()
    copies = []
    for pair, part in enumerate(parted(heads, size)):
        copies.append(
            (
                pltpu.make_async_copy(key_far.at[:, part], key_ref.at[:, part], sems.at[2 * pair]),
                pltpu.make_async_copy(value_far.at[:, part], value_ref.at[:, part], sems.at[2 * pair + 1]),
            )
        )
        for copy in copies[-1]:
            copy.start()
    first.wait()
    tall, wide = decays(decay_ref[...])
    tall_ref[...] = tall
    wide_ref[...] = wide
    total = tall[-1:, :]
    trailing = jnp.exp(total - tall)
    for head in range(heads):
        if head % 2 == 0:
            for copy in copies[head // 2]:
                copy.wait()
        here = cols(head, size)
        key, value = key_ref[:, here], value_ref[:, here]
        state = product(key.astype(f32) * trailing[:, head : head + 1], value, TN)
        mark = jnp.broadcast_to(total[:, head : head + 1], (8, size))
        place = turned(head, heads) * per
        for part in range(per):
            out_ref[place + part, :rows, :] = state[part * rows : (part + 1) * rows, :]
            out_ref[place + part, rows:, :] = mark


def times(gain, state):
    return (gain[None] * state.reshape(-1, 8, state.shape[-1])).reshape(state.shape)


def group_kernel(members, copies, rows, piece_ref, out_ref):
    _, _, cut = whereabouts(members // 2)
    total = jnp.zeros((rows, piece_ref.shape[-1]), f32)
    whole = jnp.zeros((8, piece_ref.shape[-1]), f32)
    early = total
    for member in range(members):
        if member == members // 2:
            early = total
        place = rank(member, cut)
        mark = piece_ref[place, rows:, :]
        total = times(jnp.exp(mark), total) + piece_ref[place, :rows, :]
        whole = whole + mark
    total = jnp.where(cut, early, total)
    for copy in range(copies):
        out_ref[copy, :rows, :] = total
        out_ref[copy, rows:, :] = whole


def spread_kernel(members, groups, rows, piece_ref, total_ref, out_ref, near_ref, far_ref):
    mine, shift, cut = whereabouts(members // 2)
    first = jnp.where(shift > 0, groups - 1, 0)
    before = jnp.where(cut, 0, mine + jnp.where(shift > 0, 1, 0))
    every = jnp.zeros((rows, piece_ref.shape[-1]), f32)
    running = every
    for step in range(groups):
        group = (step + first) & (groups - 1)
        gain = jnp.exp(total_ref[group, rows:, :])
        far_ref[group] = gain
        every = times(gain, every) + total_ref[group, :rows, :]
        running = jnp.where(step < before, every, running)
    for member in range(members):
        if member == members // 2:
            running = jnp.where(cut, every, running)
        place = rank(member, cut)
        gain = jnp.exp(piece_ref[place, rows:, :])
        near_ref[place] = gain
        out_ref[place] = running
        running = times(gain, running) + piece_ref[place, :rows, :]


def back_group_kernel(members, copies, piece_ref, near_ref, out_ref):
    _, _, cut = whereabouts(members // 2)
    total = jnp.zeros(piece_ref.shape[1:], f32)
    late = total
    for member in reversed(range(members)):
        place = rank(member, cut)
        total = times(near_ref[place], total) + piece_ref[place]
        if member == members // 2:
            late = total
    total = jnp.where(cut, late, total)
    for copy in range(copies):
        out_ref[copy] = total


def back_spread_kernel(members, groups, piece_ref, near_ref, total_ref, far_ref, out_ref):
    mine, _, cut = whereabouts(members // 2)
    every = jnp.zeros(piece_ref.shape[1:], f32)
    running = every
    for group in reversed(range(groups)):
        every = times(far_ref[group], every) + total_ref[group]
        running = jnp.where(group > mine, every, running)
    for member in reversed(range(members)):
        place = rank(member, cut)
        out_ref[place] = running
        running = times(near_ref[place], running) + piece_ref[place]
        if member == members // 2:
            running = jnp.where(cut, every, running)


def mixed_kernel(
    heads, query_ref, key_ref, value_ref, tall_ref, wide_ref, state_ref, gain_ref, grad_ref, out_ref, sums_ref
):
    size = query_ref.shape[1] // heads
    rows = query_ref.shape[0]
    tall, wide = tall_ref[...], wide_ref[...]
    rising = jnp.exp(tall)
    squares = jnp.zeros((rows, size), f32)
    products = jnp.zeros((rows, size), f32)
    for head in range(heads):
        here = cols(head, size)
        query = query_ref[:, here]
        scores = product(query, key_ref[:, here], NT) * weights_of(tall, wide, head)
        outside = product(query, state_ref[turned(head, heads)], NN)
        mixed = product(scores, value_ref[:, here], NN) + outside * rising[:, head : head + 1]
        out_ref[:, here] = mixed
        squares = squares + mixed * mixed
        products = products + grad_ref[:, here].astype(f32) * gain_ref[:, here] * mixed
    ones = jnp.ones((8, size), f32)
    square = lax.dot_general(ones, squares, NT, precision=highest, preferred_element_type=f32)
    product_ = lax.dot_general(ones, products, NT, precision=highest, preferred_element_type=f32)
    for copy in range(sums_ref.shape[0]):
        sums_ref[copy, 0:1, :] = square[0:1, :]
        sums_ref[copy, 1:2, :] = product_[0:1, :]


def row_factors(full_width, size, sums_ref):
    ones = jnp.ones((sums_ref.shape[0], size), f32)
    square = lax.dot_general(sums_ref[:, 0, :], ones, TN, precision=highest, preferred_element_type=f32)
    product_ = lax.dot_general(sums_ref[:, 1, :], ones, TN, precision=highest, preferred_element_type=f32)
    scale = lax.rsqrt(square / full_width + epsilon)
    return scale, scale * scale * scale * (product_ / full_width)


def back_kernel(
    heads, members, full_width, query_ref, tall_ref, mixed_ref, gain_ref, grad_ref, sums_ref, out_ref
):
    size = query_ref.shape[1] // heads
    per = members // heads
    cut = size // per
    rising = jnp.exp(tall_ref[...])
    scale, pull = row_factors(full_width, size, sums_ref)
    for head in range(heads):
        here = cols(head, size)
        slope = scale * (grad_ref[:, here].astype(f32) * gain_ref[:, here]) - pull * mixed_ref[:, here]
        state = product(query_ref[:, here], slope * rising[:, head : head + 1], TN)
        first = turned(head, heads) * per
        for part in range(per):
            out_ref[first + part] = state[part * cut : (part + 1) * cut, :]


def near_kernel(
    heads,
    full_width,
    query_ref,
    key_ref,
    value_ref,
    tall_ref,
    wide_ref,
    state_ref,
    mixed_ref,
    gain_ref,
    grad_ref,
    sums_ref,
    normed_ref,
    grad_q_ref,
    near_k_ref,
    near_v_ref,
):
    size = key_ref.shape[1] // heads
    tall, wide = tall_ref[...], wide_ref[...]
    rising = jnp.exp(tall)
    scale, pull = row_factors(full_width, size, sums_ref)
    for head in range(heads):
        here = cols(head, size)
        query, key, value = query_ref[:, here], key_ref[:, here], value_ref[:, here]
        gain, mixed = gain_ref[:, here], mixed_ref[:, here]
        normed_ref[:, here] = (mixed * scale * gain).astype(bf16)
        slope = scale * (grad_ref[:, here].astype(f32) * gain) - pull * mixed
        weights = weights_of(tall, wide, head)
        scores = product(query, key, NT) * weights
        grad_scores = product(slope, value, NT) * weights
        there = turned(head, heads)
        outer = product(slope, state_ref[there], NT) * rising[:, head : head + 1]
        grad_q_ref[:, here] = (product(grad_scores, key, NN) + outer).astype(bf16)
        near_k_ref[there] = product(grad_scores, query, TN)
        near_v_ref[:, here] = product(scores, slope, TN)


def far_kernel(
    heads,
    key_ref,
    value_ref,
    tall_ref,
    state_ref,
    near_k_ref,
    near_v_ref,
    far_k,
    far_v,
    grad_k_ref,
    grad_v_ref,
    sems,
):
    size = key_ref.shape[1] // heads
    tall = tall_ref[...]
    trailing = jnp.exp(tall[-1:, :] - tall)
    copies = []
    for head in range(heads):
        here = cols(head, size)
        late = trailing[:, head : head + 1]
        there = turned(head, heads)
        state = state_ref[there]
        grad_k = near_k_ref[there] + product(value_ref[:, here], state, NT) * late
        grad_v = near_v_ref[:, here] + product(key_ref[:, here], state, NN) * late
        grad_k_ref[:, here] = grad_k.astype(bf16)
        grad_v_ref[:, here] = grad_v.astype(bf16)
        if head % 2 == 1:
            part = parted(heads, size)[head // 2]
            copies += [
                pltpu.make_async_copy(grad_k_ref.at[:, part], far_k.at[:, part], sems.at[head - 1]),
                pltpu.make_async_copy(grad_v_ref.at[:, part], far_v.at[:, part], sems.at[head]),
            ]
            for copy in copies[-2:]:
                copy.start()
    for copy in copies:
        copy.wait()


def call(kernel, outs, *args, flops=0, copied=(), written=(), copies=0, aliases=None):
    vmem = pl.BlockSpec(memory_space=pltpu.VMEM)
    hbm = pl.BlockSpec(memory_space=pltpu.HBM)
    if copied:
        args = [pltpu.with_memory_space_constraint(a, pltpu.HBM) for a in args]
    moved = sum(a.size * a.dtype.itemsize for a in (*args, *outs))
    return pl.pallas_call(
        kernel,
        out_shape=outs,
        in_specs=[hbm if copied else vmem] * len(args),
        out_specs=[hbm if written else vmem] * len(outs),
        input_output_aliases=aliases or {},
        scratch_shapes=[pltpu.VMEM(a.shape, a.dtype) for a in (*copied, *written)]
        + ([pltpu.SemaphoreType.DMA((copies,))] if copies else []),
        cost_estimate=pl.CostEstimate(flops=flops, bytes_accessed=moved, transcendentals=0),
        compiler_params=pltpu.CompilerParams(vmem_limit_bytes=12 * 1024 * 1024),
    )(*args)


def levels(count, tp, heads):
    members = 2 * heads
    span = members // 4
    groups = count // members
    near, far = [], []
    for index in range(tp):
        shift = index % 2 * (span // 2)

        def device(group, place):
            z = (group * span + shift + place % 4) % (count // 4)
            return (z * 4 + place // 4) * tp + index

        for group in range(groups):
            near.append([device(group, place) for place in range(members)])
        for piece in range(members):
            far.append(
                [device(group, piece ^ (2 if group >= groups // 2 else 0)) for group in range(groups)]
            )
    return groups, members, near, far


def shards(queries, key_rows, value_rows, log_decay, norm_gain, grad_output):
    tok_rows, feat_width = queries.shape
    heads = log_decay.shape[1]
    groups, members, near, far = levels(lax.axis_size("ctx"), lax.axis_size("tp"), heads)
    size = feat_width // heads
    rows = heads * size // members
    wide = jax.ShapeDtypeStruct((tok_rows, feat_width), f32)
    narrow = jax.ShapeDtypeStruct((tok_rows, feat_width), bf16)
    gain = norm_gain.reshape(1, feat_width)
    log_decay = log_decay.T
    bind = functools.partial
    shape = jax.ShapeDtypeStruct
    unit = 2 * heads * tok_rows * size * size

    def exchange(parts, lists):
        return lax.all_to_all(parts, ("ctx", "tp"), 0, 0, axis_index_groups=lists)

    states, tall, across = call(
        bind(states_kernel, heads, members),
        [shape((members, rows + 8, size), f32), shape((tok_rows, heads), f32), shape((heads, tok_rows), f32)],
        key_rows,
        value_rows,
        log_decay,
        flops=2 * unit,
        copied=(key_rows, value_rows, log_decay),
        copies=heads + 1,
    )
    pieces = exchange(states, near)
    (total,) = call(
        bind(group_kernel, members, groups, rows), [shape((groups, rows + 8, size), f32)], pieces
    )
    entering, near_gains, far_gains = call(
        bind(spread_kernel, members, groups, rows),
        [shape((members, rows, size), f32), shape((members, 8, size), f32), shape((groups, 8, size), f32)],
        pieces,
        exchange(total, far),
    )
    entry = exchange(entering, near).reshape(heads, size, size)
    mixed, sums = call(
        bind(mixed_kernel, heads),
        [wide, shape((lax.axis_size("tp"), 2, tok_rows), f32)],
        queries,
        key_rows,
        value_rows,
        tall,
        across,
        entry,
        gain,
        grad_output,
        flops=5 * unit,
    )
    gathered = lax.all_to_all(sums, "tp", 0, 0)
    full_width = feat_width * lax.axis_size("tp")
    (back,) = call(
        bind(back_kernel, heads, members, full_width),
        [shape((members, rows, size), f32)],
        queries,
        tall,
        mixed,
        gain,
        grad_output,
        gathered,
        flops=2 * unit,
    )
    back_pieces = exchange(back, near)
    (back_total,) = call(
        bind(back_group_kernel, members, groups),
        [shape((groups, rows, size), f32)],
        back_pieces,
        near_gains,
    )
    (returning,) = call(
        bind(back_spread_kernel, members, groups),
        [shape((members, rows, size), f32)],
        back_pieces,
        near_gains,
        exchange(back_total, far),
        far_gains,
    )
    leaving = exchange(returning, near).reshape(heads, size, size)
    normed, grad_q, near_k, near_v = call(
        bind(near_kernel, heads, full_width),
        [narrow, narrow, shape((heads, size, size), f32), wide],
        queries,
        key_rows,
        value_rows,
        tall,
        across,
        entry,
        mixed,
        gain,
        grad_output,
        gathered,
        flops=13 * unit,
        aliases={5: 2, 6: 3},
    )
    grad_k, grad_v = call(
        bind(far_kernel, heads),
        [narrow, narrow],
        key_rows,
        value_rows,
        tall,
        leaving,
        near_k,
        near_v,
        flops=4 * unit,
        written=(narrow, narrow),
        copies=heads,
    )
    return normed, grad_q, grad_k, grad_v


def solution(mesh):
    both = P("ctx", "tp")
    return jax.shard_map(
        shards,
        mesh=mesh,
        in_specs=(both, both, both, both, P("tp"), both),
        out_specs=(both, both, both, both),
        check_vma=False,
    )
```

```python
import functools

import jax
import jax.numpy as jnp
from jax import lax
from jax.experimental import pallas as pl
from jax.experimental.pallas import tpu as pltpu
from jax.sharding import PartitionSpec as P

epsilon = 1e-06
highest = lax.Precision.HIGHEST
f32 = jnp.float32
bf16 = jnp.bfloat16

NN = (((1,), (0,)), ((), ()))
NT = (((1,), (1,)), ((), ()))
TN = (((0,), (0,)), ((), ()))


def halves(wide):
    high = wide.astype(bf16)
    return high, (wide - high.astype(f32)).astype(bf16)


def product(left, right, dims):
    (left_axes, right_axes), _ = dims
    lefts = halves(left) if left.dtype == f32 else (left,)
    rights = halves(right) if right.dtype == f32 else (right,)
    pairs = [(a, b) for i, a in enumerate(lefts) for j, b in enumerate(rights) if i + j < 2]
    if len(pairs) > 1:
        left = jnp.concatenate([a for a, _ in pairs], axis=left_axes[0])
        right = jnp.concatenate([b for _, b in pairs], axis=right_axes[0])
    return lax.dot_general(left, right, dims, preferred_element_type=f32)


def decays(log_decay):
    rows = log_decay.shape[1]
    above = lax.broadcasted_iota(jnp.int32, (rows, rows), 0)
    along = lax.broadcasted_iota(jnp.int32, (rows, rows), 1)
    upper = (above <= along).astype(f32)
    lower = (above >= along).astype(f32)
    tall = lax.dot_general(lower, log_decay, NT, precision=highest, preferred_element_type=f32)
    wide = lax.dot_general(log_decay, upper, NN, precision=highest, preferred_element_type=f32)
    return tall, wide


def weights_of(tall, wide, head):
    rows = tall.shape[0]
    above = lax.broadcasted_iota(jnp.int32, (rows, rows), 0)
    along = lax.broadcasted_iota(jnp.int32, (rows, rows), 1)
    mask = above >= along
    differences = tall[:, head : head + 1] - wide[head : head + 1, :]
    return jnp.where(mask, jnp.exp(jnp.where(mask, differences, 0.0)), 0.0)


def whereabouts(heads):
    span = 2 * heads // 4
    z_rows = lax.axis_size("ctx") // 4
    shift = (lax.axis_index("tp") & 1) * (span // 2)
    group = lax.div((lax.div(lax.axis_index("ctx"), 4) - shift) & (z_rows - 1), span)
    cut = jnp.logical_and(shift > 0, group == z_rows // span - 1)
    return group, shift, cut


def turned(head, heads):
    half = lax.axis_size("ctx") // (2 * heads) // 2
    return head ^ jnp.where(whereabouts(heads)[0] < half, 0, 1)


def rank(member, cut):
    return member % 4 * 4 + ((member // 4) ^ jnp.where(cut, 2, 0))


def cols(head, size):
    return slice(head * size, (head + 1) * size)


def states_kernel(
    heads, members, key_far, value_far, decay_far, out_ref, tall_ref, wide_ref, key_ref, value_ref, decay_ref, sems
):
    size = key_ref.shape[1] // heads
    per = members // heads
    rows = size // per
    copies = [
        pltpu.make_async_copy(source, target, sems.at[i])
        for i, (source, target) in enumerate(
            ((decay_far, decay_ref), (key_far, key_ref), (value_far, value_ref))
        )
    ]
    for copy in copies:
        copy.start()
    copies[0].wait()
    tall, wide = decays(decay_ref[...])
    tall_ref[...] = tall
    wide_ref[...] = wide
    total = tall[-1:, :]
    trailing = jnp.exp(total - tall)
    copies[1].wait()
    copies[2].wait()
    for head in range(heads):
        here = cols(head, size)
        key, value = key_ref[:, here], value_ref[:, here]
        state = product(key.astype(f32) * trailing[:, head : head + 1], value, TN)
        mark = jnp.broadcast_to(total[:, head : head + 1], (8, size))
        first = turned(head, heads) * per
        for part in range(per):
            out_ref[first + part, :rows, :] = state[part * rows : (part + 1) * rows, :]
            out_ref[first + part, rows:, :] = mark


def times(gain, state):
    return (gain[None] * state.reshape(-1, 8, state.shape[-1])).reshape(state.shape)


def group_kernel(members, rows, piece_ref, out_ref):
    _, _, cut = whereabouts(members // 2)
    total = jnp.zeros((rows, piece_ref.shape[-1]), f32)
    whole = jnp.zeros((8, piece_ref.shape[-1]), f32)
    early = total
    for member in range(members):
        if member == members // 2:
            early = total
        place = rank(member, cut)
        mark = piece_ref[place, rows:, :]
        total = times(jnp.exp(mark), total) + piece_ref[place, :rows, :]
        whole = whole + mark
    out_ref[:rows, :] = jnp.where(cut, early, total)
    out_ref[rows:, :] = whole


def spread_kernel(members, rows, piece_ref, own_ref, *refs):
    *total_refs, out_ref, near_ref, far_ref = refs
    mine, shift, cut = whereabouts(members // 2)
    before = mine + jnp.where(shift > 0, 1, 0)
    nothing = jnp.zeros((rows, piece_ref.shape[-1]), f32)
    every = jnp.where(cut, own_ref[:rows, :], nothing)
    for distance in range(len(total_refs), 0, -1):
        total_ref = total_refs[distance - 1]
        gain = jnp.exp(total_ref[rows:, :])
        far_ref[distance] = gain
        longer = times(gain, every) + total_ref[:rows, :]
        every = jnp.where(jnp.logical_or(cut, distance <= before), longer, every)
    running = jnp.where(cut, nothing, every)
    for member in range(members):
        if member == members // 2:
            running = jnp.where(cut, every, running)
        place = rank(member, cut)
        gain = jnp.exp(piece_ref[place, rows:, :])
        near_ref[place] = gain
        out_ref[place] = running
        running = times(gain, running) + piece_ref[place, :rows, :]


def back_group_kernel(members, piece_ref, near_ref, out_ref):
    _, _, cut = whereabouts(members // 2)
    total = jnp.zeros(piece_ref.shape[1:], f32)
    late = total
    for member in reversed(range(members)):
        place = rank(member, cut)
        total = times(near_ref[place], total) + piece_ref[place]
        if member == members // 2:
            late = total
    out_ref[...] = jnp.where(cut, late, total)


def back_spread_kernel(members, piece_ref, near_ref, far_ref, own_ref, *refs):
    *total_refs, out_ref = refs
    groups = len(total_refs) + 1
    mine, _, cut = whereabouts(members // 2)
    nothing = jnp.zeros(piece_ref.shape[1:], f32)
    every = jnp.where(cut, own_ref[...], nothing)
    for distance in range(groups - 1, 0, -1):
        longer = times(far_ref[groups - distance], every) + total_refs[distance - 1][...]
        every = jnp.where(jnp.logical_or(cut, distance < groups - mine), longer, every)
    running = jnp.where(cut, nothing, every)
    for member in reversed(range(members)):
        place = rank(member, cut)
        out_ref[place] = running
        running = times(near_ref[place], running) + piece_ref[place]
        if member == members // 2:
            running = jnp.where(cut, every, running)


def inside_kernel(heads, query_ref, key_ref, value_ref, tall_ref, wide_ref, out_ref):
    size = key_ref.shape[1] // heads
    tall, wide = tall_ref[...], wide_ref[...]
    for head in range(heads):
        here = cols(head, size)
        scores = product(query_ref[:, here], key_ref[:, here], NT) * weights_of(tall, wide, head)
        out_ref[:, here] = product(scores, value_ref[:, here], NN)


def mixed_kernel(
    heads, query_ref, tall_ref, inside_ref, state_ref, gain_ref, grad_ref, out_ref, sums_ref
):
    size = query_ref.shape[1] // heads
    rows = query_ref.shape[0]
    rising = jnp.exp(tall_ref[...])
    squares = jnp.zeros((rows, size), f32)
    products = jnp.zeros((rows, size), f32)
    for head in range(heads):
        here = cols(head, size)
        outside = product(query_ref[:, here], state_ref[turned(head, heads)], NN)
        mixed = inside_ref[:, here] + outside * rising[:, head : head + 1]
        out_ref[:, here] = mixed
        squares = squares + mixed * mixed
        products = products + grad_ref[:, here].astype(f32) * gain_ref[:, here] * mixed
    ones = jnp.ones((8, size), f32)
    square = lax.dot_general(ones, squares, NT, precision=highest, preferred_element_type=f32)
    product_ = lax.dot_general(ones, products, NT, precision=highest, preferred_element_type=f32)
    for copy in range(sums_ref.shape[0]):
        sums_ref[copy, 0:1, :] = square[0:1, :]
        sums_ref[copy, 1:2, :] = product_[0:1, :]


def row_factors(full_width, size, sums_ref):
    ones = jnp.ones((sums_ref.shape[0], size), f32)
    square = lax.dot_general(sums_ref[:, 0, :], ones, TN, precision=highest, preferred_element_type=f32)
    product_ = lax.dot_general(sums_ref[:, 1, :], ones, TN, precision=highest, preferred_element_type=f32)
    scale = lax.rsqrt(square / full_width + epsilon)
    return scale, scale * scale * scale * (product_ / full_width)


def back_kernel(
    heads, members, full_width, query_ref, tall_ref, mixed_ref, gain_ref, grad_ref, sums_ref, out_ref
):
    size = query_ref.shape[1] // heads
    per = members // heads
    cut = size // per
    rising = jnp.exp(tall_ref[...])
    scale, pull = row_factors(full_width, size, sums_ref)
    for head in range(heads):
        here = cols(head, size)
        slope = scale * (grad_ref[:, here].astype(f32) * gain_ref[:, here]) - pull * mixed_ref[:, here]
        state = product(query_ref[:, here], slope * rising[:, head : head + 1], TN)
        first = turned(head, heads) * per
        for part in range(per):
            out_ref[first + part] = state[part * cut : (part + 1) * cut, :]


def near_kernel(
    heads,
    full_width,
    query_ref,
    key_ref,
    value_ref,
    tall_ref,
    wide_ref,
    state_ref,
    mixed_ref,
    gain_ref,
    grad_ref,
    sums_ref,
    normed_ref,
    grad_q_ref,
    near_k_ref,
    near_v_ref,
):
    size = key_ref.shape[1] // heads
    tall, wide = tall_ref[...], wide_ref[...]
    rising = jnp.exp(tall)
    scale, pull = row_factors(full_width, size, sums_ref)
    for head in range(heads):
        here = cols(head, size)
        query, key, value = query_ref[:, here], key_ref[:, here], value_ref[:, here]
        gain, mixed = gain_ref[:, here], mixed_ref[:, here]
        normed_ref[:, here] = (mixed * scale * gain).astype(bf16)
        slope = scale * (grad_ref[:, here].astype(f32) * gain) - pull * mixed
        weights = weights_of(tall, wide, head)
        scores = product(query, key, NT) * weights
        grad_scores = product(slope, value, NT) * weights
        there = turned(head, heads)
        outer = product(slope, state_ref[there], NT) * rising[:, head : head + 1]
        grad_q_ref[:, here] = (product(grad_scores, key, NN) + outer).astype(bf16)
        near_k_ref[there] = product(grad_scores, query, TN)
        near_v_ref[:, here] = product(scores, slope, TN)


def far_kernel(heads, key_ref, value_ref, tall_ref, state_ref, near_k_ref, near_v_ref, grad_k_ref, grad_v_ref):
    size = key_ref.shape[1] // heads
    tall = tall_ref[...]
    trailing = jnp.exp(tall[-1:, :] - tall)
    for head in range(heads):
        here = cols(head, size)
        late = trailing[:, head : head + 1]
        there = turned(head, heads)
        state = state_ref[there]
        grad_k = near_k_ref[there] + product(value_ref[:, here], state, NT) * late
        grad_v = near_v_ref[:, here] + product(key_ref[:, here], state, NN) * late
        grad_k_ref[:, here] = grad_k.astype(bf16)
        grad_v_ref[:, here] = grad_v.astype(bf16)


def call(kernel, outs, *args, flops=0, copied=(), aliases=None):
    vmem = pl.BlockSpec(memory_space=pltpu.VMEM)
    hbm = pl.BlockSpec(memory_space=pltpu.HBM)
    if copied:
        args = [pltpu.with_memory_space_constraint(a, pltpu.HBM) for a in args]
    moved = sum(a.size * a.dtype.itemsize for a in (*args, *outs))
    return pl.pallas_call(
        kernel,
        out_shape=outs,
        in_specs=[hbm if copied else vmem] * len(args),
        out_specs=[vmem] * len(outs),
        input_output_aliases=aliases or {},
        scratch_shapes=[pltpu.VMEM(a.shape, a.dtype) for a in copied]
        + ([pltpu.SemaphoreType.DMA((len(copied),))] if copied else []),
        cost_estimate=pl.CostEstimate(flops=flops, bytes_accessed=moved, transcendentals=0),
        compiler_params=pltpu.CompilerParams(vmem_limit_bytes=12 * 1024 * 1024),
    )(*args)


def levels(count, tp, heads):
    members = 2 * heads
    span = members // 4
    groups = count // members
    near, far = [], []
    for index in range(tp):
        shift = index % 2 * (span // 2)

        def device(group, place):
            z = (group * span + shift + place % 4) % (count // 4)
            return (z * 4 + place // 4) * tp + index

        for group in range(groups):
            near.append([device(group, place) for place in range(members)])
        for piece in range(members):
            far.append(
                [device(group, piece ^ (2 if group >= groups // 2 else 0)) for group in range(groups)]
            )
    return groups, members, near, far


def shards(queries, key_rows, value_rows, log_decay, norm_gain, grad_output):
    tok_rows, feat_width = queries.shape
    heads = log_decay.shape[1]
    groups, members, near, far = levels(lax.axis_size("ctx"), lax.axis_size("tp"), heads)
    size = feat_width // heads
    rows = heads * size // members
    wide = jax.ShapeDtypeStruct((tok_rows, feat_width), f32)
    narrow = jax.ShapeDtypeStruct((tok_rows, feat_width), bf16)
    gain = norm_gain.reshape(1, feat_width)
    log_decay = log_decay.T
    bind = functools.partial
    shape = jax.ShapeDtypeStruct
    unit = 2 * heads * tok_rows * size * size

    def exchange(parts, lists):
        return lax.all_to_all(parts, ("ctx", "tp"), 0, 0, axis_index_groups=lists)

    def passed_on(total, way):
        return [
            lax.ppermute(
                total,
                ("ctx", "tp"),
                [(line[g], line[(g + way * distance) % groups]) for line in far for g in range(groups)],
            )
            for distance in range(1, groups)
        ]

    states, tall, across = call(
        bind(states_kernel, heads, members),
        [shape((members, rows + 8, size), f32), shape((tok_rows, heads), f32), shape((heads, tok_rows), f32)],
        key_rows,
        value_rows,
        log_decay,
        flops=2 * unit,
        copied=(key_rows, value_rows, log_decay),
    )
    pieces = exchange(states, near)
    (total,) = call(bind(group_kernel, members, rows), [shape((rows + 8, size), f32)], pieces)
    (inside,) = call(
        bind(inside_kernel, heads), [wide], queries, key_rows, value_rows, tall, across, flops=3 * unit
    )
    entering, near_gains, far_gains = call(
        bind(spread_kernel, members, rows),
        [shape((members, rows, size), f32), shape((members, 8, size), f32), shape((groups, 8, size), f32)],
        pieces,
        total,
        *passed_on(total, 1),
    )
    entry = exchange(entering, near).reshape(heads, size, size)
    mixed, sums = call(
        bind(mixed_kernel, heads),
        [wide, shape((lax.axis_size("tp"), 2, tok_rows), f32)],
        queries,
        tall,
        inside,
        entry,
        gain,
        grad_output,
        flops=2 * unit,
    )
    gathered = lax.all_to_all(sums, "tp", 0, 0)
    full_width = feat_width * lax.axis_size("tp")
    (back,) = call(
        bind(back_kernel, heads, members, full_width),
        [shape((members, rows, size), f32)],
        queries,
        tall,
        mixed,
        gain,
        grad_output,
        gathered,
        flops=2 * unit,
    )
    back_pieces = exchange(back, near)
    (back_total,) = call(
        bind(back_group_kernel, members),
        [shape((rows, size), f32)],
        back_pieces,
        near_gains,
    )
    (returning,) = call(
        bind(back_spread_kernel, members),
        [shape((members, rows, size), f32)],
        back_pieces,
        near_gains,
        far_gains,
        back_total,
        *passed_on(back_total, -1),
    )
    leaving = exchange(returning, near).reshape(heads, size, size)
    normed, grad_q, near_k, near_v = call(
        bind(near_kernel, heads, full_width),
        [narrow, narrow, shape((heads, size, size), f32), wide],
        queries,
        key_rows,
        value_rows,
        tall,
        across,
        entry,
        mixed,
        gain,
        grad_output,
        gathered,
        flops=13 * unit,
        aliases={5: 2, 6: 3},
    )
    grad_k, grad_v = call(
        bind(far_kernel, heads),
        [narrow, narrow],
        key_rows,
        value_rows,
        tall,
        leaving,
        near_k,
        near_v,
        flops=4 * unit,
    )
    return normed, grad_q, grad_k, grad_v


def solution(mesh):
    both = P("ctx", "tp")
    return jax.shard_map(
        shards,
        mesh=mesh,
        in_specs=(both, both, both, both, P("tp"), both),
        out_specs=(both, both, both, both),
        check_vma=False,
    )
```

```python
import functools

import jax
import jax.numpy as jnp
from jax import lax
from jax.experimental import pallas as pl
from jax.experimental.pallas import tpu as pltpu
from jax.sharding import PartitionSpec as P

epsilon = 1e-06
highest = lax.Precision.HIGHEST
f32 = jnp.float32
bf16 = jnp.bfloat16

NN = (((1,), (0,)), ((), ()))
NT = (((1,), (1,)), ((), ()))
TN = (((0,), (0,)), ((), ()))


def halves(wide):
    high = wide.astype(bf16)
    return high, (wide - high.astype(f32)).astype(bf16)


def product(left, right, dims, deep=False):
    (left_axes, right_axes), _ = dims
    lefts = halves(left) if left.dtype == f32 else (left,)
    rights = halves(right) if right.dtype == f32 else (right,)
    pairs = [(a, b) for i, a in enumerate(lefts) for j, b in enumerate(rights) if i + j < 2]
    if deep and len(pairs) > 1:
        left = jnp.concatenate([a for a, _ in pairs], axis=left_axes[0])
        right = jnp.concatenate([b for _, b in pairs], axis=right_axes[0])
        pairs = [(left, right)]
    total = None
    for a, b in pairs:
        term = lax.dot_general(a, b, dims, preferred_element_type=f32)
        total = term if total is None else total + term
    return total


def decays(log_decay):
    rows = log_decay.shape[1]
    above = lax.broadcasted_iota(jnp.int32, (rows, rows), 0)
    along = lax.broadcasted_iota(jnp.int32, (rows, rows), 1)
    upper = (above <= along).astype(f32)
    lower = (above >= along).astype(f32)
    tall = lax.dot_general(lower, log_decay, NT, precision=highest, preferred_element_type=f32)
    wide = lax.dot_general(log_decay, upper, NN, precision=highest, preferred_element_type=f32)
    return tall, wide


def weights_of(tall, wide, head):
    rows = tall.shape[0]
    above = lax.broadcasted_iota(jnp.int32, (rows, rows), 0)
    along = lax.broadcasted_iota(jnp.int32, (rows, rows), 1)
    mask = above >= along
    differences = tall[:, head : head + 1] - wide[head : head + 1, :]
    return jnp.where(mask, jnp.exp(jnp.where(mask, differences, 0.0)), 0.0)


def whereabouts(heads):
    span = 2 * heads // 4
    z_rows = lax.axis_size("ctx") // 4
    shift = (lax.axis_index("tp") & 1) * (span // 2)
    group = lax.div((lax.div(lax.axis_index("ctx"), 4) - shift) & (z_rows - 1), span)
    cut = jnp.logical_and(shift > 0, group == z_rows // span - 1)
    return group, shift, cut


def turned(head, heads):
    group, shift, _ = whereabouts(heads)
    half = lax.axis_size("ctx") // (2 * heads) // 2
    return head ^ jnp.where(group < half, 0, jnp.where(shift > 0, 4, 1))


def rank(member, shift, cut):
    x, z = member % 4, (member // 4) ^ jnp.where(cut, 2, 0)
    return jnp.where(shift > 0, z * 4 + x, x * 4 + z)


def cols(head, size):
    return slice(head * size, (head + 1) * size)


def states_kernel(
    heads, members, key_far, value_far, decay_far, out_ref, tall_ref, wide_ref, key_ref, value_ref, decay_ref, sems
):
    size = key_ref.shape[1] // heads
    per = members // heads
    rows = size // per
    copies = [
        pltpu.make_async_copy(source, target, sems.at[i])
        for i, (source, target) in enumerate(
            ((decay_far, decay_ref), (key_far, key_ref), (value_far, value_ref))
        )
    ]
    for copy in copies:
        copy.start()
    copies[0].wait()
    tall, wide = decays(decay_ref[...])
    tall_ref[...] = tall
    wide_ref[...] = wide
    total = tall[-1:, :]
    trailing = jnp.exp(total - tall)
    copies[1].wait()
    copies[2].wait()
    for head in range(heads):
        here = cols(head, size)
        key, value = key_ref[:, here], value_ref[:, here]
        state = product(key.astype(f32) * trailing[:, head : head + 1], value, TN)
        mark = jnp.broadcast_to(total[:, head : head + 1], (8, size))
        first = turned(head, heads) * per
        for part in range(per):
            out_ref[first + part, :rows, :] = state[part * rows : (part + 1) * rows, :]
            out_ref[first + part, rows:, :] = mark


def times(gain, state):
    return (gain[None] * state.reshape(-1, 8, state.shape[-1])).reshape(state.shape)


def group_kernel(members, copies, rows, piece_ref, out_ref):
    _, shift, cut = whereabouts(members // 2)
    total = jnp.zeros((rows, piece_ref.shape[-1]), f32)
    whole = jnp.zeros((8, piece_ref.shape[-1]), f32)
    early = total
    for member in range(members):
        if member == members // 2:
            early = total
        place = rank(member, shift, cut)
        mark = piece_ref[place, rows:, :]
        total = times(jnp.exp(mark), total) + piece_ref[place, :rows, :]
        whole = whole + mark
    total = jnp.where(cut, early, total)
    for copy in range(copies):
        out_ref[copy, :rows, :] = total
        out_ref[copy, rows:, :] = whole


def spread_kernel(members, groups, rows, piece_ref, total_ref, out_ref, near_ref, far_ref):
    mine, shift, cut = whereabouts(members // 2)
    first = jnp.where(shift > 0, groups - 1, 0)
    before = jnp.where(cut, 0, mine + jnp.where(shift > 0, 1, 0))
    every = jnp.zeros((rows, piece_ref.shape[-1]), f32)
    running = every
    for step in range(groups):
        group = (step + first) & (groups - 1)
        gain = jnp.exp(total_ref[group, rows:, :])
        far_ref[group] = gain
        every = times(gain, every) + total_ref[group, :rows, :]
        running = jnp.where(step < before, every, running)
    for member in range(members):
        if member == members // 2:
            running = jnp.where(cut, every, running)
        place = rank(member, shift, cut)
        gain = jnp.exp(piece_ref[place, rows:, :])
        near_ref[place] = gain
        out_ref[place] = running
        running = times(gain, running) + piece_ref[place, :rows, :]


def back_group_kernel(members, copies, piece_ref, near_ref, out_ref):
    _, shift, cut = whereabouts(members // 2)
    total = jnp.zeros(piece_ref.shape[1:], f32)
    late = total
    for member in reversed(range(members)):
        place = rank(member, shift, cut)
        total = times(near_ref[place], total) + piece_ref[place]
        if member == members // 2:
            late = total
    total = jnp.where(cut, late, total)
    for copy in range(copies):
        out_ref[copy] = total


def back_spread_kernel(members, groups, piece_ref, near_ref, total_ref, far_ref, out_ref):
    mine, shift, cut = whereabouts(members // 2)
    every = jnp.zeros(piece_ref.shape[1:], f32)
    running = every
    for group in reversed(range(groups)):
        every = times(far_ref[group], every) + total_ref[group]
        running = jnp.where(group > mine, every, running)
    for member in reversed(range(members)):
        place = rank(member, shift, cut)
        out_ref[place] = running
        running = times(near_ref[place], running) + piece_ref[place]
        if member == members // 2:
            running = jnp.where(cut, every, running)


def inside_kernel(heads, query_ref, key_ref, value_ref, tall_ref, wide_ref, out_ref):
    size = key_ref.shape[1] // heads
    tall, wide = tall_ref[...], wide_ref[...]
    for head in range(heads):
        here = cols(head, size)
        scores = product(query_ref[:, here], key_ref[:, here], NT) * weights_of(tall, wide, head)
        out_ref[:, here] = product(scores, value_ref[:, here], NN)


def mixed_kernel(
    heads, query_ref, tall_ref, inside_ref, state_ref, gain_ref, grad_ref, out_ref, sums_ref
):
    size = query_ref.shape[1] // heads
    rows = query_ref.shape[0]
    rising = jnp.exp(tall_ref[...])
    squares = jnp.zeros((rows, size), f32)
    products = jnp.zeros((rows, size), f32)
    for head in range(heads):
        here = cols(head, size)
        outside = product(query_ref[:, here], state_ref[turned(head, heads)], NN)
        mixed = inside_ref[:, here] + outside * rising[:, head : head + 1]
        out_ref[:, here] = mixed
        squares = squares + mixed * mixed
        products = products + grad_ref[:, here].astype(f32) * gain_ref[:, here] * mixed
    ones = jnp.ones((8, size), f32)
    square = lax.dot_general(ones, squares, NT, precision=highest, preferred_element_type=f32)
    product_ = lax.dot_general(ones, products, NT, precision=highest, preferred_element_type=f32)
    for copy in range(sums_ref.shape[0]):
        sums_ref[copy, 0:1, :] = square[0:1, :]
        sums_ref[copy, 1:2, :] = product_[0:1, :]


def row_factors(full_width, size, sums_ref):
    ones = jnp.ones((sums_ref.shape[0], size), f32)
    square = lax.dot_general(sums_ref[:, 0, :], ones, TN, precision=highest, preferred_element_type=f32)
    product_ = lax.dot_general(sums_ref[:, 1, :], ones, TN, precision=highest, preferred_element_type=f32)
    scale = lax.rsqrt(square / full_width + epsilon)
    return scale, scale * scale * scale * (product_ / full_width)


def back_kernel(
    heads, members, full_width, query_ref, tall_ref, mixed_ref, gain_ref, grad_ref, sums_ref, out_ref
):
    size = query_ref.shape[1] // heads
    per = members // heads
    cut = size // per
    rising = jnp.exp(tall_ref[...])
    scale, pull = row_factors(full_width, size, sums_ref)
    for head in range(heads):
        here = cols(head, size)
        slope = scale * (grad_ref[:, here].astype(f32) * gain_ref[:, here]) - pull * mixed_ref[:, here]
        state = product(query_ref[:, here], slope * rising[:, head : head + 1], TN)
        first = turned(head, heads) * per
        for part in range(per):
            out_ref[first + part] = state[part * cut : (part + 1) * cut, :]


def near_kernel(
    heads,
    full_width,
    query_ref,
    key_ref,
    value_ref,
    tall_ref,
    wide_ref,
    state_ref,
    mixed_ref,
    gain_ref,
    grad_ref,
    sums_ref,
    normed_ref,
    grad_q_ref,
    near_k_ref,
    near_v_ref,
):
    size = key_ref.shape[1] // heads
    tall, wide = tall_ref[...], wide_ref[...]
    rising = jnp.exp(tall)
    scale, pull = row_factors(full_width, size, sums_ref)
    for head in range(heads):
        here = cols(head, size)
        query, key, value = query_ref[:, here], key_ref[:, here], value_ref[:, here]
        gain, mixed = gain_ref[:, here], mixed_ref[:, here]
        normed_ref[:, here] = (mixed * scale * gain).astype(bf16)
        slope = scale * (grad_ref[:, here].astype(f32) * gain) - pull * mixed
        weights = weights_of(tall, wide, head)
        scores = product(query, key, NT, True) * weights
        grad_scores = product(slope, value, NT, True) * weights
        there = turned(head, heads)
        outer = product(slope, state_ref[there], NT, True) * rising[:, head : head + 1]
        grad_q_ref[:, here] = (product(grad_scores, key, NN, True) + outer).astype(bf16)
        near_k_ref[there] = product(grad_scores, query, TN, True)
        near_v_ref[:, here] = product(scores, slope, TN, True)


def far_kernel(heads, key_ref, value_ref, tall_ref, state_ref, near_k_ref, near_v_ref, grad_k_ref, grad_v_ref):
    size = key_ref.shape[1] // heads
    tall = tall_ref[...]
    trailing = jnp.exp(tall[-1:, :] - tall)
    for head in range(heads):
        here = cols(head, size)
        late = trailing[:, head : head + 1]
        there = turned(head, heads)
        state = state_ref[there]
        grad_k = near_k_ref[there] + product(value_ref[:, here], state, NT, True) * late
        grad_v = near_v_ref[:, here] + product(key_ref[:, here], state, NN, True) * late
        grad_k_ref[:, here] = grad_k.astype(bf16)
        grad_v_ref[:, here] = grad_v.astype(bf16)


def call(kernel, outs, *args, flops=0, copied=(), aliases=None):
    vmem = pl.BlockSpec(memory_space=pltpu.VMEM)
    hbm = pl.BlockSpec(memory_space=pltpu.HBM)
    if copied:
        args = [pltpu.with_memory_space_constraint(a, pltpu.HBM) for a in args]
    moved = sum(a.size * a.dtype.itemsize for a in (*args, *outs))
    return pl.pallas_call(
        kernel,
        out_shape=outs,
        in_specs=[hbm if copied else vmem] * len(args),
        out_specs=[vmem] * len(outs),
        input_output_aliases=aliases or {},
        scratch_shapes=[pltpu.VMEM(a.shape, a.dtype) for a in copied]
        + ([pltpu.SemaphoreType.DMA((len(copied),))] if copied else []),
        cost_estimate=pl.CostEstimate(flops=flops, bytes_accessed=moved, transcendentals=0),
        compiler_params=pltpu.CompilerParams(vmem_limit_bytes=12 * 1024 * 1024),
    )(*args)


def levels(count, tp, heads):
    members = 2 * heads
    span = members // 4
    groups = count // members
    near, far = [], []
    for index in range(tp):
        shift = index % 2 * (span // 2)

        def device(group, place):
            x, z = (place % 4, place // 4) if shift else (place // 4, place % 4)
            return ((group * span + shift + z) % (count // 4) * 4 + x) * tp + index

        for group in range(groups):
            near.append([device(group, place) for place in range(members)])
        for piece in range(members):
            far.append(
                [
                    device(group, piece ^ ((8 if shift else 2) if group >= groups // 2 else 0))
                    for group in range(groups)
                ]
            )
    return groups, members, near, far


def shards(queries, key_rows, value_rows, log_decay, norm_gain, grad_output):
    tok_rows, feat_width = queries.shape
    heads = log_decay.shape[1]
    groups, members, near, far = levels(lax.axis_size("ctx"), lax.axis_size("tp"), heads)
    size = feat_width // heads
    rows = heads * size // members
    wide = jax.ShapeDtypeStruct((tok_rows, feat_width), f32)
    narrow = jax.ShapeDtypeStruct((tok_rows, feat_width), bf16)
    gain = norm_gain.reshape(1, feat_width)
    log_decay = log_decay.T
    bind = functools.partial
    shape = jax.ShapeDtypeStruct
    unit = 2 * heads * tok_rows * size * size

    def exchange(parts, lists):
        return lax.all_to_all(parts, ("ctx", "tp"), 0, 0, axis_index_groups=lists)

    states, tall, across = call(
        bind(states_kernel, heads, members),
        [shape((members, rows + 8, size), f32), shape((tok_rows, heads), f32), shape((heads, tok_rows), f32)],
        key_rows,
        value_rows,
        log_decay,
        flops=2 * unit,
        copied=(key_rows, value_rows, log_decay),
    )
    pieces = exchange(states, near)
    (total,) = call(
        bind(group_kernel, members, groups, rows), [shape((groups, rows + 8, size), f32)], pieces
    )
    (inside,) = call(
        bind(inside_kernel, heads), [wide], queries, key_rows, value_rows, tall, across, flops=3 * unit
    )
    entering, near_gains, far_gains = call(
        bind(spread_kernel, members, groups, rows),
        [shape((members, rows, size), f32), shape((members, 8, size), f32), shape((groups, 8, size), f32)],
        pieces,
        exchange(total, far),
    )
    entry = exchange(entering, near).reshape(heads, size, size)
    mixed, sums = call(
        bind(mixed_kernel, heads),
        [wide, shape((lax.axis_size("tp"), 2, tok_rows), f32)],
        queries,
        tall,
        inside,
        entry,
        gain,
        grad_output,
        flops=2 * unit,
    )
    gathered = lax.all_to_all(sums, "tp", 0, 0)
    full_width = feat_width * lax.axis_size("tp")
    (back,) = call(
        bind(back_kernel, heads, members, full_width),
        [shape((members, rows, size), f32)],
        queries,
        tall,
        mixed,
        gain,
        grad_output,
        gathered,
        flops=2 * unit,
    )
    back_pieces = exchange(back, near)
    (back_total,) = call(
        bind(back_group_kernel, members, groups),
        [shape((groups, rows, size), f32)],
        back_pieces,
        near_gains,
    )
    (returning,) = call(
        bind(back_spread_kernel, members, groups),
        [shape((members, rows, size), f32)],
        back_pieces,
        near_gains,
        exchange(back_total, far),
        far_gains,
    )
    leaving = exchange(returning, near).reshape(heads, size, size)
    normed, grad_q, near_k, near_v = call(
        bind(near_kernel, heads, full_width),
        [narrow, narrow, shape((heads, size, size), f32), wide],
        queries,
        key_rows,
        value_rows,
        tall,
        across,
        entry,
        mixed,
        gain,
        grad_output,
        gathered,
        flops=13 * unit,
        aliases={5: 2, 6: 3},
    )
    grad_k, grad_v = call(
        bind(far_kernel, heads),
        [narrow, narrow],
        key_rows,
        value_rows,
        tall,
        leaving,
        near_k,
        near_v,
        flops=4 * unit,
    )
    return normed, grad_q, grad_k, grad_v


def solution(mesh):
    both = P("ctx", "tp")
    return jax.shard_map(
        shards,
        mesh=mesh,
        in_specs=(both, both, both, both, P("tp"), both),
        out_specs=(both, both, both, both),
        check_vma=False,
    )
```

```python
import functools

import jax
import jax.numpy as jnp
from jax import lax
from jax.experimental import pallas as pl
from jax.experimental.pallas import tpu as pltpu
from jax.sharding import PartitionSpec as P

epsilon = 1e-06
highest = lax.Precision.HIGHEST
f32 = jnp.float32
bf16 = jnp.bfloat16

NN = (((1,), (0,)), ((), ()))
NT = (((1,), (1,)), ((), ()))
TN = (((0,), (0,)), ((), ()))


def halves(wide):
    high = wide.astype(bf16)
    return high, (wide - high.astype(f32)).astype(bf16)


def product(left, right, dims, deep=False):
    (left_axes, right_axes), _ = dims
    lefts = halves(left) if left.dtype == f32 else (left,)
    rights = halves(right) if right.dtype == f32 else (right,)
    pairs = [(a, b) for i, a in enumerate(lefts) for j, b in enumerate(rights) if i + j < 2]
    if deep and len(pairs) > 1:
        left = jnp.concatenate([a for a, _ in pairs], axis=left_axes[0])
        right = jnp.concatenate([b for _, b in pairs], axis=right_axes[0])
        pairs = [(left, right)]
    total = None
    for a, b in pairs:
        term = lax.dot_general(a, b, dims, preferred_element_type=f32)
        total = term if total is None else total + term
    return total


def decays(log_decay):
    rows = log_decay.shape[1]
    above = lax.broadcasted_iota(jnp.int32, (rows, rows), 0)
    along = lax.broadcasted_iota(jnp.int32, (rows, rows), 1)
    upper = (above <= along).astype(f32)
    lower = (above >= along).astype(f32)
    tall = lax.dot_general(lower, log_decay, NT, precision=highest, preferred_element_type=f32)
    wide = lax.dot_general(log_decay, upper, NN, precision=highest, preferred_element_type=f32)
    return tall, wide


def weights_of(tall, wide, head):
    rows = tall.shape[0]
    above = lax.broadcasted_iota(jnp.int32, (rows, rows), 0)
    along = lax.broadcasted_iota(jnp.int32, (rows, rows), 1)
    mask = above >= along
    differences = tall[:, head : head + 1] - wide[head : head + 1, :]
    return jnp.where(mask, jnp.exp(jnp.where(mask, differences, 0.0)), 0.0)


def whereabouts(heads):
    span = 2 * heads // 4
    z_rows = lax.axis_size("ctx") // 4
    shift = (1 - (lax.axis_index("tp") & 1)) * (span // 2)
    group = lax.div((lax.div(lax.axis_index("ctx"), 4) - shift) & (z_rows - 1), span)
    cut = jnp.logical_and(shift > 0, group == z_rows // span - 1)
    return group, shift, cut


def turned(head, heads):
    half = lax.axis_size("ctx") // (2 * heads) // 2
    return head ^ jnp.where(whereabouts(heads)[0] < half, 0, 1)


def rank(member, cut):
    return member % 4 * 4 + ((member // 4) ^ jnp.where(cut, 2, 0))


def cols(head, size):
    return slice(head * size, (head + 1) * size)


def states_kernel(
    heads, members, key_far, value_far, decay_far, out_ref, tall_ref, wide_ref, key_ref, value_ref, decay_ref, sems
):
    size = key_ref.shape[1] // heads
    per = members // heads
    rows = size // per
    copies = [
        pltpu.make_async_copy(source, target, sems.at[i])
        for i, (source, target) in enumerate(
            ((decay_far, decay_ref), (key_far, key_ref), (value_far, value_ref))
        )
    ]
    for copy in copies:
        copy.start()
    copies[0].wait()
    tall, wide = decays(decay_ref[...])
    tall_ref[...] = tall
    wide_ref[...] = wide
    total = tall[-1:, :]
    trailing = jnp.exp(total - tall)
    copies[1].wait()
    copies[2].wait()
    for head in range(heads):
        here = cols(head, size)
        key, value = key_ref[:, here], value_ref[:, here]
        state = product(key.astype(f32) * trailing[:, head : head + 1], value, TN)
        mark = jnp.broadcast_to(total[:, head : head + 1], (8, size))
        first = turned(head, heads) * per
        for part in range(per):
            out_ref[first + part, :rows, :] = state[part * rows : (part + 1) * rows, :]
            out_ref[first + part, rows:, :] = mark


def times(gain, state):
    return (gain[None] * state.reshape(-1, 8, state.shape[-1])).reshape(state.shape)


def group_kernel(members, copies, rows, piece_ref, out_ref):
    _, _, cut = whereabouts(members // 2)
    total = jnp.zeros((rows, piece_ref.shape[-1]), f32)
    whole = jnp.zeros((8, piece_ref.shape[-1]), f32)
    early = total
    for member in range(members):
        if member == members // 2:
            early = total
        place = rank(member, cut)
        mark = piece_ref[place, rows:, :]
        total = times(jnp.exp(mark), total) + piece_ref[place, :rows, :]
        whole = whole + mark
    total = jnp.where(cut, early, total)
    for copy in range(copies):
        out_ref[copy, :rows, :] = total
        out_ref[copy, rows:, :] = whole


def spread_kernel(members, groups, rows, piece_ref, total_ref, out_ref, near_ref, far_ref):
    mine, shift, cut = whereabouts(members // 2)
    first = jnp.where(shift > 0, groups - 1, 0)
    before = jnp.where(cut, 0, mine + jnp.where(shift > 0, 1, 0))
    every = jnp.zeros((rows, piece_ref.shape[-1]), f32)
    running = every
    for step in range(groups):
        group = (step + first) & (groups - 1)
        gain = jnp.exp(total_ref[group, rows:, :])
        far_ref[group] = gain
        every = times(gain, every) + total_ref[group, :rows, :]
        running = jnp.where(step < before, every, running)
    for member in range(members):
        if member == members // 2:
            running = jnp.where(cut, every, running)
        place = rank(member, cut)
        gain = jnp.exp(piece_ref[place, rows:, :])
        near_ref[place] = gain
        out_ref[place] = running
        running = times(gain, running) + piece_ref[place, :rows, :]


def back_group_kernel(members, copies, piece_ref, near_ref, out_ref):
    _, _, cut = whereabouts(members // 2)
    total = jnp.zeros(piece_ref.shape[1:], f32)
    late = total
    for member in reversed(range(members)):
        place = rank(member, cut)
        total = times(near_ref[place], total) + piece_ref[place]
        if member == members // 2:
            late = total
    total = jnp.where(cut, late, total)
    for copy in range(copies):
        out_ref[copy] = total


def back_spread_kernel(members, groups, piece_ref, near_ref, total_ref, far_ref, out_ref):
    mine, _, cut = whereabouts(members // 2)
    every = jnp.zeros(piece_ref.shape[1:], f32)
    running = every
    for group in reversed(range(groups)):
        every = times(far_ref[group], every) + total_ref[group]
        running = jnp.where(group > mine, every, running)
    for member in reversed(range(members)):
        place = rank(member, cut)
        out_ref[place] = running
        running = times(near_ref[place], running) + piece_ref[place]
        if member == members // 2:
            running = jnp.where(cut, every, running)


def inside_kernel(heads, query_ref, key_ref, value_ref, tall_ref, wide_ref, out_ref):
    size = key_ref.shape[1] // heads
    tall, wide = tall_ref[...], wide_ref[...]
    for head in range(heads):
        here = cols(head, size)
        scores = product(query_ref[:, here], key_ref[:, here], NT) * weights_of(tall, wide, head)
        out_ref[:, here] = product(scores, value_ref[:, here], NN)


def mixed_kernel(
    heads, query_ref, tall_ref, inside_ref, state_ref, gain_ref, grad_ref, out_ref, sums_ref
):
    size = query_ref.shape[1] // heads
    rows = query_ref.shape[0]
    rising = jnp.exp(tall_ref[...])
    squares = jnp.zeros((rows, size), f32)
    products = jnp.zeros((rows, size), f32)
    for head in range(heads):
        here = cols(head, size)
        outside = product(query_ref[:, here], state_ref[turned(head, heads)], NN)
        mixed = inside_ref[:, here] + outside * rising[:, head : head + 1]
        out_ref[:, here] = mixed
        squares = squares + mixed * mixed
        products = products + grad_ref[:, here].astype(f32) * gain_ref[:, here] * mixed
    ones = jnp.ones((8, size), f32)
    square = lax.dot_general(ones, squares, NT, precision=highest, preferred_element_type=f32)
    product_ = lax.dot_general(ones, products, NT, precision=highest, preferred_element_type=f32)
    for copy in range(sums_ref.shape[0]):
        sums_ref[copy, 0:1, :] = square[0:1, :]
        sums_ref[copy, 1:2, :] = product_[0:1, :]


def row_factors(full_width, size, sums_ref):
    ones = jnp.ones((sums_ref.shape[0], size), f32)
    square = lax.dot_general(sums_ref[:, 0, :], ones, TN, precision=highest, preferred_element_type=f32)
    product_ = lax.dot_general(sums_ref[:, 1, :], ones, TN, precision=highest, preferred_element_type=f32)
    scale = lax.rsqrt(square / full_width + epsilon)
    return scale, scale * scale * scale * (product_ / full_width)


def back_kernel(
    heads, members, full_width, query_ref, tall_ref, mixed_ref, gain_ref, grad_ref, sums_ref, out_ref
):
    size = query_ref.shape[1] // heads
    per = members // heads
    cut = size // per
    rising = jnp.exp(tall_ref[...])
    scale, pull = row_factors(full_width, size, sums_ref)
    for head in range(heads):
        here = cols(head, size)
        slope = scale * (grad_ref[:, here].astype(f32) * gain_ref[:, here]) - pull * mixed_ref[:, here]
        state = product(query_ref[:, here], slope * rising[:, head : head + 1], TN)
        first = turned(head, heads) * per
        for part in range(per):
            out_ref[first + part] = state[part * cut : (part + 1) * cut, :]


def near_kernel(
    heads,
    full_width,
    query_ref,
    key_ref,
    value_ref,
    tall_ref,
    wide_ref,
    state_ref,
    mixed_ref,
    gain_ref,
    grad_ref,
    sums_ref,
    normed_ref,
    grad_q_ref,
    near_k_ref,
    near_v_ref,
):
    size = key_ref.shape[1] // heads
    tall, wide = tall_ref[...], wide_ref[...]
    rising = jnp.exp(tall)
    scale, pull = row_factors(full_width, size, sums_ref)
    for head in range(heads):
        here = cols(head, size)
        query, key, value = query_ref[:, here], key_ref[:, here], value_ref[:, here]
        gain, mixed = gain_ref[:, here], mixed_ref[:, here]
        normed_ref[:, here] = (mixed * scale * gain).astype(bf16)
        slope = scale * (grad_ref[:, here].astype(f32) * gain) - pull * mixed
        weights = weights_of(tall, wide, head)
        scores = product(query, key, NT, True) * weights
        grad_scores = product(slope, value, NT, True) * weights
        there = turned(head, heads)
        outer = product(slope, state_ref[there], NT, True) * rising[:, head : head + 1]
        grad_q_ref[:, here] = (product(grad_scores, key, NN, True) + outer).astype(bf16)
        near_k_ref[there] = product(grad_scores, query, TN, True)
        near_v_ref[:, here] = product(scores, slope, TN, True)


def far_kernel(heads, key_ref, value_ref, tall_ref, state_ref, near_k_ref, near_v_ref, grad_k_ref, grad_v_ref):
    size = key_ref.shape[1] // heads
    tall = tall_ref[...]
    trailing = jnp.exp(tall[-1:, :] - tall)
    for head in range(heads):
        here = cols(head, size)
        late = trailing[:, head : head + 1]
        there = turned(head, heads)
        state = state_ref[there]
        grad_k = near_k_ref[there] + product(value_ref[:, here], state, NT, True) * late
        grad_v = near_v_ref[:, here] + product(key_ref[:, here], state, NN, True) * late
        grad_k_ref[:, here] = grad_k.astype(bf16)
        grad_v_ref[:, here] = grad_v.astype(bf16)


def call(kernel, outs, *args, flops=0, copied=(), aliases=None):
    vmem = pl.BlockSpec(memory_space=pltpu.VMEM)
    hbm = pl.BlockSpec(memory_space=pltpu.HBM)
    if copied:
        args = [pltpu.with_memory_space_constraint(a, pltpu.HBM) for a in args]
    moved = sum(a.size * a.dtype.itemsize for a in (*args, *outs))
    return pl.pallas_call(
        kernel,
        out_shape=outs,
        in_specs=[hbm if copied else vmem] * len(args),
        out_specs=[vmem] * len(outs),
        input_output_aliases=aliases or {},
        scratch_shapes=[pltpu.VMEM(a.shape, a.dtype) for a in copied]
        + ([pltpu.SemaphoreType.DMA((len(copied),))] if copied else []),
        cost_estimate=pl.CostEstimate(flops=flops, bytes_accessed=moved, transcendentals=0),
        compiler_params=pltpu.CompilerParams(vmem_limit_bytes=12 * 1024 * 1024),
    )(*args)


def levels(count, tp, heads):
    members = 2 * heads
    span = members // 4
    groups = count // members
    near, far = [], []
    for index in range(tp):
        shift = (1 - index % 2) * (span // 2)

        def device(group, place):
            z = (group * span + shift + place % 4) % (count // 4)
            return (z * 4 + place // 4) * tp + index

        for group in range(groups):
            near.append([device(group, place) for place in range(members)])
        for piece in range(members):
            far.append(
                [device(group, piece ^ (2 if group >= groups // 2 else 0)) for group in range(groups)]
            )
    return groups, members, near, far


def shards(queries, key_rows, value_rows, log_decay, norm_gain, grad_output):
    tok_rows, feat_width = queries.shape
    heads = log_decay.shape[1]
    groups, members, near, far = levels(lax.axis_size("ctx"), lax.axis_size("tp"), heads)
    size = feat_width // heads
    rows = heads * size // members
    wide = jax.ShapeDtypeStruct((tok_rows, feat_width), f32)
    narrow = jax.ShapeDtypeStruct((tok_rows, feat_width), bf16)
    gain = norm_gain.reshape(1, feat_width)
    log_decay = log_decay.T
    bind = functools.partial
    shape = jax.ShapeDtypeStruct
    unit = 2 * heads * tok_rows * size * size

    def exchange(parts, lists):
        return lax.all_to_all(parts, ("ctx", "tp"), 0, 0, axis_index_groups=lists)

    states, tall, across = call(
        bind(states_kernel, heads, members),
        [shape((members, rows + 8, size), f32), shape((tok_rows, heads), f32), shape((heads, tok_rows), f32)],
        key_rows,
        value_rows,
        log_decay,
        flops=2 * unit,
        copied=(key_rows, value_rows, log_decay),
    )
    pieces = exchange(states, near)
    (total,) = call(
        bind(group_kernel, members, groups, rows), [shape((groups, rows + 8, size), f32)], pieces
    )
    (inside,) = call(
        bind(inside_kernel, heads), [wide], queries, key_rows, value_rows, tall, across, flops=3 * unit
    )
    entering, near_gains, far_gains = call(
        bind(spread_kernel, members, groups, rows),
        [shape((members, rows, size), f32), shape((members, 8, size), f32), shape((groups, 8, size), f32)],
        pieces,
        exchange(total, far),
    )
    entry = exchange(entering, near).reshape(heads, size, size)
    mixed, sums = call(
        bind(mixed_kernel, heads),
        [wide, shape((lax.axis_size("tp"), 2, tok_rows), f32)],
        queries,
        tall,
        inside,
        entry,
        gain,
        grad_output,
        flops=2 * unit,
    )
    gathered = lax.all_to_all(sums, "tp", 0, 0)
    full_width = feat_width * lax.axis_size("tp")
    (back,) = call(
        bind(back_kernel, heads, members, full_width),
        [shape((members, rows, size), f32)],
        queries,
        tall,
        mixed,
        gain,
        grad_output,
        gathered,
        flops=2 * unit,
    )
    back_pieces = exchange(back, near)
    (back_total,) = call(
        bind(back_group_kernel, members, groups),
        [shape((groups, rows, size), f32)],
        back_pieces,
        near_gains,
    )
    (returning,) = call(
        bind(back_spread_kernel, members, groups),
        [shape((members, rows, size), f32)],
        back_pieces,
        near_gains,
        exchange(back_total, far),
        far_gains,
    )
    leaving = exchange(returning, near).reshape(heads, size, size)
    normed, grad_q, near_k, near_v = call(
        bind(near_kernel, heads, full_width),
        [narrow, narrow, shape((heads, size, size), f32), wide],
        queries,
        key_rows,
        value_rows,
        tall,
        across,
        entry,
        mixed,
        gain,
        grad_output,
        gathered,
        flops=13 * unit,
        aliases={5: 2, 6: 3},
    )
    grad_k, grad_v = call(
        bind(far_kernel, heads),
        [narrow, narrow],
        key_rows,
        value_rows,
        tall,
        leaving,
        near_k,
        near_v,
        flops=4 * unit,
    )
    return normed, grad_q, grad_k, grad_v


def solution(mesh):
    both = P("ctx", "tp")
    return jax.shard_map(
        shards,
        mesh=mesh,
        in_specs=(both, both, both, both, P("tp"), both),
        out_specs=(both, both, both, both),
        check_vma=False,
    )
```

```python
import functools

import jax
import jax.numpy as jnp
from jax import lax
from jax.experimental import pallas as pl
from jax.experimental.pallas import tpu as pltpu
from jax.sharding import PartitionSpec as P

epsilon = 1e-06
highest = lax.Precision.HIGHEST
f32 = jnp.float32
bf16 = jnp.bfloat16

NN = (((1,), (0,)), ((), ()))
NT = (((1,), (1,)), ((), ()))
TN = (((0,), (0,)), ((), ()))


def halves(wide):
    high = wide.astype(bf16)
    return high, (wide - high.astype(f32)).astype(bf16)


def product(left, right, dims, deep=False):
    (left_axes, right_axes), _ = dims
    lefts = halves(left) if left.dtype == f32 else (left,)
    rights = halves(right) if right.dtype == f32 else (right,)
    pairs = [(a, b) for i, a in enumerate(lefts) for j, b in enumerate(rights) if i + j < 2]
    if deep and len(pairs) > 1:
        left = jnp.concatenate([a for a, _ in pairs], axis=left_axes[0])
        right = jnp.concatenate([b for _, b in pairs], axis=right_axes[0])
        pairs = [(left, right)]
    total = None
    for a, b in pairs:
        term = lax.dot_general(a, b, dims, preferred_element_type=f32)
        total = term if total is None else total + term
    return total


def decays(log_decay):
    rows = log_decay.shape[1]
    above = lax.broadcasted_iota(jnp.int32, (rows, rows), 0)
    along = lax.broadcasted_iota(jnp.int32, (rows, rows), 1)
    upper = (above <= along).astype(f32)
    lower = (above >= along).astype(f32)
    tall = lax.dot_general(lower, log_decay, NT, precision=highest, preferred_element_type=f32)
    wide = lax.dot_general(log_decay, upper, NN, precision=highest, preferred_element_type=f32)
    return tall, wide


def weights_of(tall, wide, head):
    rows = tall.shape[0]
    above = lax.broadcasted_iota(jnp.int32, (rows, rows), 0)
    along = lax.broadcasted_iota(jnp.int32, (rows, rows), 1)
    mask = above >= along
    differences = tall[:, head : head + 1] - wide[head : head + 1, :]
    return jnp.where(mask, jnp.exp(jnp.where(mask, differences, 0.0)), 0.0)


def whereabouts(heads):
    span = 2 * heads // 4
    z_rows = lax.axis_size("ctx") // 4
    shift = (lax.axis_index("tp") & 1) * (span // 2)
    group = lax.div((lax.div(lax.axis_index("ctx"), 4) - shift) & (z_rows - 1), span)
    cut = jnp.logical_and(shift > 0, group == z_rows // span - 1)
    return group, shift, cut


def turned(head, heads):
    half = lax.axis_size("ctx") // (2 * heads) // 2
    return head ^ jnp.where(whereabouts(heads)[0] < half, 0, 1)


def rank(member, cut):
    return member % 4 * 4 + ((member // 4) ^ jnp.where(cut, 2, 0))


def cols(head, size):
    return slice(head * size, (head + 1) * size)


def states_kernel(
    heads, members, key_far, value_far, decay_far, out_ref, tall_ref, wide_ref, key_ref, value_ref, decay_ref, sems
):
    size = key_ref.shape[1] // heads
    per = members // heads
    rows = size // per
    copies = [
        pltpu.make_async_copy(source, target, sems.at[i])
        for i, (source, target) in enumerate(
            ((decay_far, decay_ref), (key_far, key_ref), (value_far, value_ref))
        )
    ]
    for copy in copies:
        copy.start()
    copies[0].wait()
    tall, wide = decays(decay_ref[...])
    tall_ref[...] = tall
    wide_ref[...] = wide
    total = tall[-1:, :]
    trailing = jnp.exp(total - tall)
    copies[1].wait()
    copies[2].wait()
    for head in range(heads):
        here = cols(head, size)
        key, value = key_ref[:, here], value_ref[:, here]
        state = product(key.astype(f32) * trailing[:, head : head + 1], value, TN)
        mark = jnp.broadcast_to(total[:, head : head + 1], (8, size))
        first = turned(head, heads) * per
        for part in range(per):
            out_ref[first + part, :rows, :] = state[part * rows : (part + 1) * rows, :]
            out_ref[first + part, rows:, :] = mark


def times(gain, state):
    return (gain[None] * state.reshape(-1, 8, state.shape[-1])).reshape(state.shape)


def group_kernel(members, copies, rows, piece_ref, out_ref):
    _, _, cut = whereabouts(members // 2)
    total = jnp.zeros((rows, piece_ref.shape[-1]), f32)
    whole = jnp.zeros((8, piece_ref.shape[-1]), f32)
    early = total
    for member in range(members):
        if member == members // 2:
            early = total
        place = rank(member, cut)
        mark = piece_ref[place, rows:, :]
        total = times(jnp.exp(mark), total) + piece_ref[place, :rows, :]
        whole = whole + mark
    total = jnp.where(cut, early, total)
    for copy in range(copies):
        out_ref[copy, :rows, :] = total
        out_ref[copy, rows:, :] = whole


def spread_kernel(members, groups, rows, piece_ref, total_ref, out_ref, near_ref, far_ref):
    mine, shift, cut = whereabouts(members // 2)
    first = jnp.where(shift > 0, groups - 1, 0)
    before = jnp.where(cut, 0, mine + jnp.where(shift > 0, 1, 0))
    every = jnp.zeros((rows, piece_ref.shape[-1]), f32)
    running = every
    for step in range(groups):
        group = (step + first) & (groups - 1)
        gain = jnp.exp(total_ref[group, rows:, :])
        far_ref[group] = gain
        every = times(gain, every) + total_ref[group, :rows, :]
        running = jnp.where(step < before, every, running)
    for member in range(members):
        if member == members // 2:
            running = jnp.where(cut, every, running)
        place = rank(member, cut)
        gain = jnp.exp(piece_ref[place, rows:, :])
        near_ref[place] = gain
        out_ref[place] = running
        running = times(gain, running) + piece_ref[place, :rows, :]


def back_group_kernel(members, copies, piece_ref, near_ref, out_ref):
    _, _, cut = whereabouts(members // 2)
    total = jnp.zeros(piece_ref.shape[1:], f32)
    late = total
    for member in reversed(range(members)):
        place = rank(member, cut)
        total = times(near_ref[place], total) + piece_ref[place]
        if member == members // 2:
            late = total
    total = jnp.where(cut, late, total)
    for copy in range(copies):
        out_ref[copy] = total


def back_spread_kernel(members, groups, piece_ref, near_ref, total_ref, far_ref, out_ref):
    mine, _, cut = whereabouts(members // 2)
    every = jnp.zeros(piece_ref.shape[1:], f32)
    running = every
    for group in reversed(range(groups)):
        every = times(far_ref[group], every) + total_ref[group]
        running = jnp.where(group > mine, every, running)
    for member in reversed(range(members)):
        place = rank(member, cut)
        out_ref[place] = running
        running = times(near_ref[place], running) + piece_ref[place]
        if member == members // 2:
            running = jnp.where(cut, every, running)


def inside_kernel(heads, query_ref, key_ref, value_ref, tall_ref, wide_ref, out_ref):
    size = key_ref.shape[1] // heads
    tall, wide = tall_ref[...], wide_ref[...]
    for head in range(heads):
        here = cols(head, size)
        scores = product(query_ref[:, here], key_ref[:, here], NT) * weights_of(tall, wide, head)
        out_ref[:, here] = product(scores, value_ref[:, here], NN)


def mixed_kernel(
    heads, query_ref, tall_ref, inside_ref, state_ref, gain_ref, grad_ref, out_ref, sums_ref
):
    size = query_ref.shape[1] // heads
    rows = query_ref.shape[0]
    rising = jnp.exp(tall_ref[...])
    squares = jnp.zeros((rows, size), f32)
    products = jnp.zeros((rows, size), f32)
    for head in range(heads):
        here = cols(head, size)
        outside = product(query_ref[:, here], state_ref[turned(head, heads)], NN)
        mixed = inside_ref[:, here] + outside * rising[:, head : head + 1]
        out_ref[:, here] = mixed
        squares = squares + mixed * mixed
        products = products + grad_ref[:, here].astype(f32) * gain_ref[:, here] * mixed
    ones = jnp.ones((8, size), f32)
    square = lax.dot_general(ones, squares, NT, precision=highest, preferred_element_type=f32)
    product_ = lax.dot_general(ones, products, NT, precision=highest, preferred_element_type=f32)
    sums_ref[0:1, :] = square[0:1, :]
    sums_ref[1:2, :] = product_[0:1, :]


def row_factors(full_width, size, sums_ref):
    ones = jnp.ones((sums_ref.shape[0], size), f32)
    square = lax.dot_general(sums_ref[:, 0, :], ones, TN, precision=highest, preferred_element_type=f32)
    product_ = lax.dot_general(sums_ref[:, 1, :], ones, TN, precision=highest, preferred_element_type=f32)
    scale = lax.rsqrt(square / full_width + epsilon)
    return scale, scale * scale * scale * (product_ / full_width)


def back_kernel(
    heads, members, full_width, query_ref, tall_ref, mixed_ref, gain_ref, grad_ref, sums_ref, out_ref
):
    size = query_ref.shape[1] // heads
    per = members // heads
    cut = size // per
    rising = jnp.exp(tall_ref[...])
    scale, pull = row_factors(full_width, size, sums_ref)
    for head in range(heads):
        here = cols(head, size)
        slope = scale * (grad_ref[:, here].astype(f32) * gain_ref[:, here]) - pull * mixed_ref[:, here]
        state = product(query_ref[:, here], slope * rising[:, head : head + 1], TN)
        first = turned(head, heads) * per
        for part in range(per):
            out_ref[first + part] = state[part * cut : (part + 1) * cut, :]


def near_kernel(
    heads,
    full_width,
    query_ref,
    key_ref,
    value_ref,
    tall_ref,
    wide_ref,
    state_ref,
    mixed_ref,
    gain_ref,
    grad_ref,
    sums_ref,
    normed_ref,
    grad_q_ref,
    near_k_ref,
    near_v_ref,
):
    size = key_ref.shape[1] // heads
    tall, wide = tall_ref[...], wide_ref[...]
    rising = jnp.exp(tall)
    scale, pull = row_factors(full_width, size, sums_ref)
    for head in range(heads):
        here = cols(head, size)
        query, key, value = query_ref[:, here], key_ref[:, here], value_ref[:, here]
        gain, mixed = gain_ref[:, here], mixed_ref[:, here]
        normed_ref[:, here] = (mixed * scale * gain).astype(bf16)
        slope = scale * (grad_ref[:, here].astype(f32) * gain) - pull * mixed
        weights = weights_of(tall, wide, head)
        scores = product(query, key, NT, True) * weights
        grad_scores = product(slope, value, NT, True) * weights
        there = turned(head, heads)
        outer = product(slope, state_ref[there], NT, True) * rising[:, head : head + 1]
        grad_q_ref[:, here] = (product(grad_scores, key, NN, True) + outer).astype(bf16)
        near_k_ref[there] = product(grad_scores, query, TN, True)
        near_v_ref[:, here] = product(scores, slope, TN, True)


def far_kernel(heads, key_ref, value_ref, tall_ref, state_ref, near_k_ref, near_v_ref, grad_k_ref, grad_v_ref):
    size = key_ref.shape[1] // heads
    tall = tall_ref[...]
    trailing = jnp.exp(tall[-1:, :] - tall)
    for head in range(heads):
        here = cols(head, size)
        late = trailing[:, head : head + 1]
        there = turned(head, heads)
        state = state_ref[there]
        grad_k = near_k_ref[there] + product(value_ref[:, here], state, NT, True) * late
        grad_v = near_v_ref[:, here] + product(key_ref[:, here], state, NN, True) * late
        grad_k_ref[:, here] = grad_k.astype(bf16)
        grad_v_ref[:, here] = grad_v.astype(bf16)


def call(kernel, outs, *args, flops=0, copied=(), aliases=None):
    vmem = pl.BlockSpec(memory_space=pltpu.VMEM)
    hbm = pl.BlockSpec(memory_space=pltpu.HBM)
    if copied:
        args = [pltpu.with_memory_space_constraint(a, pltpu.HBM) for a in args]
    moved = sum(a.size * a.dtype.itemsize for a in (*args, *outs))
    return pl.pallas_call(
        kernel,
        out_shape=outs,
        in_specs=[hbm if copied else vmem] * len(args),
        out_specs=[vmem] * len(outs),
        input_output_aliases=aliases or {},
        scratch_shapes=[pltpu.VMEM(a.shape, a.dtype) for a in copied]
        + ([pltpu.SemaphoreType.DMA((len(copied),))] if copied else []),
        cost_estimate=pl.CostEstimate(flops=flops, bytes_accessed=moved, transcendentals=0),
        compiler_params=pltpu.CompilerParams(vmem_limit_bytes=12 * 1024 * 1024),
    )(*args)


def levels(count, tp, heads):
    members = 2 * heads
    span = members // 4
    groups = count // members
    near, far = [], []
    for index in range(tp):
        shift = index % 2 * (span // 2)

        def device(group, place):
            z = (group * span + shift + place % 4) % (count // 4)
            return (z * 4 + place // 4) * tp + index

        for group in range(groups):
            near.append([device(group, place) for place in range(members)])
        for piece in range(members):
            far.append(
                [device(group, piece ^ (2 if group >= groups // 2 else 0)) for group in range(groups)]
            )
    return groups, members, near, far


def shards(queries, key_rows, value_rows, log_decay, norm_gain, grad_output):
    tok_rows, feat_width = queries.shape
    heads = log_decay.shape[1]
    groups, members, near, far = levels(lax.axis_size("ctx"), lax.axis_size("tp"), heads)
    size = feat_width // heads
    rows = heads * size // members
    wide = jax.ShapeDtypeStruct((tok_rows, feat_width), f32)
    narrow = jax.ShapeDtypeStruct((tok_rows, feat_width), bf16)
    gain = norm_gain.reshape(1, feat_width)
    log_decay = log_decay.T
    bind = functools.partial
    shape = jax.ShapeDtypeStruct
    unit = 2 * heads * tok_rows * size * size

    def exchange(parts, lists):
        return lax.all_to_all(parts, ("ctx", "tp"), 0, 0, axis_index_groups=lists)

    states, tall, across = call(
        bind(states_kernel, heads, members),
        [shape((members, rows + 8, size), f32), shape((tok_rows, heads), f32), shape((heads, tok_rows), f32)],
        key_rows,
        value_rows,
        log_decay,
        flops=2 * unit,
        copied=(key_rows, value_rows, log_decay),
    )
    pieces = exchange(states, near)
    (total,) = call(
        bind(group_kernel, members, groups, rows), [shape((groups, rows + 8, size), f32)], pieces
    )
    (inside,) = call(
        bind(inside_kernel, heads), [wide], queries, key_rows, value_rows, tall, across, flops=3 * unit
    )
    entering, near_gains, far_gains = call(
        bind(spread_kernel, members, groups, rows),
        [shape((members, rows, size), f32), shape((members, 8, size), f32), shape((groups, 8, size), f32)],
        pieces,
        exchange(total, far),
    )
    entry = exchange(entering, near).reshape(heads, size, size)
    mixed, sums = call(
        bind(mixed_kernel, heads),
        [wide, shape((2, tok_rows), f32)],
        queries,
        tall,
        inside,
        entry,
        gain,
        grad_output,
        flops=2 * unit,
    )
    gathered = lax.all_gather(sums, "tp")
    full_width = feat_width * lax.axis_size("tp")
    (back,) = call(
        bind(back_kernel, heads, members, full_width),
        [shape((members, rows, size), f32)],
        queries,
        tall,
        mixed,
        gain,
        grad_output,
        gathered,
        flops=2 * unit,
    )
    back_pieces = exchange(back, near)
    (back_total,) = call(
        bind(back_group_kernel, members, groups),
        [shape((groups, rows, size), f32)],
        back_pieces,
        near_gains,
    )
    (returning,) = call(
        bind(back_spread_kernel, members, groups),
        [shape((members, rows, size), f32)],
        back_pieces,
        near_gains,
        exchange(back_total, far),
        far_gains,
    )
    leaving = exchange(returning, near).reshape(heads, size, size)
    normed, grad_q, near_k, near_v = call(
        bind(near_kernel, heads, full_width),
        [narrow, narrow, shape((heads, size, size), f32), wide],
        queries,
        key_rows,
        value_rows,
        tall,
        across,
        entry,
        mixed,
        gain,
        grad_output,
        gathered,
        flops=13 * unit,
        aliases={5: 2, 6: 3},
    )
    grad_k, grad_v = call(
        bind(far_kernel, heads),
        [narrow, narrow],
        key_rows,
        value_rows,
        tall,
        leaving,
        near_k,
        near_v,
        flops=4 * unit,
    )
    return normed, grad_q, grad_k, grad_v


def solution(mesh):
    both = P("ctx", "tp")
    return jax.shard_map(
        shards,
        mesh=mesh,
        in_specs=(both, both, both, both, P("tp"), both),
        out_specs=(both, both, both, both),
        check_vma=False,
    )
```

```python
import functools

import jax
import jax.numpy as jnp
from jax import lax
from jax.experimental import pallas as pl
from jax.experimental.pallas import tpu as pltpu
from jax.sharding import PartitionSpec as P

epsilon = 1e-06
highest = lax.Precision.HIGHEST
f32 = jnp.float32
bf16 = jnp.bfloat16

NN = (((1,), (0,)), ((), ()))
NT = (((1,), (1,)), ((), ()))
TN = (((0,), (0,)), ((), ()))


def halves(wide):
    high = wide.astype(bf16)
    return high, (wide - high.astype(f32)).astype(bf16)


def product(left, right, dims, deep=False):
    (left_axes, right_axes), _ = dims
    lefts = halves(left) if left.dtype == f32 else (left,)
    rights = halves(right) if right.dtype == f32 else (right,)
    pairs = [(a, b) for i, a in enumerate(lefts) for j, b in enumerate(rights) if i + j < 2]
    if deep and len(pairs) > 1:
        left = jnp.concatenate([a for a, _ in pairs], axis=left_axes[0])
        right = jnp.concatenate([b for _, b in pairs], axis=right_axes[0])
        pairs = [(left, right)]
    total = None
    for a, b in pairs:
        term = lax.dot_general(a, b, dims, preferred_element_type=f32)
        total = term if total is None else total + term
    return total


def decays(log_decay):
    rows = log_decay.shape[1]
    above = lax.broadcasted_iota(jnp.int32, (rows, rows), 0)
    along = lax.broadcasted_iota(jnp.int32, (rows, rows), 1)
    upper = (above <= along).astype(f32)
    lower = (above >= along).astype(f32)
    tall = lax.dot_general(lower, log_decay, NT, precision=highest, preferred_element_type=f32)
    wide = lax.dot_general(log_decay, upper, NN, precision=highest, preferred_element_type=f32)
    return tall, wide


def weights_of(tall, wide, head):
    rows = tall.shape[0]
    above = lax.broadcasted_iota(jnp.int32, (rows, rows), 0)
    along = lax.broadcasted_iota(jnp.int32, (rows, rows), 1)
    mask = above >= along
    differences = tall[:, head : head + 1] - wide[head : head + 1, :]
    return jnp.where(mask, jnp.exp(jnp.where(mask, differences, 0.0)), 0.0)


def whereabouts(heads):
    span = 2 * heads // 4
    z_rows = lax.axis_size("ctx") // 4
    shift = (lax.axis_index("tp") & 1) * (span // 2)
    group = lax.div((lax.div(lax.axis_index("ctx"), 4) - shift) & (z_rows - 1), span)
    cut = jnp.logical_and(shift > 0, group == z_rows // span - 1)
    return group, shift, cut


def turned(head, heads):
    half = lax.axis_size("ctx") // (2 * heads) // 2
    return head ^ jnp.where(whereabouts(heads)[0] < half, 0, 1)


def rank(member, cut):
    return member % 4 * 4 + ((member // 4) ^ jnp.where(cut, 2, 0))


def cols(head, size):
    return slice(head * size, (head + 1) * size)


def states_kernel(
    heads, members, key_far, value_far, decay_far, out_ref, tall_ref, wide_ref, key_ref, value_ref, decay_ref, sems
):
    size = key_ref.shape[1] // heads
    per = members // heads
    rows = size // per
    copies = [
        pltpu.make_async_copy(source, target, sems.at[i])
        for i, (source, target) in enumerate(
            ((decay_far, decay_ref), (key_far, key_ref), (value_far, value_ref))
        )
    ]
    for copy in copies:
        copy.start()
    copies[0].wait()
    tall, wide = decays(decay_ref[...])
    tall_ref[...] = tall
    wide_ref[...] = wide
    total = tall[-1:, :]
    trailing = jnp.exp(total - tall)
    copies[1].wait()
    copies[2].wait()
    for head in range(heads):
        here = cols(head, size)
        key, value = key_ref[:, here], value_ref[:, here]
        state = product(key.astype(f32) * trailing[:, head : head + 1], value, TN)
        mark = jnp.broadcast_to(total[:, head : head + 1], (8, size))
        first = turned(head, heads) * per
        for part in range(per):
            out_ref[first + part, :rows, :] = state[part * rows : (part + 1) * rows, :]
            out_ref[first + part, rows:, :] = mark


def times(gain, state):
    return (gain[None] * state.reshape(-1, 8, state.shape[-1])).reshape(state.shape)


def group_kernel(members, copies, rows, piece_ref, out_ref):
    _, _, cut = whereabouts(members // 2)
    total = jnp.zeros((rows, piece_ref.shape[-1]), f32)
    whole = jnp.zeros((8, piece_ref.shape[-1]), f32)
    early = total
    for member in range(members):
        if member == members // 2:
            early = total
        place = rank(member, cut)
        mark = piece_ref[place, rows:, :]
        total = times(jnp.exp(mark), total) + piece_ref[place, :rows, :]
        whole = whole + mark
    total = jnp.where(cut, early, total)
    for copy in range(copies):
        out_ref[copy, :rows, :] = total
        out_ref[copy, rows:, :] = whole


def spread_kernel(members, groups, rows, piece_ref, total_ref, out_ref, near_ref, far_ref):
    mine, shift, cut = whereabouts(members // 2)
    first = jnp.where(shift > 0, groups - 1, 0)
    before = jnp.where(cut, 0, mine + jnp.where(shift > 0, 1, 0))
    every = jnp.zeros((rows, piece_ref.shape[-1]), f32)
    running = every
    for step in range(groups):
        group = (step + first) & (groups - 1)
        gain = jnp.exp(total_ref[group, rows:, :])
        far_ref[group] = gain
        every = times(gain, every) + total_ref[group, :rows, :]
        running = jnp.where(step < before, every, running)
    for member in range(members):
        if member == members // 2:
            running = jnp.where(cut, every, running)
        place = rank(member, cut)
        gain = jnp.exp(piece_ref[place, rows:, :])
        near_ref[place] = gain
        out_ref[place] = running
        running = times(gain, running) + piece_ref[place, :rows, :]


def back_group_kernel(members, copies, piece_ref, near_ref, out_ref):
    _, _, cut = whereabouts(members // 2)
    total = jnp.zeros(piece_ref.shape[1:], f32)
    late = total
    for member in reversed(range(members)):
        place = rank(member, cut)
        total = times(near_ref[place], total) + piece_ref[place]
        if member == members // 2:
            late = total
    total = jnp.where(cut, late, total)
    for copy in range(copies):
        out_ref[copy] = total


def back_spread_kernel(members, groups, piece_ref, near_ref, total_ref, far_ref, out_ref):
    mine, _, cut = whereabouts(members // 2)
    every = jnp.zeros(piece_ref.shape[1:], f32)
    running = every
    for group in reversed(range(groups)):
        every = times(far_ref[group], every) + total_ref[group]
        running = jnp.where(group > mine, every, running)
    for member in reversed(range(members)):
        place = rank(member, cut)
        out_ref[place] = running
        running = times(near_ref[place], running) + piece_ref[place]
        if member == members // 2:
            running = jnp.where(cut, every, running)


def inside_kernel(heads, query_ref, key_ref, value_ref, tall_ref, wide_ref, out_ref):
    size = key_ref.shape[1] // heads
    tall, wide = tall_ref[...], wide_ref[...]
    for head in range(heads):
        here = cols(head, size)
        scores = product(query_ref[:, here], key_ref[:, here], NT) * weights_of(tall, wide, head)
        out_ref[:, here] = product(scores, value_ref[:, here], NN)


def mixed_kernel(
    heads, query_ref, tall_ref, inside_ref, state_ref, gain_ref, grad_ref, out_ref, sums_ref
):
    size = query_ref.shape[1] // heads
    rows = query_ref.shape[0]
    rising = jnp.exp(tall_ref[...])
    squares = jnp.zeros((rows, size), f32)
    products = jnp.zeros((rows, size), f32)
    for head in range(heads):
        here = cols(head, size)
        outside = product(query_ref[:, here], state_ref[turned(head, heads)], NN)
        mixed = inside_ref[:, here] + outside * rising[:, head : head + 1]
        out_ref[:, here] = mixed
        squares = squares + mixed * mixed
        products = products + grad_ref[:, here].astype(f32) * gain_ref[:, here] * mixed
    ones = jnp.ones((8, size), f32)
    square = lax.dot_general(ones, squares, NT, precision=highest, preferred_element_type=f32)
    product_ = lax.dot_general(ones, products, NT, precision=highest, preferred_element_type=f32)
    for copy in range(sums_ref.shape[0]):
        sums_ref[copy, 0:1, :] = square[0:1, :]
        sums_ref[copy, 1:2, :] = product_[0:1, :]


def row_factors(full_width, size, sums_ref):
    ones = jnp.ones((sums_ref.shape[0], size), f32)
    square = lax.dot_general(sums_ref[:, 0, :], ones, TN, precision=highest, preferred_element_type=f32)
    product_ = lax.dot_general(sums_ref[:, 1, :], ones, TN, precision=highest, preferred_element_type=f32)
    scale = lax.rsqrt(square / full_width + epsilon)
    return scale, scale * scale * scale * (product_ / full_width)


def back_kernel(
    heads, members, full_width, query_ref, tall_ref, mixed_ref, gain_ref, grad_ref, sums_ref, out_ref
):
    size = query_ref.shape[1] // heads
    per = members // heads
    cut = size // per
    rising = jnp.exp(tall_ref[...])
    scale, pull = row_factors(full_width, size, sums_ref)
    for head in range(heads):
        here = cols(head, size)
        slope = scale * (grad_ref[:, here].astype(f32) * gain_ref[:, here]) - pull * mixed_ref[:, here]
        state = product(query_ref[:, here], slope * rising[:, head : head + 1], TN)
        first = turned(head, heads) * per
        for part in range(per):
            out_ref[first + part] = state[part * cut : (part + 1) * cut, :]


def near_kernel(
    heads,
    full_width,
    query_ref,
    key_ref,
    value_ref,
    tall_ref,
    wide_ref,
    state_ref,
    mixed_ref,
    gain_ref,
    grad_ref,
    sums_ref,
    normed_ref,
    grad_q_ref,
    near_k_ref,
    near_v_ref,
):
    size = key_ref.shape[1] // heads
    tall, wide = tall_ref[...], wide_ref[...]
    rising = jnp.exp(tall)
    scale, pull = row_factors(full_width, size, sums_ref)
    for head in range(heads):
        here = cols(head, size)
        query, key, value = query_ref[:, here], key_ref[:, here], value_ref[:, here]
        gain, mixed = gain_ref[:, here], mixed_ref[:, here]
        normed_ref[:, here] = (mixed * scale * gain).astype(bf16)
        slope = scale * (grad_ref[:, here].astype(f32) * gain) - pull * mixed
        weights = weights_of(tall, wide, head)
        scores = product(query, key, NT, True) * weights
        grad_scores = product(slope, value, NT, True) * weights
        there = turned(head, heads)
        outer = product(slope, state_ref[there], NT, True) * rising[:, head : head + 1]
        grad_q_ref[:, here] = (product(grad_scores, key, NN, True) + outer).astype(bf16)
        near_k_ref[there] = product(grad_scores, query, TN, True)
        near_v_ref[:, here] = product(scores, slope, TN, True)


def far_kernel(heads, key_ref, value_ref, tall_ref, state_ref, near_k_ref, near_v_ref, grad_k_ref, grad_v_ref):
    size = key_ref.shape[1] // heads
    tall = tall_ref[...]
    trailing = jnp.exp(tall[-1:, :] - tall)
    for head in range(heads):
        here = cols(head, size)
        late = trailing[:, head : head + 1]
        there = turned(head, heads)
        state = state_ref[there]
        grad_k = near_k_ref[there] + product(value_ref[:, here], state, NT, True) * late
        grad_v = near_v_ref[:, here] + product(key_ref[:, here], state, NN, True) * late
        grad_k_ref[:, here] = grad_k.astype(bf16)
        grad_v_ref[:, here] = grad_v.astype(bf16)


def call(kernel, outs, *args, flops=0, copied=(), aliases=None):
    vmem = pl.BlockSpec(memory_space=pltpu.VMEM)
    hbm = pl.BlockSpec(memory_space=pltpu.HBM)
    if copied:
        args = [pltpu.with_memory_space_constraint(a, pltpu.HBM) for a in args]
    moved = sum(a.size * a.dtype.itemsize for a in (*args, *outs))
    return pl.pallas_call(
        kernel,
        out_shape=outs,
        in_specs=[hbm if copied else vmem] * len(args),
        out_specs=[vmem] * len(outs),
        input_output_aliases=aliases or {},
        scratch_shapes=[pltpu.VMEM(a.shape, a.dtype) for a in copied]
        + ([pltpu.SemaphoreType.DMA((len(copied),))] if copied else []),
        cost_estimate=pl.CostEstimate(flops=flops, bytes_accessed=moved, transcendentals=0),
        compiler_params=pltpu.CompilerParams(vmem_limit_bytes=12 * 1024 * 1024),
    )(*args)


def levels(count, tp, heads):
    members = 2 * heads
    span = members // 4
    groups = count // members
    near, far = [], []
    for index in range(tp):
        shift = index % 2 * (span // 2)

        def device(group, place):
            z = (group * span + shift + place % 4) % (count // 4)
            return (z * 4 + place // 4) * tp + index

        for group in range(groups):
            near.append([device(group, place) for place in range(members)])
        for piece in range(members):
            far.append(
                [device(group, piece ^ (2 if group >= groups // 2 else 0)) for group in range(groups)]
            )
    return groups, members, near, far


def shards(queries, key_rows, value_rows, log_decay, norm_gain, grad_output):
    tok_rows, feat_width = queries.shape
    heads = log_decay.shape[1]
    groups, members, near, far = levels(lax.axis_size("ctx"), lax.axis_size("tp"), heads)
    size = feat_width // heads
    rows = heads * size // members
    wide = jax.ShapeDtypeStruct((tok_rows, feat_width), f32)
    narrow = jax.ShapeDtypeStruct((tok_rows, feat_width), bf16)
    gain = norm_gain.reshape(1, feat_width)
    log_decay = log_decay.T
    bind = functools.partial
    shape = jax.ShapeDtypeStruct
    unit = 2 * heads * tok_rows * size * size

    def exchange(parts, lists):
        return lax.all_to_all(parts, ("ctx", "tp"), 0, 0, axis_index_groups=lists)

    states, tall, across = call(
        bind(states_kernel, heads, members),
        [shape((members, rows + 8, size), f32), shape((tok_rows, heads), f32), shape((heads, tok_rows), f32)],
        key_rows,
        value_rows,
        log_decay,
        flops=2 * unit,
        copied=(key_rows, value_rows, log_decay),
    )
    pieces = exchange(states, near)
    (total,) = call(
        bind(group_kernel, members, groups, rows), [shape((groups, rows + 8, size), f32)], pieces
    )
    (inside,) = call(
        bind(inside_kernel, heads), [wide], queries, key_rows, value_rows, tall, across, flops=3 * unit
    )
    entering, near_gains, far_gains = call(
        bind(spread_kernel, members, groups, rows),
        [shape((members, rows, size), f32), shape((members, 8, size), f32), shape((groups, 8, size), f32)],
        pieces,
        exchange(total, far),
    )
    entry = exchange(entering, near).reshape(heads, size, size)
    mixed, sums = call(
        bind(mixed_kernel, heads),
        [wide, shape((lax.axis_size("tp"), 2, tok_rows), f32)],
        queries,
        tall,
        inside,
        entry,
        gain,
        grad_output,
        flops=2 * unit,
    )
    gathered = lax.all_to_all(sums, "tp", 0, 0)
    full_width = feat_width * lax.axis_size("tp")
    (back,) = call(
        bind(back_kernel, heads, members, full_width),
        [shape((members, rows, size), f32)],
        queries,
        tall,
        mixed,
        gain,
        grad_output,
        gathered,
        flops=2 * unit,
    )
    back_pieces = exchange(back, near)
    (back_total,) = call(
        bind(back_group_kernel, members, groups),
        [shape((groups, rows, size), f32)],
        back_pieces,
        near_gains,
    )
    (returning,) = call(
        bind(back_spread_kernel, members, groups),
        [shape((members, rows, size), f32)],
        back_pieces,
        near_gains,
        exchange(back_total, far),
        far_gains,
    )
    leaving = exchange(returning, near).reshape(heads, size, size)
    normed, grad_q, near_k, near_v = call(
        bind(near_kernel, heads, full_width),
        [narrow, narrow, shape((heads, size, size), f32), wide],
        queries,
        key_rows,
        value_rows,
        tall,
        across,
        entry,
        mixed,
        gain,
        grad_output,
        gathered,
        flops=13 * unit,
        aliases={5: 2, 6: 3},
    )
    grad_k, grad_v = call(
        bind(far_kernel, heads),
        [narrow, narrow],
        key_rows,
        value_rows,
        tall,
        leaving,
        near_k,
        near_v,
        flops=4 * unit,
    )
    return normed, grad_q, grad_k, grad_v


def solution(mesh):
    both = P("ctx", "tp")
    return jax.shard_map(
        shards,
        mesh=mesh,
        in_specs=(both, both, both, both, P("tp"), both),
        out_specs=(both, both, both, both),
        check_vma=False,
    )
```

```python
import functools

import jax
import jax.numpy as jnp
from jax import lax
from jax.experimental import pallas as pl
from jax.experimental.pallas import tpu as pltpu
from jax.sharding import PartitionSpec as P

epsilon = 1e-06
highest = lax.Precision.HIGHEST
f32 = jnp.float32
bf16 = jnp.bfloat16

NN = (((1,), (0,)), ((), ()))
NT = (((1,), (1,)), ((), ()))
TN = (((0,), (0,)), ((), ()))


def halves(wide):
    high = wide.astype(bf16)
    return high, (wide - high.astype(f32)).astype(bf16)


def product(left, right, dims, deep=False):
    (left_axes, right_axes), _ = dims
    lefts = halves(left) if left.dtype == f32 else (left,)
    rights = halves(right) if right.dtype == f32 else (right,)
    pairs = [(a, b) for i, a in enumerate(lefts) for j, b in enumerate(rights) if i + j < 2]
    if deep and len(pairs) > 1:
        left = jnp.concatenate([a for a, _ in pairs], axis=left_axes[0])
        right = jnp.concatenate([b for _, b in pairs], axis=right_axes[0])
        pairs = [(left, right)]
    total = None
    for a, b in pairs:
        term = lax.dot_general(a, b, dims, preferred_element_type=f32)
        total = term if total is None else total + term
    return total


def decays(log_decay):
    rows = log_decay.shape[1]
    above = lax.broadcasted_iota(jnp.int32, (rows, rows), 0)
    along = lax.broadcasted_iota(jnp.int32, (rows, rows), 1)
    upper = (above <= along).astype(f32)
    lower = (above >= along).astype(f32)
    tall = lax.dot_general(lower, log_decay, NT, precision=highest, preferred_element_type=f32)
    wide = lax.dot_general(log_decay, upper, NN, precision=highest, preferred_element_type=f32)
    return tall, wide


def weights_of(tall, wide, head):
    rows = tall.shape[0]
    above = lax.broadcasted_iota(jnp.int32, (rows, rows), 0)
    along = lax.broadcasted_iota(jnp.int32, (rows, rows), 1)
    mask = above >= along
    differences = tall[:, head : head + 1] - wide[head : head + 1, :]
    return jnp.where(mask, jnp.exp(jnp.where(mask, differences, 0.0)), 0.0)


def whereabouts(heads):
    span = 2 * heads // 4
    z_rows = lax.axis_size("ctx") // 4
    shift = (lax.axis_index("tp") & 1) * (span // 2)
    group = lax.div((lax.div(lax.axis_index("ctx"), 4) - shift) & (z_rows - 1), span)
    cut = jnp.logical_and(shift > 0, group == z_rows // span - 1)
    return group, shift, cut


def turned(head, heads):
    group, _, _ = whereabouts(heads)
    half = lax.axis_size("ctx") // (2 * heads) // 2
    return head ^ jnp.where(group < half, 0, 4)


def rank(member, shift, cut):
    x, z = member % 4, (member // 4) ^ jnp.where(cut, 2, 0)
    return z * 4 + x


def cols(head, size):
    return slice(head * size, (head + 1) * size)


def states_kernel(
    heads, members, key_far, value_far, decay_far, out_ref, tall_ref, wide_ref, key_ref, value_ref, decay_ref, sems
):
    size = key_ref.shape[1] // heads
    per = members // heads
    rows = size // per
    copies = [
        pltpu.make_async_copy(source, target, sems.at[i])
        for i, (source, target) in enumerate(
            ((decay_far, decay_ref), (key_far, key_ref), (value_far, value_ref))
        )
    ]
    for copy in copies:
        copy.start()
    copies[0].wait()
    tall, wide = decays(decay_ref[...])
    tall_ref[...] = tall
    wide_ref[...] = wide
    total = tall[-1:, :]
    trailing = jnp.exp(total - tall)
    copies[1].wait()
    copies[2].wait()
    for head in range(heads):
        here = cols(head, size)
        key, value = key_ref[:, here], value_ref[:, here]
        state = product(key.astype(f32) * trailing[:, head : head + 1], value, TN)
        mark = jnp.broadcast_to(total[:, head : head + 1], (8, size))
        first = turned(head, heads) * per
        for part in range(per):
            out_ref[first + part, :rows, :] = state[part * rows : (part + 1) * rows, :]
            out_ref[first + part, rows:, :] = mark


def times(gain, state):
    return (gain[None] * state.reshape(-1, 8, state.shape[-1])).reshape(state.shape)


def group_kernel(members, copies, rows, piece_ref, out_ref):
    _, shift, cut = whereabouts(members // 2)
    total = jnp.zeros((rows, piece_ref.shape[-1]), f32)
    whole = jnp.zeros((8, piece_ref.shape[-1]), f32)
    early = total
    for member in range(members):
        if member == members // 2:
            early = total
        place = rank(member, shift, cut)
        mark = piece_ref[place, rows:, :]
        total = times(jnp.exp(mark), total) + piece_ref[place, :rows, :]
        whole = whole + mark
    total = jnp.where(cut, early, total)
    for copy in range(copies):
        out_ref[copy, :rows, :] = total
        out_ref[copy, rows:, :] = whole


def spread_kernel(members, groups, rows, piece_ref, total_ref, out_ref, near_ref, far_ref):
    mine, shift, cut = whereabouts(members // 2)
    first = jnp.where(shift > 0, groups - 1, 0)
    before = jnp.where(cut, 0, mine + jnp.where(shift > 0, 1, 0))
    every = jnp.zeros((rows, piece_ref.shape[-1]), f32)
    running = every
    for step in range(groups):
        group = (step + first) & (groups - 1)
        gain = jnp.exp(total_ref[group, rows:, :])
        far_ref[group] = gain
        every = times(gain, every) + total_ref[group, :rows, :]
        running = jnp.where(step < before, every, running)
    for member in range(members):
        if member == members // 2:
            running = jnp.where(cut, every, running)
        place = rank(member, shift, cut)
        gain = jnp.exp(piece_ref[place, rows:, :])
        near_ref[place] = gain
        out_ref[place] = running
        running = times(gain, running) + piece_ref[place, :rows, :]


def back_group_kernel(members, copies, piece_ref, near_ref, out_ref):
    _, shift, cut = whereabouts(members // 2)
    total = jnp.zeros(piece_ref.shape[1:], f32)
    late = total
    for member in reversed(range(members)):
        place = rank(member, shift, cut)
        total = times(near_ref[place], total) + piece_ref[place]
        if member == members // 2:
            late = total
    total = jnp.where(cut, late, total)
    for copy in range(copies):
        out_ref[copy] = total


def back_spread_kernel(members, groups, piece_ref, near_ref, total_ref, far_ref, out_ref):
    mine, shift, cut = whereabouts(members // 2)
    every = jnp.zeros(piece_ref.shape[1:], f32)
    running = every
    for group in reversed(range(groups)):
        every = times(far_ref[group], every) + total_ref[group]
        running = jnp.where(group > mine, every, running)
    for member in reversed(range(members)):
        place = rank(member, shift, cut)
        out_ref[place] = running
        running = times(near_ref[place], running) + piece_ref[place]
        if member == members // 2:
            running = jnp.where(cut, every, running)


def inside_kernel(heads, query_ref, key_ref, value_ref, tall_ref, wide_ref, out_ref):
    size = key_ref.shape[1] // heads
    tall, wide = tall_ref[...], wide_ref[...]
    for head in range(heads):
        here = cols(head, size)
        scores = product(query_ref[:, here], key_ref[:, here], NT) * weights_of(tall, wide, head)
        out_ref[:, here] = product(scores, value_ref[:, here], NN)


def mixed_kernel(
    heads, query_ref, tall_ref, inside_ref, state_ref, gain_ref, grad_ref, out_ref, sums_ref
):
    size = query_ref.shape[1] // heads
    rows = query_ref.shape[0]
    rising = jnp.exp(tall_ref[...])
    squares = jnp.zeros((rows, size), f32)
    products = jnp.zeros((rows, size), f32)
    for head in range(heads):
        here = cols(head, size)
        outside = product(query_ref[:, here], state_ref[turned(head, heads)], NN)
        mixed = inside_ref[:, here] + outside * rising[:, head : head + 1]
        out_ref[:, here] = mixed
        squares = squares + mixed * mixed
        products = products + grad_ref[:, here].astype(f32) * gain_ref[:, here] * mixed
    ones = jnp.ones((8, size), f32)
    square = lax.dot_general(ones, squares, NT, precision=highest, preferred_element_type=f32)
    product_ = lax.dot_general(ones, products, NT, precision=highest, preferred_element_type=f32)
    for copy in range(sums_ref.shape[0]):
        sums_ref[copy, 0:1, :] = square[0:1, :]
        sums_ref[copy, 1:2, :] = product_[0:1, :]


def row_factors(full_width, size, sums_ref):
    ones = jnp.ones((sums_ref.shape[0], size), f32)
    square = lax.dot_general(sums_ref[:, 0, :], ones, TN, precision=highest, preferred_element_type=f32)
    product_ = lax.dot_general(sums_ref[:, 1, :], ones, TN, precision=highest, preferred_element_type=f32)
    scale = lax.rsqrt(square / full_width + epsilon)
    return scale, scale * scale * scale * (product_ / full_width)


def back_kernel(
    heads, members, full_width, query_ref, tall_ref, mixed_ref, gain_ref, grad_ref, sums_ref, out_ref
):
    size = query_ref.shape[1] // heads
    per = members // heads
    cut = size // per
    rising = jnp.exp(tall_ref[...])
    scale, pull = row_factors(full_width, size, sums_ref)
    for head in range(heads):
        here = cols(head, size)
        slope = scale * (grad_ref[:, here].astype(f32) * gain_ref[:, here]) - pull * mixed_ref[:, here]
        state = product(query_ref[:, here], slope * rising[:, head : head + 1], TN)
        first = turned(head, heads) * per
        for part in range(per):
            out_ref[first + part] = state[part * cut : (part + 1) * cut, :]


def near_kernel(
    heads,
    full_width,
    query_ref,
    key_ref,
    value_ref,
    tall_ref,
    wide_ref,
    state_ref,
    mixed_ref,
    gain_ref,
    grad_ref,
    sums_ref,
    normed_ref,
    grad_q_ref,
    near_k_ref,
    near_v_ref,
):
    size = key_ref.shape[1] // heads
    tall, wide = tall_ref[...], wide_ref[...]
    rising = jnp.exp(tall)
    scale, pull = row_factors(full_width, size, sums_ref)
    for head in range(heads):
        here = cols(head, size)
        query, key, value = query_ref[:, here], key_ref[:, here], value_ref[:, here]
        gain, mixed = gain_ref[:, here], mixed_ref[:, here]
        normed_ref[:, here] = (mixed * scale * gain).astype(bf16)
        slope = scale * (grad_ref[:, here].astype(f32) * gain) - pull * mixed
        weights = weights_of(tall, wide, head)
        scores = product(query, key, NT, True) * weights
        grad_scores = product(slope, value, NT, True) * weights
        there = turned(head, heads)
        outer = product(slope, state_ref[there], NT, True) * rising[:, head : head + 1]
        grad_q_ref[:, here] = (product(grad_scores, key, NN, True) + outer).astype(bf16)
        near_k_ref[there] = product(grad_scores, query, TN, True)
        near_v_ref[:, here] = product(scores, slope, TN, True)


def far_kernel(heads, key_ref, value_ref, tall_ref, state_ref, near_k_ref, near_v_ref, grad_k_ref, grad_v_ref):
    size = key_ref.shape[1] // heads
    tall = tall_ref[...]
    trailing = jnp.exp(tall[-1:, :] - tall)
    for head in range(heads):
        here = cols(head, size)
        late = trailing[:, head : head + 1]
        there = turned(head, heads)
        state = state_ref[there]
        grad_k = near_k_ref[there] + product(value_ref[:, here], state, NT, True) * late
        grad_v = near_v_ref[:, here] + product(key_ref[:, here], state, NN, True) * late
        grad_k_ref[:, here] = grad_k.astype(bf16)
        grad_v_ref[:, here] = grad_v.astype(bf16)


def call(kernel, outs, *args, flops=0, copied=(), aliases=None):
    vmem = pl.BlockSpec(memory_space=pltpu.VMEM)
    hbm = pl.BlockSpec(memory_space=pltpu.HBM)
    if copied:
        args = [pltpu.with_memory_space_constraint(a, pltpu.HBM) for a in args]
    moved = sum(a.size * a.dtype.itemsize for a in (*args, *outs))
    return pl.pallas_call(
        kernel,
        out_shape=outs,
        in_specs=[hbm if copied else vmem] * len(args),
        out_specs=[vmem] * len(outs),
        input_output_aliases=aliases or {},
        scratch_shapes=[pltpu.VMEM(a.shape, a.dtype) for a in copied]
        + ([pltpu.SemaphoreType.DMA((len(copied),))] if copied else []),
        cost_estimate=pl.CostEstimate(flops=flops, bytes_accessed=moved, transcendentals=0),
        compiler_params=pltpu.CompilerParams(vmem_limit_bytes=12 * 1024 * 1024),
    )(*args)


def levels(count, tp, heads):
    members = 2 * heads
    span = members // 4
    groups = count // members
    near, far = [], []
    for index in range(tp):
        shift = index % 2 * (span // 2)

        def device(group, place):
            x, z = place % 4, place // 4
            return ((group * span + shift + z) % (count // 4) * 4 + x) * tp + index

        for group in range(groups):
            near.append([device(group, place) for place in range(members)])
        for piece in range(members):
            far.append(
                [
                    device(group, piece ^ (8 if group >= groups // 2 else 0))
                    for group in range(groups)
                ]
            )
    return groups, members, near, far


def shards(queries, key_rows, value_rows, log_decay, norm_gain, grad_output):
    tok_rows, feat_width = queries.shape
    heads = log_decay.shape[1]
    groups, members, near, far = levels(lax.axis_size("ctx"), lax.axis_size("tp"), heads)
    size = feat_width // heads
    rows = heads * size // members
    wide = jax.ShapeDtypeStruct((tok_rows, feat_width), f32)
    narrow = jax.ShapeDtypeStruct((tok_rows, feat_width), bf16)
    gain = norm_gain.reshape(1, feat_width)
    log_decay = log_decay.T
    bind = functools.partial
    shape = jax.ShapeDtypeStruct
    unit = 2 * heads * tok_rows * size * size

    def exchange(parts, lists):
        return lax.all_to_all(parts, ("ctx", "tp"), 0, 0, axis_index_groups=lists)

    states, tall, across = call(
        bind(states_kernel, heads, members),
        [shape((members, rows + 8, size), f32), shape((tok_rows, heads), f32), shape((heads, tok_rows), f32)],
        key_rows,
        value_rows,
        log_decay,
        flops=2 * unit,
        copied=(key_rows, value_rows, log_decay),
    )
    pieces = exchange(states, near)
    (total,) = call(
        bind(group_kernel, members, groups, rows), [shape((groups, rows + 8, size), f32)], pieces
    )
    (inside,) = call(
        bind(inside_kernel, heads), [wide], queries, key_rows, value_rows, tall, across, flops=3 * unit
    )
    entering, near_gains, far_gains = call(
        bind(spread_kernel, members, groups, rows),
        [shape((members, rows, size), f32), shape((members, 8, size), f32), shape((groups, 8, size), f32)],
        pieces,
        exchange(total, far),
    )
    entry = exchange(entering, near).reshape(heads, size, size)
    mixed, sums = call(
        bind(mixed_kernel, heads),
        [wide, shape((lax.axis_size("tp"), 2, tok_rows), f32)],
        queries,
        tall,
        inside,
        entry,
        gain,
        grad_output,
        flops=2 * unit,
    )
    gathered = lax.all_to_all(sums, "tp", 0, 0)
    full_width = feat_width * lax.axis_size("tp")
    (back,) = call(
        bind(back_kernel, heads, members, full_width),
        [shape((members, rows, size), f32)],
        queries,
        tall,
        mixed,
        gain,
        grad_output,
        gathered,
        flops=2 * unit,
    )
    back_pieces = exchange(back, near)
    (back_total,) = call(
        bind(back_group_kernel, members, groups),
        [shape((groups, rows, size), f32)],
        back_pieces,
        near_gains,
    )
    (returning,) = call(
        bind(back_spread_kernel, members, groups),
        [shape((members, rows, size), f32)],
        back_pieces,
        near_gains,
        exchange(back_total, far),
        far_gains,
    )
    leaving = exchange(returning, near).reshape(heads, size, size)
    normed, grad_q, near_k, near_v = call(
        bind(near_kernel, heads, full_width),
        [narrow, narrow, shape((heads, size, size), f32), wide],
        queries,
        key_rows,
        value_rows,
        tall,
        across,
        entry,
        mixed,
        gain,
        grad_output,
        gathered,
        flops=13 * unit,
        aliases={5: 2, 6: 3},
    )
    grad_k, grad_v = call(
        bind(far_kernel, heads),
        [narrow, narrow],
        key_rows,
        value_rows,
        tall,
        leaving,
        near_k,
        near_v,
        flops=4 * unit,
    )
    return normed, grad_q, grad_k, grad_v


def solution(mesh):
    both = P("ctx", "tp")
    return jax.shard_map(
        shards,
        mesh=mesh,
        in_specs=(both, both, both, both, P("tp"), both),
        out_specs=(both, both, both, both),
        check_vma=False,
    )
```
